32 devices in a mesh: img: 2 (over x), row: 16 (over z, y, core).
Axes of the slice: x: 2, y: 2, z: 4, core: 2. Of those that a mesh axis runs over, the one named last changes fastest.
Arguments:
- inputs: bfloat16 [32, 16, 96, 256], P('row', 'img'), may hold values from -6 to 6
- cotangent: bfloat16 [32, 16, 96, 256], P('row', 'img'), may hold values from -6 to 6
- rows_gain: float32 [256], replicated, may hold values from 0.25 to 1.75
- rows_query: bfloat16 [256, 256], replicated, may hold values from -0.5 to 0.5
- rows_keys: bfloat16 [256, 256], replicated, may hold values from -0.5 to 0.5
- rows_values: bfloat16 [256, 256], replicated, may hold values from -0.375 to 0.375
- rows_mixer: bfloat16 [256, 256], replicated, may hold values from -1 to 1
- rows_scale: float32 [256], replicated, may hold values from 0.25 to 1.75
- rows_expand: bfloat16 [256, 1024], replicated, may hold values from -0.375 to 0.375
- rows_shrink: bfloat16 [1024, 256], replicated, may hold values from -0.375 to 0.375
- column_gain: float32 [256], replicated, may hold values from 0.25 to 1.75
- column_query: bfloat16 [256, 256], replicated, may hold values from -0.5 to 0.5
- column_keys: bfloat16 [256, 256], replicated, may hold values from -0.5 to 0.5
- column_values: bfloat16 [256, 256], replicated, may hold values from -0.375 to 0.375
- column_mixer: bfloat16 [256, 256], replicated, may hold values from -1 to 1
- column_scale: float32 [256], replicated, may hold values from 0.25 to 1.75
- column_expand: bfloat16 [256, 1024], replicated, may hold values from -0.375 to 0.375
- column_shrink: bfloat16 [1024, 256], replicated, may hold values from -0.375 to 0.375
Outputs:
- output: bfloat16 [32, 16, 96, 256], P('row', 'img')
- input_grad: float32 [32, 16, 96, 256], P('row', 'img')
- rows_gain_grad: float32 [256], replicated
- rows_query_grad: float32 [256, 256], replicated
- rows_keys_grad: float32 [256, 256], replicated
- rows_values_grad: float32 [256, 256], replicated
- rows_mixer_grad: float32 [256, 256], replicated
- rows_scale_grad: float32 [256], replicated
- rows_expand_grad: float32 [256, 1024], replicated
- rows_shrink_grad: float32 [1024, 256], replicated
- column_gain_grad: float32 [256], replicated
- column_query_grad: float32 [256, 256], replicated
- column_keys_grad: float32 [256, 256], replicated
- column_values_grad: float32 [256, 256], replicated
- column_mixer_grad: float32 [256, 256], replicated
- column_scale_grad: float32 [256], replicated
- column_expand_grad: float32 [256, 1024], replicated
- column_shrink_grad: float32 [1024, 256], replicated
The draws below stay inside these ranges and needn't reach their ends.
All inputs are finite; a program needn't handle non-finite values.
Results may differ from the reference program's by a relative error of at most 0.023.
The reference program's roundings to bfloat16 on the way count: a program that leaves them out, or rounds other values in their place, can miss the bound.
Values may be sent and summed in bfloat16 or wider, within the bound.
No kernel may reach another device: no remote copies, remote signals or barrier semaphores. Data moves between devices by JAX's collectives and lax.ppermute only.
A program may use at most 448 MiB of HBM per device.

```python
import jax
import jax.numpy as jnp
from jax import lax

D = 256
HEADS = 2
FF = 1024
ROWS = 32
COLS = 96
IMAGES = 16


def block_levels(stream_key, shape, split, low, top_value):
    def one(axis_at, shards_of):
        draws = jax.random.uniform(jax.random.fold_in(jax.random.fold_in(stream_key, 6), axis_at), (shards_of,), jnp.float32, low / len(split), top_value / len(split))
        return jnp.repeat(jnp.exp(draws), shape[axis_at] // shards_of).reshape((-1,) + (1,) * (len(shape) - axis_at - 1))

    loudness = one(*split[0])
    for cut in split[1:]:
        loudness = loudness * one(*cut)
    return loudness


def bell_draw(rng, shape, spread, bound, shards=(), kind=jnp.bfloat16):
    level = block_levels(rng, shape, shards, -0.22, 0.18) if shards else 1.0
    result = jax.random.normal(rng, shape, jnp.float32) * spread * level
    return jnp.minimum(jnp.maximum(result, -bound), bound).astype(kind)


def setup_inputs(seed: int = 0) -> dict:
    key_list = jax.random.split(jax.random.key(seed), 19)
    return {
        "inputs": bell_draw(key_list[0], (ROWS, IMAGES, COLS, D), 1.0, 6.0, ((0, 16), (1, 2))),
        "cotangent": bell_draw(key_list[1], (ROWS, IMAGES, COLS, D), 1.0, 6.0, ((0, 16), (1, 2))),
        "rows_gain": jnp.clip(1.0 + 0.15 * jax.random.normal(key_list[2], (D,), jnp.float32), 0.25, 1.75),
        "rows_query": bell_draw(key_list[3], (D, D), (D // 2) ** -0.5, 0.5),
        "rows_keys": bell_draw(key_list[4], (D, D), (D // 2) ** -0.5, 0.5),
        "rows_values": bell_draw(key_list[5], (D, D), D ** -0.5, 0.375),
        "rows_mixer": bell_draw(key_list[6], (D, D), (D // 8) ** -0.5, 1.0),
        "rows_scale": jnp.clip(1.0 + 0.15 * jax.random.normal(key_list[7], (D,), jnp.float32), 0.25, 1.75),
        "rows_expand": bell_draw(key_list[8], (D, FF), D ** -0.5, 0.375),
        "rows_shrink": bell_draw(key_list[9], (FF, D), (FF // 4) ** -0.5, 0.375),
        "column_gain": jnp.clip(1.0 + 0.15 * jax.random.normal(key_list[10], (D,), jnp.float32), 0.25, 1.75),
        "column_query": bell_draw(key_list[11], (D, D), (D // 2) ** -0.5, 0.5),
        "column_keys": bell_draw(key_list[12], (D, D), (D // 2) ** -0.5, 0.5),
        "column_values": bell_draw(key_list[13], (D, D), D ** -0.5, 0.375),
        "column_mixer": bell_draw(key_list[14], (D, D), (D // 8) ** -0.5, 1.0),
        "column_scale": jnp.clip(1.0 + 0.15 * jax.random.normal(key_list[15], (D,), jnp.float32), 0.25, 1.75),
        "column_expand": bell_draw(key_list[16], (D, FF), D ** -0.5, 0.375),
        "column_shrink": bell_draw(key_list[17], (FF, D), (FF // 4) ** -0.5, 0.375),
    }


EPS = 1e-05

@jax.custom_vjp
def low(v):
    return lax.optimization_barrier(v.astype(jnp.bfloat16)).astype(jnp.float32)

@jax.custom_vjp
def low_back(v):
    return v

def low_keep(v):
    return (low(v), None)

def low_pass(kept, grad):
    return (grad,)

def back_keep(v):
    return (v, None)

def back_low(kept, grad):
    return (low(grad),)
low.defvjp(low_keep, low_pass)
low_back.defvjp(back_keep, back_low)

def product(left, right):
    return jnp.dot(left, right, precision=lax.Precision.HIGHEST)

def layer_norm(stream, gain):
    centred = stream - lax.optimization_barrier(jnp.mean(stream, axis=-1, keepdims=True))
    return centred * lax.rsqrt(lax.optimization_barrier(jnp.mean(centred * centred, axis=-1, keepdims=True)) + EPS) * gain

def attention(query, keyed, valued, pattern):
    height, breadth, channels = query.shape
    features = channels // HEADS
    scaling = 1.0 / jnp.sqrt(jnp.float32(features))
    query_heads = query.reshape(height, breadth, HEADS, features)
    key_heads = keyed.reshape(height, breadth, HEADS, features)
    value_heads = valued.reshape(height, breadth, HEADS, features)
    if pattern == 'row':
        scores = jnp.einsum('rihe,rjhe->rhij', query_heads, key_heads, precision=lax.Precision.HIGHEST) * scaling
        places = jnp.arange(breadth)
    else:
        scores = jnp.einsum('iche,jche->chij', query_heads, key_heads, precision=lax.Precision.HIGHEST) * scaling
        places = jnp.arange(height)
    scores = low_back(scores)
    visible = places[:, None] >= places[None, :]
    softened = jax.nn.softmax(jnp.where(visible, scores, -jnp.inf), axis=-1)
    rounded = low(softened)
    if pattern == 'row':
        attended = jnp.einsum('rhij,rjhe->rihe', rounded, value_heads, precision=lax.Precision.HIGHEST)
    else:
        attended = jnp.einsum('chij,jche->iche', rounded, value_heads, precision=lax.Precision.HIGHEST)
    return low(low_back(attended.reshape(height, breadth, channels)))

def block(stream, weights, pattern):
    gain_a, query_w, key_w, value_w, mixer_w, gain_b, expand_w, shrink_w = weights
    normed = low(layer_norm(stream, gain_a))
    query = low(low_back(product(normed, query_w)))
    keyed = low(low_back(product(normed, key_w)))
    valued = low(low_back(product(normed, value_w)))
    attended = attention(query, keyed, valued, pattern)
    middle = stream + low_back(product(attended, mixer_w))
    normed_b = low(layer_norm(middle, gain_b))
    hidden = low(jax.nn.gelu(low_back(product(normed_b, expand_w))))
    return middle + low_back(product(hidden, shrink_w))

def network(picture, rows_weights, column_weights):
    return block(block(picture, rows_weights, 'row'), column_weights, 'column')

def reference(inputs, cotangent, rows_gain, rows_query, rows_keys, rows_values, rows_mixer, rows_scale, rows_expand, rows_shrink, column_gain, column_query, column_keys, column_values, column_mixer, column_scale, column_expand, column_shrink):
    rows_weights = tuple((weight.astype(jnp.float32) for weight in (rows_gain, rows_query, rows_keys, rows_values, rows_mixer, rows_scale, rows_expand, rows_shrink)))
    column_weights = tuple((weight.astype(jnp.float32) for weight in (column_gain, column_query, column_keys, column_values, column_mixer, column_scale, column_expand, column_shrink)))
    pictures = jnp.moveaxis(inputs.astype(jnp.float32), 1, 0)
    upstreams = jnp.moveaxis(cotangent.astype(jnp.float32), 1, 0)

    def advance(totals, couple):
        picture, upstream = couple
        produced, pullback = jax.vjp(network, picture, rows_weights, column_weights)
        d_picture, d_rows, d_columns = pullback(upstream)
        totals = jax.tree.map(lambda first, second: first + second, totals, (d_rows, d_columns))
        return (totals, (produced, d_picture))
    initial = jax.tree.map(jnp.zeros_like, (rows_weights, column_weights))
    (grads_rows, grads_columns), (produced, d_pictures) = lax.scan(advance, initial, (pictures, upstreams))
    output = jnp.moveaxis(produced, 0, 1).astype(jnp.bfloat16)
    input_grad = jnp.moveaxis(d_pictures, 0, 1)
    return (output, input_grad, grads_rows[0], grads_rows[1], grads_rows[2], grads_rows[3], grads_rows[4], grads_rows[5], grads_rows[6], grads_rows[7], grads_columns[0], grads_columns[1], grads_columns[2], grads_columns[3], grads_columns[4], grads_columns[5], grads_columns[6], grads_columns[7])
```

```python
import functools
import math

import jax
import jax.numpy as jnp
from jax import lax
from jax.experimental import pallas as pl
from jax.experimental.pallas import tpu as pltpu
from jax.sharding import PartitionSpec as P

HEADS = 2
EPS = 1e-05
GROUP = 8
TAIL = 16
HIDDEN_TILE = 256
VMEM_LIMIT = 56 * 1024 * 1024
ALL = ("img", "row")
F32 = jnp.float32
BF16 = jnp.bfloat16


def mm(left, right):
    return lax.dot_general(left, right, (((1,), (0,)), ((), ())), preferred_element_type=F32)


def mm_right_t(left, right):
    return lax.dot_general(left, right, (((1,), (1,)), ((), ())), preferred_element_type=F32)


def mm_left_t(left, right):
    return lax.dot_general(left, right, (((0,), (0,)), ((), ())), preferred_element_type=F32)


def normalize(stream):
    centred = stream - jnp.mean(stream, axis=-1, keepdims=True)
    inverse = lax.rsqrt(jnp.mean(centred * centred, axis=-1, keepdims=True) + EPS)
    return centred * inverse, inverse


def normalize_back(upstream, normal, inverse, gain):
    scaled = upstream * gain
    centred = (
        scaled
        - jnp.mean(scaled, axis=-1, keepdims=True)
        - normal * jnp.mean(scaled * normal, axis=-1, keepdims=True)
    )
    return inverse * centred, jnp.sum(upstream * normal, axis=0, keepdims=True)


ROOT = math.sqrt(2.0 / math.pi)
CUBE = 0.044715


def gelu(value):
    bent = jnp.tanh(ROOT * (value + CUBE * (value * value * value)))
    return 0.5 * value * (1.0 + bent)


def gelu_both(value):
    square = value * value
    bent = jnp.tanh(ROOT * (value + CUBE * (square * value)))
    half = 0.5 * (1.0 + bent)
    slope = half + (0.5 * ROOT) * value * (1.0 - bent * bent) * (1.0 + (3.0 * CUBE) * square)
    return value * half, slope


def softmax(scores):
    risen = jnp.exp(scores - jnp.max(scores, axis=-1, keepdims=True))
    return risen / jnp.sum(risen, axis=-1, keepdims=True)


def causal_bias(size, period):
    row = lax.broadcasted_iota(jnp.int32, (size, size), 0)
    col = lax.broadcasted_iota(jnp.int32, (size, size), 1)
    visible = (row >= col) & (((row ^ col) & (period - 1)) == 0)
    return jnp.where(visible, 0.0, -1e30).astype(F32)


def attend_back(up, query, key, value, probs, scaling):
    prob_grad = mm_right_t(up, value)
    inner = jnp.sum(probs * prob_grad, axis=-1, keepdims=True)
    score_grad = (probs * (prob_grad - inner)).astype(BF16)
    query_grad = (mm(score_grad, key) * scaling).astype(BF16)
    key_grad = (mm_left_t(score_grad, query) * scaling).astype(BF16)
    value_grad = mm_left_t(probs.astype(BF16), up).astype(BF16)
    return query_grad, key_grad, value_grad


def feed_back(normed, up_low, expand_ref, shrink_ref, acc, first, forward):
    width = normed.shape[-1]
    hidden_width = expand_ref.shape[1]
    tile = min(HIDDEN_TILE, hidden_width)
    result = None
    normed_grad = None
    for j in range(hidden_width // tile):
        cut = slice(j * tile, (j + 1) * tile)
        expand = expand_ref[:, cut]
        shrink = shrink_ref[cut, :]
        hidden, slope = gelu_both(mm(normed, expand))
        hidden = hidden.astype(BF16)
        if forward:
            part = mm(hidden, shrink)
            result = part if result is None else result + part
        expanded_grad = (slope * mm_right_t(up_low, shrink)).astype(BF16)
        at = first + j * width
        acc[at : at + width, :] += mm_left_t(normed, expanded_grad)
        at = first + hidden_width // tile * width + j * width
        acc[at : at + width, :] += mm_left_t(up_low, hidden)
        part = mm_right_t(expanded_grad, expand)
        normed_grad = part if normed_grad is None else normed_grad + part
    return result, normed_grad


def project_back(normed_low, grads, weight_refs, acc):
    width = normed_low.shape[-1]
    total = None
    for i, (grad, weight_ref) in enumerate(zip(grads, weight_refs)):
        acc[i * width : (i + 1) * width, :] += mm_left_t(normed_low, grad)
        part = mm_right_t(grad, weight_ref[...])
        total = part if total is None else total + part
    return total


def store_tail(ref, at, gains):
    high = gains.astype(BF16)
    ref[at : at + 8, :] = high
    ref[at + 8 : at + 16, :] = (gains - high.astype(F32)).astype(BF16)


def emit_grads(core, acc, gains, keep_ref, send_ref):
    half = acc.shape[0] // 2
    for which, (mine, other) in enumerate(((keep_ref, send_ref), (send_ref, keep_ref))):

        @pl.when(core == which)
        def _():
            mine[0:half, :] = acc[0:half, :].astype(BF16)
            other[0:half, :] = acc[half:, :].astype(BF16)

    store_tail(keep_ref, half, gains[...])
    store_tail(send_ref, half, gains[...])


def rows_forward_kernel(
    x_ref, ga_ref, wq_ref, wk_ref, wv_ref, wo_ref, gb_ref, w1_ref, w2_ref,
    send_ref, q_ref, k_ref, v_ref, att_ref, mid_ref, p_ref,
):
    rows, images, cols, width = x_ref.shape
    tokens = rows * images * cols
    features = width // HEADS
    scaling = 1.0 / math.sqrt(features)
    stream = x_ref[...].astype(F32).reshape(tokens, width)
    normed = (normalize(stream)[0] * ga_ref[...]).astype(BF16)
    query = mm(normed, wq_ref[...]).astype(BF16)
    key = mm(normed, wk_ref[...]).astype(BF16)
    value = mm(normed, wv_ref[...]).astype(BF16)
    q_ref[...] = query.reshape(q_ref.shape)
    k_ref[...] = key.reshape(q_ref.shape)
    v_ref[...] = value.reshape(q_ref.shape)
    bias = causal_bias(cols, 1)
    groups = []
    for g in range(rows * images):
        span = slice(g * cols, (g + 1) * cols)
        heads = []
        for m in range(HEADS):
            part = slice(m * features, (m + 1) * features)
            probs = softmax(mm_right_t(query[span, part], key[span, part]) * scaling + bias)
            p_ref[g // images, g % images, m] = probs
            heads.append(mm(probs.astype(BF16), value[span, part]))
        groups.append(jnp.concatenate(heads, axis=1))
    attended = jnp.concatenate(groups, axis=0).astype(BF16)
    att_ref[...] = attended.reshape(att_ref.shape)
    middle = stream + mm(attended, wo_ref[...])
    mid_ref[...] = middle.reshape(mid_ref.shape)
    normed_b = (normalize(middle)[0] * gb_ref[...]).astype(BF16)
    hidden_width = w1_ref.shape[1]
    tile = min(HIDDEN_TILE, hidden_width)
    result = middle
    for j in range(hidden_width // tile):
        cut = slice(j * tile, (j + 1) * tile)
        hidden = gelu(mm(normed_b, w1_ref[:, cut])).astype(BF16)
        result = result + mm(hidden, w2_ref[cut, :])
    result = result.reshape(rows, images * cols // GROUP, GROUP, width)
    result = jnp.concatenate([result[r] for r in range(rows)], axis=1)
    send_ref[...] = result.astype(BF16).reshape(send_ref.shape)


def rows_backward_kernel(
    core_ref, x_ref, q_ref, k_ref, v_ref, att_ref, mid_ref, p_ref, up_ref,
    ga_ref, wq_ref, wk_ref, wv_ref, wo_ref, gb_ref, w1_ref, w2_ref,
    grad_ref, keep_ref, send_ref, acc, gains,
):
    rows, images, cols, width = x_ref.shape
    tokens = rows * images * cols
    features = width // HEADS
    scaling = 1.0 / math.sqrt(features)
    step = pl.program_id(0)

    @pl.when(step == 0)
    def _():
        acc[...] = jnp.zeros_like(acc)
        gains[...] = jnp.zeros_like(gains)

    up = up_ref[...].astype(F32).reshape(images * cols // GROUP, rows * GROUP, width)
    up = jnp.concatenate(
        [up[:, r * GROUP : (r + 1) * GROUP].reshape(images * cols, width) for r in range(rows)], axis=0
    )
    up_low = up.astype(BF16)
    middle = mid_ref[...].reshape(tokens, width)
    normal_b, inverse_b = normalize(middle)
    normed_b = (normal_b * gb_ref[...]).astype(BF16)
    _, normed_grad = feed_back(normed_b, up_low, w1_ref, w2_ref, acc, 4 * width, False)
    middle_norm, scale_grad = normalize_back(normed_grad, normal_b, inverse_b, gb_ref[...])
    gains[1:2, :] += scale_grad
    middle_grad = up + middle_norm
    middle_low = middle_grad.astype(BF16)
    acc[3 * width : 4 * width, :] += mm_left_t(att_ref[...].reshape(tokens, width), middle_low)
    up_att = mm_right_t(middle_low, wo_ref[...]).astype(BF16)
    query = q_ref[...].reshape(tokens, width)
    key = k_ref[...].reshape(tokens, width)
    value = v_ref[...].reshape(tokens, width)
    parts = ([], [], [])
    for g in range(rows * images):
        span = slice(g * cols, (g + 1) * cols)
        heads = []
        for m in range(HEADS):
            part = slice(m * features, (m + 1) * features)
            heads.append(
                attend_back(
                    up_att[span, part], query[span, part], key[span, part], value[span, part],
                    p_ref[g // images, g % images, m], scaling,
                )
            )
        for i in range(3):
            parts[i].append(jnp.concatenate([head[i] for head in heads], axis=1))
    grads = tuple(jnp.concatenate(part, axis=0) for part in parts)
    normal_a, inverse_a = normalize(x_ref[...].astype(F32).reshape(tokens, width))
    normed_a = (normal_a * ga_ref[...]).astype(BF16)
    normed_grad = project_back(normed_a, grads, (wq_ref, wk_ref, wv_ref), acc)
    stream_norm, gain_grad = normalize_back(normed_grad, normal_a, inverse_a, ga_ref[...])
    gains[0:1, :] += gain_grad
    grad_ref[...] = (middle_grad + stream_norm).reshape(grad_ref.shape)

    @pl.when(step == pl.num_programs(0) - 1)
    def _():
        emit_grads(core_ref[0], acc, gains, keep_ref, send_ref)


def columns_kernel(
    core_ref, x_ref, up_ref, ga_ref, wq_ref, wk_ref, wv_ref, wo_ref, gb_ref, w1_ref, w2_ref,
    out_ref, grad_ref, keep_ref, send_ref, acc, gains, bias,
):
    width = x_ref.shape[-1]
    tokens = x_ref.shape[0] * x_ref.shape[2]
    features = width // HEADS
    scaling = 1.0 / math.sqrt(features)
    step = pl.program_id(0)

    @pl.when(step == 0)
    def _():
        acc[...] = jnp.zeros_like(acc)
        gains[...] = jnp.zeros_like(gains)
        bias[...] = causal_bias(tokens, GROUP)

    stream = x_ref[...].astype(F32).reshape(tokens, width)
    normal_a, inverse_a = normalize(stream)
    normed_a = (normal_a * ga_ref[...]).astype(BF16)
    query = mm(normed_a, wq_ref[...]).astype(BF16)
    key = mm(normed_a, wk_ref[...]).astype(BF16)
    value = mm(normed_a, wv_ref[...]).astype(BF16)
    probs, heads = [], []
    for m in range(HEADS):
        part = slice(m * features, (m + 1) * features)
        probs.append(softmax(mm_right_t(query[:, part], key[:, part]) * scaling + bias[...]))
        heads.append(mm(probs[m].astype(BF16), value[:, part]))
    attended = jnp.concatenate(heads, axis=1).astype(BF16)
    middle = stream + mm(attended, wo_ref[...])
    normal_b, inverse_b = normalize(middle)
    normed_b = (normal_b * gb_ref[...]).astype(BF16)
    up = up_ref[...].astype(F32).reshape(tokens, width)
    up_low = up.astype(BF16)
    result, normed_grad = feed_back(normed_b, up_low, w1_ref, w2_ref, acc, 4 * width, True)
    out_ref[...] = (middle + result).reshape(out_ref.shape).astype(BF16)
    middle_norm, scale_grad = normalize_back(normed_grad, normal_b, inverse_b, gb_ref[...])
    gains[1:2, :] += scale_grad
    middle_grad = up + middle_norm
    middle_low = middle_grad.astype(BF16)
    acc[3 * width : 4 * width, :] += mm_left_t(attended, middle_low)
    up_att = mm_right_t(middle_low, wo_ref[...]).astype(BF16)
    backs = []
    for m in range(HEADS):
        part = slice(m * features, (m + 1) * features)
        backs.append(
            attend_back(up_att[:, part], query[:, part], key[:, part], value[:, part], probs[m], scaling)
        )
    grads = tuple(jnp.concatenate([back[i] for back in backs], axis=1) for i in range(3))
    normed_grad = project_back(normed_a, grads, (wq_ref, wk_ref, wv_ref), acc)
    stream_norm, gain_grad = normalize_back(normed_grad, normal_a, inverse_a, ga_ref[...])
    gains[0:1, :] += gain_grad
    grad_ref[...] = (middle_grad + stream_norm).reshape(grad_ref.shape).astype(BF16)

    @pl.when(step == pl.num_programs(0) - 1)
    def _():
        emit_grads(core_ref[0], acc, gains, keep_ref, send_ref)


def whole(array):
    zeros = (0,) * array.ndim
    return pl.BlockSpec(array.shape, lambda i: zeros)


def whole_out(shape):
    zeros = (0,) * len(shape)
    return pl.BlockSpec(shape, lambda i: zeros)


SCALAR = pl.BlockSpec(memory_space=pltpu.SMEM)


def params():
    return pltpu.CompilerParams(vmem_limit_bytes=VMEM_LIMIT)


def shape_of(shape, dtype):
    return jax.ShapeDtypeStruct(shape, dtype)


def grad_rows(width, hidden_width):
    tile = min(HIDDEN_TILE, hidden_width)
    return 4 * width + 2 * (hidden_width // tile) * width


def cost(tokens, width, hidden_width, passes, moved):
    flops = 2 * passes * tokens * width * (4 * width + 2 * hidden_width)
    return pl.CostEstimate(flops=flops, bytes_accessed=moved, transcendentals=tokens * hidden_width)


def rows_forward(inputs, weights, images_step):
    rows, images, cols, width = inputs.shape
    groups = cols // GROUP
    block = (rows, images_step, cols, width)
    spec = pl.BlockSpec(block, lambda i: (0, i, 0, 0))
    p_spec = pl.BlockSpec((rows, images_step, HEADS, cols, cols), lambda i: (0, i, 0, 0, 0))
    send_block = (images_step, groups, rows * GROUP, width)
    low = shape_of(inputs.shape, BF16)
    return pl.pallas_call(
        rows_forward_kernel,
        grid=(images // images_step,),
        in_specs=[spec] + [whole(w) for w in weights],
        out_specs=[pl.BlockSpec(send_block, lambda i: (i, 0, 0, 0)), spec, spec, spec, spec, spec, p_spec],
        out_shape=[
            shape_of((images, groups, rows * GROUP, width), BF16),
            low, low, low, low,
            shape_of(inputs.shape, F32),
            shape_of((rows, images, HEADS, cols, cols), F32),
        ],
        compiler_params=params(),
        cost_estimate=cost(rows * images * cols, width, weights[6].shape[1], 1, 12 << 20),
        name="rows_forward",
    )(inputs, *weights)


def rows_backward(core, inputs, stored, up, weights, images_step):
    rows, images, cols, width = inputs.shape
    groups = cols // GROUP
    hidden_width = weights[6].shape[1]
    total = grad_rows(width, hidden_width)
    spec = pl.BlockSpec((rows, images_step, cols, width), lambda i: (0, i, 0, 0))
    p_spec = pl.BlockSpec((rows, images_step, HEADS, cols, cols), lambda i: (0, i, 0, 0, 0))
    up_spec = pl.BlockSpec((images_step, groups, rows * GROUP, width), lambda i: (i, 0, 0, 0))
    part = (total // 2 + TAIL, width)
    return pl.pallas_call(
        rows_backward_kernel,
        grid=(images // images_step,),
        in_specs=[SCALAR, spec, spec, spec, spec, spec, spec, p_spec, up_spec] + [whole(w) for w in weights],
        out_specs=[spec, whole_out(part), whole_out(part)],
        out_shape=[shape_of(inputs.shape, F32), shape_of(part, BF16), shape_of(part, BF16)],
        scratch_shapes=[pltpu.VMEM((total, width), F32), pltpu.VMEM((8, width), F32)],
        compiler_params=params(),
        cost_estimate=cost(rows * images * cols, width, hidden_width, 2, 16 << 20),
        name="rows_backward",
    )(core, inputs, *stored, up, *weights)


def columns_both(core, stream, up, weights):
    sources, groups, height, width = stream.shape
    hidden_width = weights[6].shape[1]
    total = grad_rows(width, hidden_width)
    tokens = sources * height
    spec = pl.BlockSpec((sources, 1, height, width), lambda i: (0, i, 0, 0))
    part = (total // 2 + TAIL, width)
    return pl.pallas_call(
        columns_kernel,
        grid=(groups,),
        in_specs=[SCALAR, spec, spec] + [whole(w) for w in weights],
        out_specs=[spec, spec, whole_out(part), whole_out(part)],
        out_shape=[shape_of(stream.shape, BF16), shape_of(stream.shape, BF16), shape_of(part, BF16), shape_of(part, BF16)],
        scratch_shapes=[
            pltpu.VMEM((total, width), F32),
            pltpu.VMEM((8, width), F32),
            pltpu.VMEM((tokens, tokens), F32),
        ],
        compiler_params=params(),
        cost_estimate=cost(tokens * groups, width, hidden_width, 3, 6 << 20),
        name="columns_both",
    )(core, stream, up, *weights)


def sum_split_kernel(count, ways, at_ref, *refs):
    ins, outs, parts = refs[:count], refs[count : count + ways], refs[-1]
    size = ins[0].shape[0] - TAIL
    total = ins[0][0:size, :].astype(F32)
    gains = ins[0][size : size + 8, :].astype(F32) + ins[0][size + 8 :, :].astype(F32)
    for ref in ins[1:]:
        total = total + ref[0:size, :].astype(F32)
        gains = gains + (ref[size : size + 8, :].astype(F32) + ref[size + 8 :, :].astype(F32))
    total = total.astype(BF16)
    if ways == 1:
        outs[0][0:size, :] = total
        store_tail(outs[0], size, gains)
        return
    step = size // ways
    for j in range(ways):
        parts[j] = total[j * step : (j + 1) * step, :]
    for j in range(ways):
        outs[j][0:step, :] = parts[at_ref[0] ^ j]
        store_tail(outs[j], step, gains)


def sum_split(at, arrays, ways):
    size, width = arrays[0].shape
    step = (size - TAIL) // ways
    shape = (step + TAIL, width)
    return pl.pallas_call(
        functools.partial(sum_split_kernel, len(arrays), ways),
        in_specs=[SCALAR] + [pl.BlockSpec(memory_space=pltpu.VMEM)] * len(arrays),
        out_specs=[pl.BlockSpec(memory_space=pltpu.VMEM)] * ways,
        out_shape=[shape_of(shape, BF16)] * ways,
        scratch_shapes=[pltpu.VMEM((ways, step, width), BF16)],
        compiler_params=params(),
        name="sum_split",
    )(at, *arrays)


def join_kernel(ways, at_ref, *refs):
    ins, out = refs[:ways], refs[-1]
    size = out.shape[1]
    for j in range(ways):
        out[at_ref[0] ^ j] = ins[j][0:size, :]


def join(at, arrays, size):
    ways, width = len(arrays), arrays[0].shape[1]
    joined = pl.pallas_call(
        functools.partial(join_kernel, ways),
        in_specs=[SCALAR] + [pl.BlockSpec(memory_space=pltpu.VMEM)] * ways,
        out_specs=pl.BlockSpec(memory_space=pltpu.VMEM),
        out_shape=shape_of((ways, size, width), BF16),
        compiler_params=params(),
        name="join",
    )(at, *arrays)
    return joined.reshape(ways * size, width)


def finish_kernel(at_ref, own_ref, other_ref, tail_ref, *refs):
    outs, halves = refs[:-1], refs[-1]
    gain, query, keys, values, mixer, scale, expand, shrink = outs
    width = own_ref.shape[1]
    halves[at_ref[0]] = own_ref[...]
    halves[at_ref[0] ^ 1] = other_ref[...]
    per_half = halves.shape[1] // width

    def block(i):
        at = (i % per_half) * width
        return halves[i // per_half, at : at + width, :].astype(F32)

    for i, ref in enumerate((query, keys, values, mixer)):
        ref[...] = block(i)
    tiles = expand.shape[1] // width
    for j in range(tiles):
        expand[:, j * width : (j + 1) * width] = block(4 + j)
        shrink[j * width : (j + 1) * width, :] = block(4 + tiles + j).T
    start = tail_ref.shape[0] - TAIL
    gains = tail_ref[start : start + 8, :].astype(F32) + tail_ref[start + 8 :, :].astype(F32)
    gain[...] = gains[0:1, :]
    scale[...] = gains[1:2, :]


def finish(at, own, other, tail, width, hidden_width):
    half = own.shape[0]
    square = shape_of((width, width), F32)
    row = shape_of((1, width), F32)
    outs = pl.pallas_call(
        finish_kernel,
        in_specs=[SCALAR] + [pl.BlockSpec(memory_space=pltpu.VMEM)] * 3,
        out_specs=[pl.BlockSpec(memory_space=pltpu.VMEM)] * 8,
        out_shape=[
            row, square, square, square, square, row,
            shape_of((width, hidden_width), F32), shape_of((hidden_width, width), F32),
        ],
        scratch_shapes=[pltpu.VMEM((2, half, width), BF16)],
        compiler_params=params(),
        name="finish",
    )(at, own, other, tail)
    return [outs[0].reshape(width)] + list(outs[1:5]) + [outs[5].reshape(width)] + list(outs[6:])


class Exchange:
    def __init__(self, bits, flat, devices):
        self.bits = bits
        self.ways = 1 << len(bits)
        place = sum(((flat >> bit) & 1) << i for i, bit in enumerate(bits))
        self.place = jnp.reshape(place, (1,)).astype(jnp.int32)
        self.devices = devices

    def swap(self, array, member):
        mask = sum(1 << bit for i, bit in enumerate(self.bits) if (member >> i) & 1)
        return lax.ppermute(array, ALL, [(i, i ^ mask) for i in range(self.devices)])


def sum_over_devices(exchanges, keep, send, width, hidden_width):
    arrays = [keep, exchanges[0].swap(send, 1)]
    spread = [exchanges[0]]
    for exchange in exchanges[1:]:
        size = arrays[0].shape[0] - TAIL
        if size % (exchange.ways * TAIL) == 0:
            parts = sum_split(exchange.place, arrays, exchange.ways)
            arrays = [parts[0]] + [exchange.swap(parts[j], j) for j in range(1, exchange.ways)]
            spread.append(exchange)
        else:
            (part,) = sum_split(exchange.place, arrays, 1)
            arrays = [part] + [exchange.swap(part, j) for j in range(1, exchange.ways)]
    (tail,) = sum_split(exchanges[0].place, arrays, 1)
    part = tail
    size = tail.shape[0] - TAIL
    for exchange in reversed(spread[1:]):
        part = part if part.shape[0] == size else part[:size]
        pieces = [part] + [exchange.swap(part, j) for j in range(1, exchange.ways)]
        part = join(exchange.place, pieces, size)
        size = part.shape[0]
    other = spread[0].swap(part, 1)
    return finish(spread[0].place, part, other, tail, width, hidden_width)


def on_device(images_step, inputs, cotangent, *weights):
    rows, images, cols, width = inputs.shape
    groups = cols // GROUP
    height = lax.axis_size("row")
    devices = height * lax.axis_size("img")
    flat = lax.axis_index("img") * height + lax.axis_index("row")
    bits = list(range(1, devices.bit_length() - 1))
    exchanges = [Exchange([0], flat, devices)]
    while bits:
        pair = [bits.pop()]
        if bits:
            pair.append(bits.pop(0))
        exchanges.append(Exchange(pair, flat, devices))
    core = exchanges[0].place
    weights = [w.reshape(1, -1) if w.ndim == 1 else w for w in weights]
    rows_weights, column_weights = weights[:8], weights[8:]
    hidden_width = rows_weights[6].shape[1]
    owned = images * groups // height

    def to_columns(array):
        array = array.reshape(height, owned, rows * GROUP, width)
        return lax.all_to_all(array, "row", 0, 0, tiled=True)

    def to_rows(array):
        array = lax.all_to_all(array, "row", 0, 0, tiled=True)
        return array.reshape(images, groups, rows * GROUP, width)

    def gather_rows(array):
        array = array.reshape(rows, images, groups, GROUP, width)
        return array.transpose(1, 2, 0, 3, 4)

    up = to_columns(gather_rows(cotangent))
    sent, *stored = rows_forward(inputs, rows_weights, images_step)
    stream = to_columns(sent)
    final, between_grad, keep, send = columns_both(core, stream, up, column_weights)
    column_grads = sum_over_devices(exchanges, keep, send, width, hidden_width)
    final = to_rows(final).reshape(images, groups, rows, GROUP, width)
    final = final.transpose(2, 0, 1, 3, 4).reshape(inputs.shape)
    stream_grad, keep, send = rows_backward(
        core, inputs, stored, to_rows(between_grad), rows_weights, images_step
    )
    rows_grads = sum_over_devices(exchanges, keep, send, width, hidden_width)
    return (final, stream_grad) + tuple(rows_grads) + tuple(column_grads)


def solution(mesh):
    moved = P("row", "img", None, None)
    return jax.shard_map(
        functools.partial(on_device, 2),
        mesh=mesh,
        in_specs=(moved, moved) + (P(),) * 16,
        out_specs=(moved, moved) + (P(),) * 16,
        check_vma=False,
    )
```

```python
import functools
import math

import jax
import jax.numpy as jnp
from jax import lax
from jax.experimental import pallas as pl
from jax.experimental.pallas import tpu as pltpu
from jax.sharding import PartitionSpec as P

HEADS = 2
EPS = 1e-05
GROUP = 8
TAIL = 16
HIDDEN_TILE = 256
VMEM_LIMIT = 24 * 1024 * 1024
SMALL_LIMIT = 12 * 1024 * 1024
ALL = ("img", "row")
HEAVY = 1 << 25
PLACE = 1
F32 = jnp.float32
BF16 = jnp.bfloat16


def mm(left, right):
    return lax.dot_general(left, right, (((1,), (0,)), ((), ())), preferred_element_type=F32)


def mm_right_t(left, right):
    return lax.dot_general(left, right, (((1,), (1,)), ((), ())), preferred_element_type=F32)


def mm_left_t(left, right):
    return lax.dot_general(left, right, (((0,), (0,)), ((), ())), preferred_element_type=F32)


def normalize(stream):
    centred = stream - jnp.mean(stream, axis=-1, keepdims=True)
    inverse = lax.rsqrt(jnp.mean(centred * centred, axis=-1, keepdims=True) + EPS)
    return centred * inverse, inverse


def normalize_back(upstream, normal, inverse, gain):
    scaled = upstream * gain
    centred = (
        scaled
        - jnp.mean(scaled, axis=-1, keepdims=True)
        - normal * jnp.mean(scaled * normal, axis=-1, keepdims=True)
    )
    return inverse * centred, jnp.sum(upstream * normal, axis=0, keepdims=True)


ROOT = math.sqrt(2.0 / math.pi)
CUBE = 0.044715


def gelu(value):
    bent = jnp.tanh(ROOT * (value + CUBE * (value * value * value)))
    return 0.5 * value * (1.0 + bent)


def gelu_both(value):
    square = value * value
    bent = jnp.tanh(ROOT * (value + CUBE * (square * value)))
    half = 0.5 * (1.0 + bent)
    slope = half + (0.5 * ROOT) * value * (1.0 - bent * bent) * (1.0 + (3.0 * CUBE) * square)
    return value * half, slope


def softmax(scores):
    risen = jnp.exp(scores - jnp.max(scores, axis=-1, keepdims=True))
    return risen * (1.0 / jnp.sum(risen, axis=-1, keepdims=True))


def causal_bias(size, period):
    row = lax.broadcasted_iota(jnp.int32, (size, size), 0)
    col = lax.broadcasted_iota(jnp.int32, (size, size), 1)
    visible = (row >= col) & (((row ^ col) & (period - 1)) == 0)
    return jnp.where(visible, 0.0, -1e30).astype(F32)


def head_places(groups, tokens, features):
    return [
        (slice(i * tokens, (i + 1) * tokens), slice(m * features, (m + 1) * features))
        for i in range(groups)
        for m in range(HEADS)
    ]


def merge_heads(parts):
    pairs = [parts[i : i + HEADS] for i in range(0, len(parts), HEADS)]
    return jnp.concatenate([jnp.concatenate(pair, axis=1) for pair in pairs], axis=0)


def attend_back(up, query, key, value, probs, places, scaling):
    prob_grads = [mm_right_t(up[at], value[at]) for at in places]
    score_grads = []
    for prob, prob_grad in zip(probs, prob_grads):
        inner = jnp.sum(prob * prob_grad, axis=-1, keepdims=True)
        score_grads.append((prob * (prob_grad - inner)).astype(BF16))
    value_grads = [mm_left_t(prob.astype(BF16), up[at]).astype(BF16) for prob, at in zip(probs, places)]
    query_grads = [(mm(grad, key[at]) * scaling).astype(BF16) for grad, at in zip(score_grads, places)]
    key_grads = [(mm_left_t(grad, query[at]) * scaling).astype(BF16) for grad, at in zip(score_grads, places)]
    return tuple(merge_heads(grads) for grads in (query_grads, key_grads, value_grads))


def feed_back(normed, up_low, expand_ref, shrink_ref, acc, first, forward):
    width = normed.shape[-1]
    hidden_width = expand_ref.shape[1]
    tile = min(HIDDEN_TILE, hidden_width)
    result = None
    normed_grad = None
    for j in range(hidden_width // tile):
        cut = slice(j * tile, (j + 1) * tile)
        expand = expand_ref[:, cut]
        shrink = shrink_ref[cut, :]
        hidden, slope = gelu_both(mm(normed, expand))
        hidden = hidden.astype(BF16)
        if forward:
            part = mm(hidden, shrink)
            result = part if result is None else result + part
        expanded_grad = (slope * mm_right_t(up_low, shrink)).astype(BF16)
        at = first + j * width
        acc[at : at + width, :] += mm_left_t(normed, expanded_grad)
        at = first + hidden_width // tile * width + j * width
        acc[at : at + width, :] += mm_left_t(up_low, hidden)
        part = mm_right_t(expanded_grad, expand)
        normed_grad = part if normed_grad is None else normed_grad + part
    return result, normed_grad


def project_back(normed_low, grads, weight_refs, acc):
    width = normed_low.shape[-1]
    total = None
    for i, (grad, weight_ref) in enumerate(zip(grads, weight_refs)):
        acc[i * width : (i + 1) * width, :] += mm_left_t(normed_low, grad)
        part = mm_right_t(grad, weight_ref[...])
        total = part if total is None else total + part
    return total


def store_tail(ref, at, gains):
    high = gains.astype(BF16)
    ref[at : at + 8, :] = high
    ref[at + 8 : at + 16, :] = (gains - high.astype(F32)).astype(BF16)


def emit_grads(core, acc, gains, keep_ref, send_ref):
    half = acc.shape[0] // 2
    for which, (mine, other) in enumerate(((keep_ref, send_ref), (send_ref, keep_ref))):

        @pl.when(core == which)
        def _():
            mine[0:half, :] = acc[0:half, :].astype(BF16)
            other[0:half, :] = acc[half:, :].astype(BF16)

    store_tail(keep_ref, half, gains)
    store_tail(send_ref, half, gains)


def rows_forward_kernel(
    x_ref, ga_ref, wq_ref, wk_ref, wv_ref, wo_ref, gb_ref, w1_ref, w2_ref,
    send_ref, q_ref, k_ref, v_ref, att_ref, mid_ref, p_ref,
):
    rows, images, cols, width = x_ref.shape
    tokens = rows * images * cols
    features = width // HEADS
    scaling = 1.0 / math.sqrt(features)
    stream = x_ref[...].astype(F32).reshape(tokens, width)
    normed = (normalize(stream)[0] * ga_ref[...]).astype(BF16)
    query = mm(normed, wq_ref[...]).astype(BF16)
    key = mm(normed, wk_ref[...]).astype(BF16)
    value = mm(normed, wv_ref[...]).astype(BF16)
    q_ref[...] = query.reshape(q_ref.shape)
    k_ref[...] = key.reshape(q_ref.shape)
    v_ref[...] = value.reshape(q_ref.shape)
    bias = causal_bias(cols, 1)
    places = head_places(rows * images, cols, features)
    probs = [softmax(mm_right_t(query[at], key[at]) * scaling + bias) for at in places]
    heads = [mm(prob.astype(BF16), value[at]) for prob, at in zip(probs, places)]
    for i, prob in enumerate(probs):
        group, m = divmod(i, HEADS)
        p_ref[group // images, group % images, m] = prob
    attended = merge_heads(heads).astype(BF16)
    att_ref[...] = attended.reshape(att_ref.shape)
    middle = stream + mm(attended, wo_ref[...])
    mid_ref[...] = middle.reshape(mid_ref.shape)
    normed_b = (normalize(middle)[0] * gb_ref[...]).astype(BF16)
    hidden_width = w1_ref.shape[1]
    tile = min(HIDDEN_TILE, hidden_width)
    result = middle
    for j in range(hidden_width // tile):
        cut = slice(j * tile, (j + 1) * tile)
        hidden = gelu(mm(normed_b, w1_ref[:, cut])).astype(BF16)
        result = result + mm(hidden, w2_ref[cut, :])
    result = result.reshape(rows, images * cols // GROUP, GROUP, width)
    result = jnp.concatenate([result[r] for r in range(rows)], axis=1)
    send_ref[...] = result.astype(BF16).reshape(send_ref.shape)


def rows_backward_kernel(
    core_ref, up_ref, ga_ref, gb_ref, mid_hbm, w1_hbm, w2_hbm, att_hbm, wo_hbm,
    q_hbm, k_hbm, v_hbm, p_hbm, x_hbm, wq_hbm, wk_hbm, wv_hbm, _,
    grad_ref, keep_ref, send_ref,
    acc, gains, mid_ref, w1_ref, w2_ref, att_ref, wo_ref, q_ref, k_ref, v_ref, p_ref, x_ref, wq_ref, wk_ref, wv_ref, done,
):
    rows, all_images, cols, width = x_ref.shape
    step = pl.program_id(0)
    images = all_images // pl.num_programs(0)
    tokens = rows * images * cols
    here = pl.ds(step * images, images)
    features = width // HEADS
    scaling = 1.0 / math.sqrt(features)
    sources = (mid_hbm, w1_hbm, w2_hbm, att_hbm, wo_hbm, q_hbm, k_hbm, v_hbm, p_hbm, x_hbm, wq_hbm, wk_hbm, wv_hbm)
    targets = (mid_ref, w1_ref, w2_ref, att_ref, wo_ref, q_ref, k_ref, v_ref, p_ref, x_ref, wq_ref, wk_ref, wv_ref)
    copies = [pltpu.make_async_copy(sources[i], targets[i], done.at[i]) for i in range(len(sources))]

    def wait(first, last):
        @pl.when(step == 0)
        def _():
            for copy in copies[first:last]:
                copy.wait()

    @pl.when(step == 0)
    def _():
        for copy in copies:
            copy.start()
        acc[...] = jnp.zeros_like(acc)
        gains[...] = jnp.zeros_like(gains)

    wait(0, 3)
    up = up_ref[here].astype(F32).reshape(images * cols // GROUP, rows * GROUP, width)
    up = jnp.concatenate(
        [up[:, r * GROUP : (r + 1) * GROUP].reshape(images * cols, width) for r in range(rows)], axis=0
    )
    up_low = up.astype(BF16)
    normal_b, inverse_b = normalize(mid_ref[:, here].reshape(tokens, width))
    normed_b = (normal_b * gb_ref[...]).astype(BF16)
    _, normed_grad = feed_back(normed_b, up_low, w1_ref, w2_ref, acc, 4 * width, False)
    middle_norm, scale_grad = normalize_back(normed_grad, normal_b, inverse_b, gb_ref[...])
    gains[1:2, :] += scale_grad
    middle_grad = up + middle_norm
    middle_low = middle_grad.astype(BF16)
    wait(3, len(sources))
    acc[3 * width : 4 * width, :] += mm_left_t(att_ref[:, here].reshape(tokens, width), middle_low)
    up_att = mm_right_t(middle_low, wo_ref[...]).astype(BF16)
    query = q_ref[:, here].reshape(tokens, width)
    key = k_ref[:, here].reshape(tokens, width)
    value = v_ref[:, here].reshape(tokens, width)
    places = head_places(rows * images, cols, features)
    probs = [p_ref[r, step * images + i, m] for r in range(rows) for i in range(images) for m in range(HEADS)]
    grads = attend_back(up_att, query, key, value, probs, places, scaling)
    normal_a, inverse_a = normalize(x_ref[:, here].astype(F32).reshape(tokens, width))
    normed_a = (normal_a * ga_ref[...]).astype(BF16)
    normed_grad = project_back(normed_a, grads, (wq_ref, wk_ref, wv_ref), acc)
    stream_norm, gain_grad = normalize_back(normed_grad, normal_a, inverse_a, ga_ref[...])
    gains[0:1, :] += gain_grad
    grad_ref[...] = (middle_grad + stream_norm).reshape(grad_ref.shape)

    @pl.when(step == pl.num_programs(0) - 1)
    def _():
        emit_grads(core_ref[0], acc, gains[...], keep_ref, send_ref)


def unpack_kernel(in_ref, _, out_ref):
    rows, images, cols, width = out_ref.shape
    array = in_ref[...].astype(F32).reshape(images * cols // GROUP, rows * GROUP, width)
    for r in range(rows):
        part = array[:, r * GROUP : (r + 1) * GROUP].reshape(images, cols, width)
        out_ref[r] = part.astype(BF16)


def load_groups(ref, first, groups):
    sources, _, height, width = ref.shape
    parts = [ref[:, first + i].astype(F32).reshape(sources * height, width) for i in range(groups)]
    return jnp.concatenate(parts, axis=0)


def store_groups(ref, first, groups, value):
    sources, _, height, width = ref.shape
    tokens = sources * height
    for i in range(groups):
        part = value[i * tokens : (i + 1) * tokens].reshape(sources, height, width)
        ref[:, first + i] = part.astype(ref.dtype)


def columns_kernel(
    core_ref, x_ref, up_ref, ga_ref, wq_ref, wk_ref, wv_ref, wo_ref, gb_ref, w1_ref, w2_ref,
    out_ref, grad_ref, keep_ref, send_ref, acc, gains, bias,
):
    width = x_ref.shape[-1]
    groups = x_ref.shape[1] // pl.num_programs(0)
    tokens = x_ref.shape[0] * x_ref.shape[2]
    features = width // HEADS
    scaling = 1.0 / math.sqrt(features)
    step = pl.program_id(0)

    @pl.when(step == 0)
    def _():
        acc[...] = jnp.zeros_like(acc)
        gains[...] = jnp.zeros_like(gains)
        bias[...] = causal_bias(tokens, GROUP)

    first = step * groups
    stream = load_groups(x_ref, first, groups)
    normal_a, inverse_a = normalize(stream)
    normed_a = (normal_a * ga_ref[...]).astype(BF16)
    query = mm(normed_a, wq_ref[...]).astype(BF16)
    key = mm(normed_a, wk_ref[...]).astype(BF16)
    value = mm(normed_a, wv_ref[...]).astype(BF16)
    places = head_places(groups, tokens, features)
    probs = [softmax(mm_right_t(query[at], key[at]) * scaling + bias[...]) for at in places]
    heads = [mm(prob.astype(BF16), value[at]) for prob, at in zip(probs, places)]

    attended = merge_heads(heads).astype(BF16)
    middle = stream + mm(attended, wo_ref[...])
    normal_b, inverse_b = normalize(middle)
    normed_b = (normal_b * gb_ref[...]).astype(BF16)
    up = load_groups(up_ref, first, groups)
    up_low = up.astype(BF16)
    result, normed_grad = feed_back(normed_b, up_low, w1_ref, w2_ref, acc, 4 * width, True)
    store_groups(out_ref, first, groups, middle + result)
    middle_norm, scale_grad = normalize_back(normed_grad, normal_b, inverse_b, gb_ref[...])
    gains[1:2, :] += scale_grad
    middle_grad = up + middle_norm
    middle_low = middle_grad.astype(BF16)
    acc[3 * width : 4 * width, :] += mm_left_t(attended, middle_low)
    up_att = mm_right_t(middle_low, wo_ref[...]).astype(BF16)
    grads = attend_back(up_att, query, key, value, probs, places, scaling)
    normed_grad = project_back(normed_a, grads, (wq_ref, wk_ref, wv_ref), acc)
    stream_norm, gain_grad = normalize_back(normed_grad, normal_a, inverse_a, ga_ref[...])
    gains[0:1, :] += gain_grad
    store_groups(grad_ref, first, groups, middle_grad + stream_norm)

    @pl.when(step == pl.num_programs(0) - 1)
    def _():
        emit_grads(core_ref[0], acc, gains[...], keep_ref, send_ref)


def whole(array):
    zeros = (0,) * array.ndim
    return pl.BlockSpec(array.shape, lambda i: zeros)


def whole_out(shape):
    zeros = (0,) * len(shape)
    return pl.BlockSpec(shape, lambda i: zeros)


SCALAR = pl.BlockSpec(memory_space=pltpu.SMEM)
HELD = pl.BlockSpec(memory_space=pltpu.VMEM)
UNREAD = pl.BlockSpec(memory_space=pl.ANY)


def held(array):
    return pltpu.with_memory_space_constraint(array, pltpu.VMEM)


def params(limit=VMEM_LIMIT):
    return pltpu.CompilerParams(vmem_limit_bytes=limit)


def shape_of(shape, dtype):
    return jax.ShapeDtypeStruct(shape, dtype)


def held_shape(shape, dtype):
    return pltpu.VMEM(shape, dtype)


def stored_shape(shape, dtype):
    return pltpu.HBM(shape, dtype)


def stored(array):
    return pltpu.with_memory_space_constraint(array, pltpu.HBM)


def grad_rows(width, hidden_width):
    tile = min(HIDDEN_TILE, hidden_width)
    return 4 * width + 2 * (hidden_width // tile) * width


def cost(*_):
    return pl.CostEstimate(flops=1, bytes_accessed=1, transcendentals=0)


def rows_forward(inputs, gains, matrices):
    rows, images, cols, width = inputs.shape
    low = stored_shape(inputs.shape, BF16)
    wq, wk, wv, wo, w1, w2 = matrices
    operands = [stored(array) for array in (inputs, gains[0], wq, wk, wv, wo, gains[1], w1, w2)]
    outs = [
        held_shape((images, cols // GROUP, rows * GROUP, width), BF16),
        low, low, low, low,
        stored_shape(inputs.shape, F32),
        stored_shape((rows, images, HEADS, cols, cols), F32),
    ]
    return pl.pallas_call(
        rows_forward_kernel,
        grid=(1,),
        in_specs=[whole(array) for array in operands],
        out_specs=[HELD] + [whole_out(out.shape) for out in outs[1:]],
        out_shape=outs,
        compiler_params=params(),
        cost_estimate=cost(),
        name="rows_forward",
    )(*operands)


def rows_backward(core, up, gains, kept, steps, after):
    rows, images, cols, width = kept[0].shape
    total = grad_rows(width, kept[1].shape[1])
    part = (total // 2 + TAIL, width)
    spec = pl.BlockSpec((rows, images // steps, cols, width), lambda i: (0, i, 0, 0))
    return pl.pallas_call(
        rows_backward_kernel,
        grid=(steps,),
        in_specs=[SCALAR] + [HELD] * 3 + [UNREAD] * (len(kept) + 1),
        out_specs=[spec, HELD, HELD],
        out_shape=[shape_of(kept[0].shape, F32), held_shape(part, BF16), held_shape(part, BF16)],
        scratch_shapes=[pltpu.VMEM((total, width), F32), pltpu.VMEM((8, width), F32)]
        + [pltpu.VMEM(array.shape, array.dtype) for array in kept]
        + [pltpu.SemaphoreType.DMA((len(kept),))],
        compiler_params=params(40 * 1024 * 1024),
        cost_estimate=cost(),
        name="rows_backward",
    )(core, held(up), *gains, *[stored(array) for array in kept], after)


def unpack(array, shape, after):
    return pl.pallas_call(
        unpack_kernel,
        in_specs=[HELD, UNREAD],
        out_specs=pl.BlockSpec(memory_space=pltpu.VMEM),
        out_shape=shape_of(shape, BF16),
        compiler_params=params(SMALL_LIMIT),
        cost_estimate=cost(),
        name="unpack",
    )(held(array), after)


def columns_both(core, stream, up, gains, matrices, steps):
    sources, groups, height, width = stream.shape
    total = grad_rows(width, matrices[4].shape[1])
    tokens = sources * height
    part = (total // 2 + TAIL, width)
    wq, wk, wv, wo, w1, w2 = matrices
    operands = [stored(array) for array in (gains[0], wq, wk, wv, wo, gains[1], w1, w2)]
    return pl.pallas_call(
        columns_kernel,
        grid=(steps,),
        in_specs=[SCALAR, HELD, HELD] + [whole(array) for array in operands],
        out_specs=[HELD] * 4,
        out_shape=[held_shape(stream.shape, BF16)] * 2 + [held_shape(part, BF16)] * 2,
        scratch_shapes=[
            pltpu.VMEM((total, width), F32),
            pltpu.VMEM((8, width), F32),
            pltpu.VMEM((tokens, tokens), F32),
        ],
        compiler_params=params(),
        cost_estimate=cost(),
        name="columns_both",
    )(core, held(stream), held(up), *operands)


def add_parts(refs, size):
    total, gains = None, None
    for ref in refs:
        rows = ref[0:size, :].astype(F32)
        tail = ref[size : size + 8, :].astype(F32) + ref[size + 8 : size + TAIL, :].astype(F32)
        total = rows if total is None else total + rows
        gains = tail if gains is None else gains + tail
    return total.astype(BF16), gains


def sum_split_kernel(count, size, ways, sends, at_ref, *refs):
    ins, rider, outs = refs[:count], refs[count + 1 : -1 - sends], refs[-1 - sends : -1]
    parts = refs[-1]
    total, gains = add_parts(ins, size)
    step = size // ways
    for j in range(ways):
        parts[j] = total[j * step : (j + 1) * step, :]
    for j, out in enumerate(outs):
        out[0:step, :] = parts[(at_ref[0] & (ways - 1)) ^ j]
        store_tail(out, step, gains)
        if rider and j:
            out[step + TAIL :, :] = rider[0][...]


def sum_split(at, arrays, size, ways, sends, after, rider=None, heavy=False):
    width = arrays[0].shape[1]
    step = size // ways
    extra = 0 if rider is None else rider.shape[0]
    shapes = [(step + TAIL + (extra if j else 0), width) for j in range(sends)]
    riders = [] if rider is None else [held(rider)]
    return pl.pallas_call(
        functools.partial(sum_split_kernel, len(arrays), size, ways, sends),
        in_specs=[SCALAR] + [HELD] * len(arrays) + [UNREAD] + [HELD] * len(riders),
        out_specs=[HELD] * sends,
        out_shape=[held_shape(shape, BF16) for shape in shapes],
        scratch_shapes=[pltpu.VMEM((ways, step, width), BF16)],
        compiler_params=params(SMALL_LIMIT),
        cost_estimate=small_cost(arrays, heavy),
        name="sum_split",
    )(at, *[held(array) for array in arrays], after, *riders)


def sum_last_kernel(count, size, *refs):
    ins, (part, tail) = refs[:count], refs[count + 1 :]
    total, gains = add_parts(ins, size)
    part[...] = total
    store_tail(tail, 0, gains)


def sum_last(arrays, size, after, heavy=False):
    width = arrays[0].shape[1]
    return pl.pallas_call(
        functools.partial(sum_last_kernel, len(arrays), size),
        in_specs=[HELD] * len(arrays) + [UNREAD],
        out_specs=[HELD] * 2,
        out_shape=[held_shape((size, width), BF16), held_shape((TAIL, width), BF16)],
        compiler_params=params(SMALL_LIMIT),
        cost_estimate=small_cost(arrays, heavy),
        name="sum_last",
    )(*[held(array) for array in arrays], after)


def join_kernel(ways, first, at_ref, *refs):
    ins, out = refs[:ways], refs[-1]
    size = out.shape[1]
    for j in range(ways):
        start = first if j else 0
        out[at_ref[0] ^ j] = ins[j][start : start + size, :]


def join(at, arrays, first, after):
    ways, (size, width) = len(arrays), arrays[0].shape
    joined = pl.pallas_call(
        functools.partial(join_kernel, ways, first),
        in_specs=[SCALAR] + [HELD] * ways + [UNREAD],
        out_specs=HELD,
        out_shape=held_shape((ways, size, width), BF16),
        compiler_params=params(SMALL_LIMIT),
        cost_estimate=small_cost(arrays),
        name="join",
    )(at, *[held(array) for array in arrays], after)
    return joined.reshape(ways * size, width)


def finish_kernel(buffers, at_ref, own_ref, other_ref, tail_ref, _, *refs):
    outs, halves = list(refs[:-1]), refs[-1]
    width = own_ref.shape[1]
    halves[at_ref[0]] = own_ref[...]
    halves[at_ref[0] ^ 1] = other_ref[...]
    gains = tail_ref[0:8, :].astype(F32) + tail_ref[8:16, :].astype(F32)
    first = 0
    for rows, kinds in buffers:
        at = 0
        for kind in kinds:
            out = outs.pop(0)
            if isinstance(kind, int):
                out[...] = gains[kind : kind + 1, :]
                continue
            for j in range(out.size // (width * width)):
                half, row = divmod(at * width, rows // 2)
                block = halves[half, first + row : first + row + width, :].astype(F32)
                if kind == "rows":
                    out[j * width : (j + 1) * width, :] = block.T
                else:
                    out[:, j * width : (j + 1) * width] = block
                at += 1
        first += rows // 2


def finish(at, own, other, tail, buffers, hidden_width, after):
    half, width = own.shape
    shapes = {"square": (width, width), "columns": (width, hidden_width), "rows": (hidden_width, width)}
    kinds = [kind for _, each in buffers for kind in each]
    outs = [shapes.get(kind, (1, width)) for kind in kinds]
    outs = pl.pallas_call(
        functools.partial(finish_kernel, buffers),
        grid=(1,),
        in_specs=[SCALAR, HELD, HELD, HELD, UNREAD],
        out_specs=[whole_out(shape) for shape in outs],
        out_shape=[shape_of(shape, F32) for shape in outs],
        scratch_shapes=[pltpu.VMEM((2, half, width), BF16)],
        compiler_params=params(24 * 1024 * 1024),
        cost_estimate=cost(),
        name="finish",
    )(at, held(own), held(other), held(tail), after)
    return [out.reshape(width) if isinstance(kind, int) else out for kind, out in zip(kinds, outs)]


def small_cost(arrays, heavy=False):
    moved = HEAVY if heavy else 1
    return pl.CostEstimate(flops=moved, bytes_accessed=moved, transcendentals=0)


class Exchange:
    def __init__(self, bits, scatter, flat, devices):
        self.bits, self.scatter = bits, scatter
        self.ways = 1 << len(bits)
        place = sum(((flat >> bit) & 1) << i for i, bit in enumerate(bits))
        self.place = jnp.reshape(place, (1,)).astype(jnp.int32)
        self.devices = devices

    def swap(self, array, member):
        mask = sum(1 << bit for i, bit in enumerate(self.bits) if (member >> i) & 1)
        return lax.ppermute(array, ALL, [(i, i ^ mask) for i in range(self.devices)])


class Chain:
    def __init__(self, exchanges, buffers, keep, send, hidden_width):
        self.pair, self.four, *self.others = exchanges
        self.rows = sum(rows for rows, _ in buffers) // 2
        self.arrays = [keep, self.pair.swap(send, 1)]
        self.token = keep
        self.buffers, self.hidden_width = buffers, hidden_width

    def cut(self, after, rider=None):
        ways = self.four.ways
        parts = sum_split(self.four.place, self.arrays, self.rows, ways, ways, after, rider)
        self.arrays = [parts[0]] + [self.four.swap(parts[j], j) for j in range(1, ways)]
        self.rows //= ways
        return parts[0]

    def add(self, after, heavy=False):
        exchange = self.others.pop(0)
        (part,) = sum_split(self.pair.place, self.arrays, self.rows, 1, 1, after, heavy=heavy)
        self.arrays = [part, exchange.swap(part, 1)]
        return part

    def last(self, after, heavy=False):
        self.part, self.tail = sum_last(self.arrays, self.rows, after, heavy)
        return self.part

    def spread(self):
        self.pieces = [self.part] + [self.four.swap(self.part, j) for j in range(1, self.four.ways)]
        self.first = 0

    def ride(self, chain):
        self.pieces = [self.part] + chain.arrays[1:]
        self.first = chain.rows + TAIL

    def join(self, after):
        self.own = join(self.four.place, self.pieces, self.first, after)
        self.other = self.pair.swap(self.own, 1)
        return self.own

    def finish(self, after):
        self.results = finish(self.pair.place, self.own, self.other, self.tail, self.buffers, self.hidden_width, after)
        return self.results[0]


def on_device(inputs, cotangent, *weights):
    rows, images, cols, width = inputs.shape
    groups = cols // GROUP
    height = lax.axis_size("row")
    devices = height * lax.axis_size("img")
    flat = lax.axis_index("img") * height + lax.axis_index("row")
    top = devices.bit_length() - 2
    exchanges = [Exchange([0], True, flat, devices), Exchange([top, 1], True, flat, devices)]
    exchanges += [Exchange([bit], False, flat, devices) for bit in range(2, top)]
    core = exchanges[0].place
    rows_gains = [weights[i].reshape(1, width) for i in (0, 5)]
    column_gains = [weights[i].reshape(1, width) for i in (8, 13)]
    matrices = [w for w in weights if w.ndim == 2]
    hidden_width = matrices[4].shape[1]
    owned = images * groups // height

    def to_columns(array):
        array = array.reshape(height, owned, rows * GROUP, width)
        return lax.all_to_all(array, "row", 0, 0, tiled=True)

    def to_rows(array):
        array = lax.all_to_all(array, "row", 0, 0, tiled=True)
        return array.reshape(images, groups, rows * GROUP, width)

    def gather_rows(array):
        array = array.reshape(rows, images, groups, GROUP, width)
        return array.transpose(1, 2, 0, 3, 4)

    squares = ("square",) * 4
    total = grad_rows(width, hidden_width)
    steps = 2 if images % 2 == 0 and owned % 2 == 0 else 1
    up = to_columns(gather_rows(cotangent))
    sent, query, key, value, attended, middle, probs = rows_forward(inputs, rows_gains, matrices[:6])
    sent, up = lax.optimization_barrier((sent, up))
    stream = to_columns(sent)
    final, between_grad, keep, send = columns_both(core, stream, up, column_gains, matrices[6:], steps)
    kinds = (0, *squares, 1, "columns", "rows")
    columns = Chain(exchanges, ((total, kinds),), keep, send, hidden_width)
    token = columns.cut(columns.token)
    token = columns.add(token)
    between_grad = to_rows(between_grad)
    between_grad, final, token = lax.optimization_barrier((between_grad, final, token))
    final = to_rows(final)
    wq, wk, wv, wo, w1, w2 = matrices[:6]
    kept = (middle, w1, w2, attended, wo, query, key, value, probs, inputs, wq, wk, wv)
    stream_grad, keep, send = rows_backward(core, between_grad, rows_gains, kept, steps, token)
    rows_chain = Chain(exchanges, ((total, kinds),), keep, send, hidden_width)
    token = rows_chain.token
    if PLACE == 0:
        token = final = unpack(final, inputs.shape, token)
    while len(columns.others):
        token = columns.add(token)
    token = rows_chain.cut(token)
    if PLACE == 1:
        token = final = unpack(final, inputs.shape, token)
    token = rows_chain.add(token)
    token = columns.last(token)
    columns.spread()
    while rows_chain.others:
        token = rows_chain.add(token)
    token = rows_chain.last(token)
    token = columns.join(token)
    rows_chain.spread()
    token = columns.finish(token)
    token = rows_chain.join(token)
    rows_chain.finish(token)
    c_gain, c_query, c_keys, c_values, c_mixer, c_scale, c_expand, c_shrink = columns.results
    r_gain, r_query, r_keys, r_values, r_mixer, r_scale, r_expand, r_shrink = rows_chain.results
    return (
        final, stream_grad,
        r_gain, r_query, r_keys, r_values, r_mixer, r_scale, r_expand, r_shrink,
        c_gain, c_query, c_keys, c_values, c_mixer, c_scale, c_expand, c_shrink,
    )


def solution(mesh):
    moved = P("row", "img", None, None)
    return jax.shard_map(
        on_device,
        mesh=mesh,
        in_specs=(moved, moved) + (P(),) * 16,
        out_specs=(moved, moved) + (P(),) * 16,
        check_vma=False,
    )
```

```python
import functools
import math

import jax
import jax.numpy as jnp
from jax import lax
from jax.experimental import pallas as pl
from jax.experimental.pallas import tpu as pltpu
from jax.sharding import PartitionSpec as P

HEADS = 2
EPS = 1e-05
GROUP = 8
TAIL = 16
HIDDEN_TILE = 256
VMEM_LIMIT = 24 * 1024 * 1024
SMALL_LIMIT = 12 * 1024 * 1024
ALL = ("img", "row")
F32 = jnp.float32
BF16 = jnp.bfloat16


def mm(left, right):
    return lax.dot_general(left, right, (((1,), (0,)), ((), ())), preferred_element_type=F32)


def mm_right_t(left, right):
    return lax.dot_general(left, right, (((1,), (1,)), ((), ())), preferred_element_type=F32)


def mm_left_t(left, right):
    return lax.dot_general(left, right, (((0,), (0,)), ((), ())), preferred_element_type=F32)


def normalize(stream):
    centred = stream - jnp.mean(stream, axis=-1, keepdims=True)
    inverse = lax.rsqrt(jnp.mean(centred * centred, axis=-1, keepdims=True) + EPS)
    return centred * inverse, inverse


def normalize_back(upstream, normal, inverse, gain):
    scaled = upstream * gain
    centred = (
        scaled
        - jnp.mean(scaled, axis=-1, keepdims=True)
        - normal * jnp.mean(scaled * normal, axis=-1, keepdims=True)
    )
    return inverse * centred, jnp.sum(upstream * normal, axis=0, keepdims=True)


ROOT = math.sqrt(2.0 / math.pi)
CUBE = 0.044715


def gelu_both(value):
    square = value * value
    bent = jnp.tanh(ROOT * (value + CUBE * (square * value)))
    half = 0.5 * (1.0 + bent)
    slope = half + (0.5 * ROOT) * value * (1.0 - bent * bent) * (1.0 + (3.0 * CUBE) * square)
    return value * half, slope


def softmax(scores):
    risen = jnp.exp(scores - jnp.max(scores, axis=-1, keepdims=True))
    return risen * (1.0 / jnp.sum(risen, axis=-1, keepdims=True))


def causal_bias(size, period):
    row = lax.broadcasted_iota(jnp.int32, (size, size), 0)
    col = lax.broadcasted_iota(jnp.int32, (size, size), 1)
    visible = (row >= col) & (((row ^ col) & (period - 1)) == 0)
    return jnp.where(visible, 0.0, -1e30).astype(F32)


def head_places(groups, tokens, features):
    return [
        (slice(i * tokens, (i + 1) * tokens), slice(m * features, (m + 1) * features))
        for i in range(groups)
        for m in range(HEADS)
    ]


def merge_heads(parts):
    pairs = [parts[i : i + HEADS] for i in range(0, len(parts), HEADS)]
    return jnp.concatenate([jnp.concatenate(pair, axis=1) for pair in pairs], axis=0)


def attend_back(up, query, key, value, probs, places, scaling):
    prob_grads = [mm_right_t(up[at], value[at]) for at in places]
    score_grads = []
    for prob, prob_grad in zip(probs, prob_grads):
        inner = jnp.sum(prob * prob_grad, axis=-1, keepdims=True)
        score_grads.append((prob * (prob_grad - inner)).astype(BF16))
    value_grads = [mm_left_t(prob.astype(BF16), up[at]).astype(BF16) for prob, at in zip(probs, places)]
    query_grads = [(mm(grad, key[at]) * scaling).astype(BF16) for grad, at in zip(score_grads, places)]
    key_grads = [(mm_left_t(grad, query[at]) * scaling).astype(BF16) for grad, at in zip(score_grads, places)]
    return tuple(merge_heads(grads) for grads in (query_grads, key_grads, value_grads))


def feed_back(normed, up_low, expand_ref, shrink_ref, put, first, forward):
    width = normed.shape[-1]
    hidden_width = expand_ref.shape[1]
    tile = min(HIDDEN_TILE, hidden_width)
    result = None
    normed_grad = None
    for j in range(hidden_width // tile):
        cut = slice(j * tile, (j + 1) * tile)
        expand = expand_ref[:, cut]
        shrink = shrink_ref[cut, :]
        hidden, slope = gelu_both(mm(normed, expand))
        hidden = hidden.astype(BF16)
        if forward:
            part = mm(hidden, shrink)
            result = part if result is None else result + part
        expanded_grad = (slope * mm_right_t(up_low, shrink)).astype(BF16)
        put(first + j, mm_left_t(normed, expanded_grad))
        put(first + hidden_width // tile + j, mm_left_t(up_low, hidden))
        part = mm_right_t(expanded_grad, expand)
        normed_grad = part if normed_grad is None else normed_grad + part
    return result, normed_grad


def project_back(normed_low, grads, weight_refs, put):
    total = None
    for i, (grad, weight_ref) in enumerate(zip(grads, weight_refs)):
        put(i, mm_left_t(normed_low, grad))
        part = mm_right_t(grad, weight_ref[...])
        total = part if total is None else total + part
    return total


def store_tail(ref, at, gains):
    high = gains.astype(BF16)
    ref[at : at + 8, :] = high
    ref[at + 8 : at + 16, :] = (gains - high.astype(F32)).astype(BF16)


def putter(core, halves):
    width = halves.shape[2]
    blocks = halves.shape[1] // width

    def put(block, value):
        half, row = divmod(block, blocks)
        halves[half ^ core, row * width : (row + 1) * width, :] = value.astype(BF16)

    return put


def emit_grads(halves, gains, keep_ref, send_ref):
    for i, ref in enumerate((keep_ref, send_ref)):
        ref[0 : halves.shape[1], :] = halves[i]
        store_tail(ref, halves.shape[1], gains)


def stack_gains(gain, scale):
    return jnp.concatenate([gain, scale, jnp.zeros((6, gain.shape[1]), F32)], axis=0)


def rows_forward_kernel(
    x_ref, ga_ref, wq_ref, wk_ref, wv_ref, wo_ref, gb_ref, w1_ref, w2_ref,
    send_ref, q_ref, k_ref, v_ref, att_ref, mid_ref, p_ref, hidden_ref, slope_ref,
):
    rows, images, cols, width = x_ref.shape
    tokens = rows * images * cols
    features = width // HEADS
    scaling = 1.0 / math.sqrt(features)
    stream = x_ref[...].astype(F32).reshape(tokens, width)
    normed = (normalize(stream)[0] * ga_ref[...]).astype(BF16)
    query = mm(normed, wq_ref[...]).astype(BF16)
    key = mm(normed, wk_ref[...]).astype(BF16)
    value = mm(normed, wv_ref[...]).astype(BF16)
    q_ref[...] = query.reshape(q_ref.shape)
    k_ref[...] = key.reshape(q_ref.shape)
    v_ref[...] = value.reshape(q_ref.shape)
    bias = causal_bias(cols, 1)
    places = head_places(rows * images, cols, features)
    probs = [softmax(mm_right_t(query[at], key[at]) * scaling + bias) for at in places]
    heads = [mm(prob.astype(BF16), value[at]) for prob, at in zip(probs, places)]
    for i, prob in enumerate(probs):
        group, m = divmod(i, HEADS)
        p_ref[group // images, group % images, m] = prob
    attended = merge_heads(heads).astype(BF16)
    att_ref[...] = attended.reshape(att_ref.shape)
    middle = stream + mm(attended, wo_ref[...])
    mid_ref[...] = middle.reshape(mid_ref.shape)
    normed_b = (normalize(middle)[0] * gb_ref[...]).astype(BF16)
    hidden_width = w1_ref.shape[1]
    tile = min(HIDDEN_TILE, hidden_width)
    result = middle
    for j in range(hidden_width // tile):
        cut = slice(j * tile, (j + 1) * tile)
        hidden, slope = gelu_both(mm(normed_b, w1_ref[:, cut]))
        hidden = hidden.astype(BF16)
        hidden_ref[j] = hidden
        slope_ref[j] = slope
        result = result + mm(hidden, w2_ref[cut, :])
    result = result.astype(BF16).reshape(rows, images, cols, width)
    part = send_ref.shape[2]
    for i in range(send_ref.shape[0]):
        image, first = divmod(i * part, cols)
        send_ref[i] = result[:, image, first : first + part]


def rows_backward_kernel(
    core_ref, up_ref, ga_ref, gb_ref, w2_hbm, slope_hbm, mid_hbm, w1_hbm, hidden_hbm, att_hbm, wo_hbm,
    q_hbm, k_hbm, v_hbm, p_hbm, x_hbm, wq_hbm, wk_hbm, wv_hbm, _,
    mid_grad_ref, dq_ref, dk_ref, dv_ref, keep_ref, send_ref,
    halves, w2_ref, slope_ref, mid_ref, w1_ref, hidden_ref, att_ref, wo_ref,
    q_ref, k_ref, v_ref, p_ref, x_ref, wq_ref, wk_ref, wv_ref, done,
):
    rows, images, cols, width = x_ref.shape
    tokens = rows * images * cols
    features = width // HEADS
    scaling = 1.0 / math.sqrt(features)
    sources = (
        w2_hbm, slope_hbm, mid_hbm, w1_hbm, hidden_hbm, att_hbm, wo_hbm,
        q_hbm, k_hbm, v_hbm, p_hbm, x_hbm, wq_hbm, wk_hbm, wv_hbm,
    )
    targets = (
        w2_ref, slope_ref, mid_ref, w1_ref, hidden_ref, att_ref, wo_ref,
        q_ref, k_ref, v_ref, p_ref, x_ref, wq_ref, wk_ref, wv_ref,
    )
    copies = [pltpu.make_async_copy(sources[i], targets[i], done.at[i]) for i in range(len(sources))]
    for copy in copies:
        copy.start()
    put = putter(core_ref[0], halves)
    up = jnp.concatenate([up_ref[:, r].reshape(images * cols, width) for r in range(rows)], axis=0).astype(F32)
    up_low = up.astype(BF16)
    tiles, _, tile = slope_ref.shape
    copies[0].wait()
    hidden_grads = [mm_right_t(up_low, w2_ref[j * tile : (j + 1) * tile, :]) for j in range(tiles)]
    for copy in copies[1:5]:
        copy.wait()
    normal_b, inverse_b = normalize(mid_ref[...].reshape(tokens, width))
    normed_b = (normal_b * gb_ref[...]).astype(BF16)
    normed_grad = None
    for j in range(tiles):
        expanded_grad = (slope_ref[j] * hidden_grads[j]).astype(BF16)
        put(4 + j, mm_left_t(normed_b, expanded_grad))
        put(4 + tiles + j, mm_left_t(up_low, hidden_ref[j]))
        part = mm_right_t(expanded_grad, w1_ref[:, j * tile : (j + 1) * tile])
        normed_grad = part if normed_grad is None else normed_grad + part
    middle_norm, scale_grad = normalize_back(normed_grad, normal_b, inverse_b, gb_ref[...])
    middle_grad = up + middle_norm
    mid_grad_ref[...] = middle_grad
    middle_low = middle_grad.astype(BF16)
    for copy in copies[5:]:
        copy.wait()
    put(3, mm_left_t(att_ref[...].reshape(tokens, width), middle_low))
    up_att = mm_right_t(middle_low, wo_ref[...]).astype(BF16)
    query = q_ref[...].reshape(tokens, width)
    key = k_ref[...].reshape(tokens, width)
    value = v_ref[...].reshape(tokens, width)
    places = head_places(rows * images, cols, features)
    probs = [p_ref[r, i, m] for r in range(rows) for i in range(images) for m in range(HEADS)]
    grads = attend_back(up_att, query, key, value, probs, places, scaling)
    normed_a = (normalize(x_ref[...].astype(F32).reshape(tokens, width))[0] * ga_ref[...]).astype(BF16)
    shared = None
    for i, (grad, target, weight_ref) in enumerate(zip(grads, (dq_ref, dk_ref, dv_ref), (wq_ref, wk_ref, wv_ref))):
        target[...] = grad
        weight_grad = mm_left_t(normed_a, grad)
        put(i, weight_grad)
        part = weight_grad * weight_ref[...].astype(F32)
        shared = part if shared is None else shared + part
    gain_grad = jnp.sum(shared.T, axis=0, keepdims=True) / ga_ref[...]
    emit_grads(halves, stack_gains(gain_grad, scale_grad), keep_ref, send_ref)


def rows_rest_kernel(mid_grad_ref, dq_ref, dk_ref, dv_ref, x_ref, ga_ref, wq_ref, wk_ref, wv_ref, _, grad_ref, token_ref):
    rows, images, cols, width = x_ref.shape
    normal, inverse = normalize(x_ref[...].astype(F32).reshape(rows * images * cols, width))
    normed_grad = None
    for grad_ref_in, weight_ref in zip((dq_ref, dk_ref, dv_ref), (wq_ref, wk_ref, wv_ref)):
        part = mm_right_t(grad_ref_in[...], weight_ref[...])
        normed_grad = part if normed_grad is None else normed_grad + part
    stream_norm, _ = normalize_back(normed_grad, normal, inverse, ga_ref[...])
    grad_ref[...] = (mid_grad_ref[...] + stream_norm).reshape(grad_ref.shape)
    token_ref[...] = jnp.zeros_like(token_ref)


def unpack_kernel(in_ref, _, out_ref, token_ref, done):
    part, cols = in_ref.shape[2], out_ref.shape[2]
    copies = []
    for i in range(in_ref.shape[0]):
        image, first = divmod(i * part, cols)
        target = out_ref.at[:, image, pl.ds(first, part)]
        copies.append(pltpu.make_async_copy(in_ref.at[i], target, done.at[i]))
    for copy in copies:
        copy.start()
    token_ref[...] = jnp.zeros_like(token_ref)
    for copy in copies:
        copy.wait()


def load_groups(ref):
    array = ref[...].astype(F32)
    width = array.shape[-1]
    parts = [array[:, :, i : i + GROUP].reshape(-1, width) for i in range(0, array.shape[2], GROUP)]
    return jnp.concatenate(parts, axis=0)


def store_groups(ref, value):
    sources, rows, cols, width = ref.shape
    groups = cols // GROUP
    tokens = sources * rows * GROUP
    parts = [value[i * tokens : (i + 1) * tokens].reshape(sources, rows, GROUP, width) for i in range(groups)]
    ref[...] = jnp.concatenate(parts, axis=2).astype(ref.dtype)


def columns_kernel(
    core_ref, x_ref, up_ref, ga_ref, gb_ref, wq_hbm, wk_hbm, wv_hbm, wo_hbm, w1_hbm, w2_hbm,
    out_ref, grad_ref, keep_ref, send_ref,
    halves, bias, wq_ref, wk_ref, wv_ref, wo_ref, w1_ref, w2_ref, done,
):
    sources, rows, cols, width = x_ref.shape
    groups = cols // GROUP
    tokens = sources * rows * GROUP
    features = width // HEADS
    scaling = 1.0 / math.sqrt(features)
    froms = (wq_hbm, wk_hbm, wv_hbm, wo_hbm, w1_hbm, w2_hbm)
    targets = (wq_ref, wk_ref, wv_ref, wo_ref, w1_ref, w2_ref)
    copies = [pltpu.make_async_copy(froms[i], targets[i], done.at[i]) for i in range(len(froms))]
    for copy in copies:
        copy.start()
    put = putter(core_ref[0], halves)
    bias[...] = causal_bias(tokens, GROUP)
    stream = load_groups(x_ref)
    normal_a, inverse_a = normalize(stream)
    normed_a = (normal_a * ga_ref[...]).astype(BF16)
    for copy in copies[:4]:
        copy.wait()
    query = mm(normed_a, wq_ref[...]).astype(BF16)
    key = mm(normed_a, wk_ref[...]).astype(BF16)
    value = mm(normed_a, wv_ref[...]).astype(BF16)
    places = head_places(groups, tokens, features)
    probs = [softmax(mm_right_t(query[at], key[at]) * scaling + bias[...]) for at in places]
    heads = [mm(prob.astype(BF16), value[at]) for prob, at in zip(probs, places)]
    attended = merge_heads(heads).astype(BF16)
    middle = stream + mm(attended, wo_ref[...])
    normal_b, inverse_b = normalize(middle)
    normed_b = (normal_b * gb_ref[...]).astype(BF16)
    up = load_groups(up_ref)
    up_low = up.astype(BF16)
    for copy in copies[4:]:
        copy.wait()
    result, normed_grad = feed_back(normed_b, up_low, w1_ref, w2_ref, put, 4, True)
    store_groups(out_ref, middle + result)
    middle_norm, scale_grad = normalize_back(normed_grad, normal_b, inverse_b, gb_ref[...])
    middle_grad = up + middle_norm
    middle_low = middle_grad.astype(BF16)
    put(3, mm_left_t(attended, middle_low))
    up_att = mm_right_t(middle_low, wo_ref[...]).astype(BF16)
    grads = attend_back(up_att, query, key, value, probs, places, scaling)
    normed_grad = project_back(normed_a, grads, (wq_ref, wk_ref, wv_ref), put)
    stream_norm, gain_grad = normalize_back(normed_grad, normal_a, inverse_a, ga_ref[...])
    store_groups(grad_ref, middle_grad + stream_norm)
    emit_grads(halves, stack_gains(gain_grad, scale_grad), keep_ref, send_ref)


def whole(array):
    zeros = (0,) * array.ndim
    return pl.BlockSpec(array.shape, lambda i: zeros)


def whole_out(shape):
    zeros = (0,) * len(shape)
    return pl.BlockSpec(shape, lambda i: zeros)


SCALAR = pl.BlockSpec(memory_space=pltpu.SMEM)
HELD = pl.BlockSpec(memory_space=pltpu.VMEM)
UNREAD = pl.BlockSpec(memory_space=pl.ANY)


def held(array):
    return pltpu.with_memory_space_constraint(array, pltpu.VMEM)


def params(limit=VMEM_LIMIT):
    return pltpu.CompilerParams(vmem_limit_bytes=limit)


def shape_of(shape, dtype):
    return jax.ShapeDtypeStruct(shape, dtype)


def held_shape(shape, dtype):
    return pltpu.VMEM(shape, dtype)


def stored_shape(shape, dtype):
    return pltpu.HBM(shape, dtype)


def stored(array):
    return pltpu.with_memory_space_constraint(array, pltpu.HBM)


def grad_rows(width, hidden_width):
    tile = min(HIDDEN_TILE, hidden_width)
    return 4 * width + 2 * (hidden_width // tile) * width


def cost(*_):
    return pl.CostEstimate(flops=1, bytes_accessed=1, transcendentals=0)


def rows_forward(inputs, gains, matrices, sent_shape):
    rows, images, cols, width = inputs.shape
    low = stored_shape(inputs.shape, BF16)
    wq, wk, wv, wo, w1, w2 = matrices
    tile = min(HIDDEN_TILE, w1.shape[1])
    feed = (w1.shape[1] // tile, rows * images * cols, tile)
    operands = [stored(array) for array in (inputs, gains[0], wq, wk, wv, wo, gains[1], w1, w2)]
    outs = [
        held_shape(sent_shape, BF16),
        low, low, low, low,
        stored_shape(inputs.shape, F32),
        stored_shape((rows, images, HEADS, cols, cols), F32),
        stored_shape(feed, BF16),
        stored_shape(feed, F32),
    ]
    return pl.pallas_call(
        rows_forward_kernel,
        grid=(1,),
        in_specs=[whole(array) for array in operands],
        out_specs=[HELD] + [whole_out(out.shape) for out in outs[1:]],
        out_shape=outs,
        compiler_params=params(48 * 1024 * 1024),
        cost_estimate=cost(),
        name="rows_forward",
    )(*operands)


def rows_backward(core, up, gains, kept, after):
    tokens, width = kept[1].shape[1], kept[2].shape[-1]
    half = grad_rows(width, kept[0].shape[0]) // 2
    part = held_shape((half + TAIL, width), BF16)
    grad = held_shape((tokens, width), BF16)
    return pl.pallas_call(
        rows_backward_kernel,
        in_specs=[SCALAR] + [HELD] * 3 + [UNREAD] * (len(kept) + 1),
        out_specs=[HELD] * 6,
        out_shape=[held_shape((tokens, width), F32), grad, grad, grad, part, part],
        scratch_shapes=[pltpu.VMEM((2, half, width), BF16)]
        + [pltpu.VMEM(array.shape, array.dtype) for array in kept]
        + [pltpu.SemaphoreType.DMA((len(kept),))],
        compiler_params=params(48 * 1024 * 1024),
        cost_estimate=cost(),
        name="rows_backward",
    )(core, held(up), *gains, *[stored(array) for array in kept], after)


def rows_rest(grads, inputs, gain, matrices, after):
    operands = [stored(array) for array in (inputs, gain, *matrices)]
    return pl.pallas_call(
        rows_rest_kernel,
        grid=(1,),
        in_specs=[HELD] * 4 + [whole(array) for array in operands] + [UNREAD],
        out_specs=[whole_out(inputs.shape), HELD],
        out_shape=[stored_shape(inputs.shape, F32), held_shape((8, 128), F32)],
        compiler_params=params(24 * 1024 * 1024),
        cost_estimate=cost(),
        name="rows_rest",
    )(*[held(grad) for grad in grads], *operands, after)


def unpack(array, shape, after):
    return pl.pallas_call(
        unpack_kernel,
        in_specs=[HELD, UNREAD],
        out_specs=[UNREAD, HELD],
        out_shape=[stored_shape(shape, BF16), held_shape((8, 128), F32)],
        scratch_shapes=[pltpu.SemaphoreType.DMA((array.shape[0],))],
        compiler_params=params(SMALL_LIMIT),
        cost_estimate=cost(),
        name="unpack",
    )(held(array), after)


def columns_both(core, stream, up, gains, matrices):
    sources, rows, cols, width = stream.shape
    half = grad_rows(width, matrices[4].shape[1]) // 2
    tokens = sources * rows * GROUP
    part = (half + TAIL, width)
    return pl.pallas_call(
        columns_kernel,
        in_specs=[SCALAR] + [HELD] * 4 + [UNREAD] * len(matrices),
        out_specs=[HELD] * 4,
        out_shape=[held_shape(stream.shape, BF16)] * 2 + [held_shape(part, BF16)] * 2,
        scratch_shapes=[pltpu.VMEM((2, half, width), BF16), pltpu.VMEM((tokens, tokens), F32)]
        + [pltpu.VMEM(array.shape, array.dtype) for array in matrices]
        + [pltpu.SemaphoreType.DMA((len(matrices),))],
        compiler_params=params(40 * 1024 * 1024),
        cost_estimate=cost(),
        name="columns_both",
    )(core, held(stream), held(up), *gains, *[stored(array) for array in matrices])


def add_parts(refs, size):
    total, gains = None, None
    for ref in refs:
        rows = ref[0:size, :].astype(F32)
        tail = ref[size : size + 8, :].astype(F32) + ref[size + 8 : size + TAIL, :].astype(F32)
        total = rows if total is None else total + rows
        gains = tail if gains is None else gains + tail
    return total.astype(BF16), gains


def sum_split_kernel(count, size, ways, sends, at_ref, *refs):
    ins, rider, outs = refs[:count], refs[count + 1 : -1 - sends], refs[-1 - sends : -1]
    parts = refs[-1]
    total, gains = add_parts(ins, size)
    step = size // ways
    for j in range(ways):
        parts[j] = total[j * step : (j + 1) * step, :]
    for j, out in enumerate(outs):
        out[0:step, :] = parts[(at_ref[0] & (ways - 1)) ^ j]
        store_tail(out, step, gains)
        if rider and j:
            out[step + TAIL :, :] = rider[0][...]


def sum_split(at, arrays, size, ways, sends, after, rider=None):
    width = arrays[0].shape[1]
    step = size // ways
    extra = 0 if rider is None else rider.shape[0]
    shapes = [(step + TAIL + (extra if j else 0), width) for j in range(sends)]
    riders = [] if rider is None else [held(rider)]
    return pl.pallas_call(
        functools.partial(sum_split_kernel, len(arrays), size, ways, sends),
        in_specs=[SCALAR] + [HELD] * len(arrays) + [UNREAD] + [HELD] * len(riders),
        out_specs=[HELD] * sends,
        out_shape=[held_shape(shape, BF16) for shape in shapes],
        scratch_shapes=[pltpu.VMEM((ways, step, width), BF16)],
        compiler_params=params(SMALL_LIMIT),
        cost_estimate=small_cost(arrays),
        name="sum_split",
    )(at, *[held(array) for array in arrays], after, *riders)


def sum_last_kernel(count, size, *refs):
    ins, (part, tail) = refs[:count], refs[count + 1 :]
    total, gains = add_parts(ins, size)
    part[...] = total
    store_tail(tail, 0, gains)


def sum_last(arrays, size, after):
    width = arrays[0].shape[1]
    return pl.pallas_call(
        functools.partial(sum_last_kernel, len(arrays), size),
        in_specs=[HELD] * len(arrays) + [UNREAD],
        out_specs=[HELD] * 2,
        out_shape=[held_shape((size, width), BF16), held_shape((TAIL, width), BF16)],
        compiler_params=params(SMALL_LIMIT),
        cost_estimate=small_cost(arrays),
        name="sum_last",
    )(*[held(array) for array in arrays], after)


def join_kernel(ways, first, at_ref, *refs):
    ins, out = refs[:ways], refs[-1]
    size = out.shape[1]
    for j in range(ways):
        start = first if j else 0
        out[at_ref[0] ^ j] = ins[j][start : start + size, :]


def join(at, arrays, first, after):
    ways, (size, width) = len(arrays), arrays[0].shape
    joined = pl.pallas_call(
        functools.partial(join_kernel, ways, first),
        in_specs=[SCALAR] + [HELD] * ways + [UNREAD],
        out_specs=HELD,
        out_shape=held_shape((ways, size, width), BF16),
        compiler_params=params(SMALL_LIMIT),
        cost_estimate=small_cost(arrays),
        name="join",
    )(at, *[held(array) for array in arrays], after)
    return joined.reshape(ways * size, width)


def finish_kernel(buffers, at_ref, own_ref, other_ref, tail_ref, _, *refs):
    *outs, token_ref, halves = refs
    token_ref[...] = jnp.zeros_like(token_ref)
    width = own_ref.shape[1]
    halves[at_ref[0]] = own_ref[...]
    halves[at_ref[0] ^ 1] = other_ref[...]
    gains = tail_ref[0:8, :].astype(F32) + tail_ref[8:16, :].astype(F32)
    first = 0
    for rows, kinds in buffers:
        at = 0
        for kind in kinds:
            out = outs.pop(0)
            if isinstance(kind, int):
                out[...] = gains[kind : kind + 1, :]
                continue
            for j in range(out.size // (width * width)):
                half, row = divmod(at * width, rows // 2)
                block = halves[half, first + row : first + row + width, :].astype(F32)
                if kind == "rows":
                    out[j * width : (j + 1) * width, :] = block.T
                else:
                    out[:, j * width : (j + 1) * width] = block
                at += 1
        first += rows // 2


def finish(at, own, other, tail, buffers, hidden_width, after):
    half, width = own.shape
    shapes = {"square": (width, width), "columns": (width, hidden_width), "rows": (hidden_width, width)}
    kinds = [kind for _, each in buffers for kind in each]
    outs = [shapes.get(kind, (1, width)) for kind in kinds]
    *outs, token = pl.pallas_call(
        functools.partial(finish_kernel, buffers),
        grid=(1,),
        in_specs=[SCALAR, HELD, HELD, HELD, UNREAD],
        out_specs=[whole_out(shape) for shape in outs] + [HELD],
        out_shape=[shape_of(shape, F32) for shape in outs] + [held_shape((8, 128), F32)],
        scratch_shapes=[pltpu.VMEM((2, half, width), BF16)],
        compiler_params=params(24 * 1024 * 1024),
        cost_estimate=cost(),
        name="finish",
    )(at, held(own), held(other), held(tail), after)
    return [out.reshape(width) if isinstance(kind, int) else out for kind, out in zip(kinds, outs)], token


def small_cost(arrays):
    return pl.CostEstimate(flops=1, bytes_accessed=1, transcendentals=0)


class Exchange:
    def __init__(self, bits, scatter, flat, devices):
        self.bits, self.scatter = bits, scatter
        self.ways = 1 << len(bits)
        place = sum(((flat >> bit) & 1) << i for i, bit in enumerate(bits))
        self.place = jnp.reshape(place, (1,)).astype(jnp.int32)
        self.devices = devices

    def swap(self, array, member):
        mask = sum(1 << bit for i, bit in enumerate(self.bits) if (member >> i) & 1)
        return lax.ppermute(array, ALL, [(i, i ^ mask) for i in range(self.devices)])


class Chain:
    def __init__(self, exchanges, buffers, keep, send, hidden_width):
        self.pair, self.four, *self.others = exchanges
        self.rows = sum(rows for rows, _ in buffers) // 2
        self.arrays = [keep, self.pair.swap(send, 1)]
        self.token = keep
        self.buffers, self.hidden_width = buffers, hidden_width

    def cut(self, after, rider=None):
        ways = self.four.ways
        parts = sum_split(self.four.place, self.arrays, self.rows, ways, ways, after, rider)
        self.arrays = [parts[0]] + [self.four.swap(parts[j], j) for j in range(1, ways)]
        self.rows //= ways
        return parts[0]

    def add(self, after):
        exchange = self.others.pop(0)
        (part,) = sum_split(self.pair.place, self.arrays, self.rows, 1, 1, after)
        self.arrays = [part, exchange.swap(part, 1)]
        return part

    def last(self, after):
        self.part, self.tail = sum_last(self.arrays, self.rows, after)
        return self.part

    def spread(self):
        self.pieces = [self.part] + [self.four.swap(self.part, j) for j in range(1, self.four.ways)]
        self.first = 0

    def ride(self, chain):
        self.pieces = [self.part] + chain.arrays[1:]
        self.first = chain.rows + TAIL

    def join(self, after):
        self.own = join(self.four.place, self.pieces, self.first, after)
        self.other = self.pair.swap(self.own, 1)
        return self.own

    def finish(self, after):
        self.results, token = finish(
            self.pair.place, self.own, self.other, self.tail, self.buffers, self.hidden_width, after
        )
        return token


def on_device(inputs, cotangent, *weights):
    rows, images, cols, width = inputs.shape
    height = lax.axis_size("row")
    devices = height * lax.axis_size("img")
    flat = lax.axis_index("img") * height + lax.axis_index("row")
    top = devices.bit_length() - 2
    exchanges = [Exchange([0], True, flat, devices), Exchange([top, 1], True, flat, devices)]
    exchanges += [Exchange([bit], False, flat, devices) for bit in range(2, top)]
    core = exchanges[0].place
    rows_gains = [weights[i].reshape(1, width) for i in (0, 5)]
    column_gains = [weights[i].reshape(1, width) for i in (8, 13)]
    matrices = [w for w in weights if w.ndim == 2]
    hidden_width = matrices[4].shape[1]
    owned = images * cols // height

    def trade(array):
        return lax.all_to_all(array, "row", 0, 0, tiled=True)

    squares = ("square",) * 4
    total = grad_rows(width, hidden_width)
    sent_shape = (height, rows, owned, width)
    up = cotangent.reshape(rows, height, owned, width).transpose(1, 0, 2, 3)
    up = trade(up)
    sent, query, key, value, attended, middle, probs, hidden, slope = rows_forward(
        inputs, rows_gains, matrices[:6], sent_shape
    )
    sent, up = lax.optimization_barrier((sent, up))
    stream = trade(sent)
    final, between_grad, keep, send = columns_both(core, stream, up, column_gains, matrices[6:])
    kinds = (0, *squares, 1, "columns", "rows")
    columns = Chain(exchanges, ((total, kinds),), keep, send, hidden_width)
    token = columns.add(columns.cut(columns.token))
    between_grad = trade(between_grad)
    between_grad, final, token = lax.optimization_barrier((between_grad, final, token))
    final = trade(final)
    wq, wk, wv, wo, w1, w2 = matrices[:6]
    kept = (w2, slope, middle, w1, hidden, attended, wo, query, key, value, probs, inputs, wq, wk, wv)
    *grads, keep, send = rows_backward(core, between_grad, rows_gains, kept, token)
    rows_chain = Chain(exchanges, ((total, kinds),), keep, send, hidden_width)
    token = rows_chain.cut(rows_chain.token)
    stream_grad, token = rows_rest(grads, inputs, rows_gains[0], (wq, wk, wv), token)
    while columns.others:
        token = columns.add(token)
    final, token = unpack(final, inputs.shape, token)
    token = rows_chain.add(token)
    token = columns.last(token)
    columns.spread()
    while rows_chain.others:
        token = rows_chain.add(token)
    token = rows_chain.last(token)
    token = columns.join(token)
    rows_chain.spread()
    token = columns.finish(token)
    token = rows_chain.join(token)
    rows_chain.finish(token)
    c_gain, c_query, c_keys, c_values, c_mixer, c_scale, c_expand, c_shrink = columns.results
    r_gain, r_query, r_keys, r_values, r_mixer, r_scale, r_expand, r_shrink = rows_chain.results
    return (
        final, stream_grad,
        r_gain, r_query, r_keys, r_values, r_mixer, r_scale, r_expand, r_shrink,
        c_gain, c_query, c_keys, c_values, c_mixer, c_scale, c_expand, c_shrink,
    )


def solution(mesh):
    moved = P("row", "img", None, None)
    return jax.shard_map(
        on_device,
        mesh=mesh,
        in_specs=(moved, moved) + (P(),) * 16,
        out_specs=(moved, moved) + (P(),) * 16,
        check_vma=False,
    )
```

```python
import functools
import math

import jax
import jax.numpy as jnp
from jax import lax
from jax.experimental import pallas as pl
from jax.experimental.pallas import tpu as pltpu
from jax.sharding import PartitionSpec as P

HEADS = 2
EPS = 1e-05
GROUP = 8
TAIL = 16
HIDDEN_TILE = 256
VMEM_LIMIT = 24 * 1024 * 1024
SMALL_LIMIT = 12 * 1024 * 1024
ALL = ("img", "row")
F32 = jnp.float32
BF16 = jnp.bfloat16


def mm(left, right):
    return lax.dot_general(left, right, (((1,), (0,)), ((), ())), preferred_element_type=F32)


def mm_right_t(left, right):
    return lax.dot_general(left, right, (((1,), (1,)), ((), ())), preferred_element_type=F32)


def mm_left_t(left, right):
    return lax.dot_general(left, right, (((0,), (0,)), ((), ())), preferred_element_type=F32)


def normalize(stream):
    centred = stream - jnp.mean(stream, axis=-1, keepdims=True)
    inverse = lax.rsqrt(jnp.mean(centred * centred, axis=-1, keepdims=True) + EPS)
    return centred * inverse, inverse


def normalize_back(upstream, normal, inverse, gain):
    scaled = upstream * gain
    centred = (
        scaled
        - jnp.mean(scaled, axis=-1, keepdims=True)
        - normal * jnp.mean(scaled * normal, axis=-1, keepdims=True)
    )
    return inverse * centred, jnp.sum(upstream * normal, axis=0, keepdims=True)


ROOT = math.sqrt(2.0 / math.pi)
CUBE = 0.044715


def gelu_both(value):
    square = value * value
    bent = jnp.tanh(ROOT * (value + CUBE * (square * value)))
    half = 0.5 * (1.0 + bent)
    slope = half + (0.5 * ROOT) * value * (1.0 - bent * bent) * (1.0 + (3.0 * CUBE) * square)
    return value * half, slope


def softmax(scores):
    risen = jnp.exp(scores - jnp.max(scores, axis=-1, keepdims=True))
    return risen * (1.0 / jnp.sum(risen, axis=-1, keepdims=True))


def causal_bias(size, period):
    row = lax.broadcasted_iota(jnp.int32, (size, size), 0)
    col = lax.broadcasted_iota(jnp.int32, (size, size), 1)
    visible = (row >= col) & (((row ^ col) & (period - 1)) == 0)
    return jnp.where(visible, 0.0, -1e30).astype(F32)


def head_places(groups, tokens, features):
    return [
        (slice(i * tokens, (i + 1) * tokens), slice(m * features, (m + 1) * features))
        for i in range(groups)
        for m in range(HEADS)
    ]


def merge_heads(parts):
    pairs = [parts[i : i + HEADS] for i in range(0, len(parts), HEADS)]
    return jnp.concatenate([jnp.concatenate(pair, axis=1) for pair in pairs], axis=0)


def attend_back(up, query, key, value, probs, places, scaling):
    prob_grads = [mm_right_t(up[at], value[at]) for at in places]
    score_grads = []
    for prob, prob_grad in zip(probs, prob_grads):
        inner = jnp.sum(prob * prob_grad, axis=-1, keepdims=True)
        score_grads.append((prob * (prob_grad - inner)).astype(BF16))
    value_grads = [mm_left_t(prob.astype(BF16), up[at]).astype(BF16) for prob, at in zip(probs, places)]
    query_grads = [(mm(grad, key[at]) * scaling).astype(BF16) for grad, at in zip(score_grads, places)]
    key_grads = [(mm_left_t(grad, query[at]) * scaling).astype(BF16) for grad, at in zip(score_grads, places)]
    return tuple(merge_heads(grads) for grads in (query_grads, key_grads, value_grads))


def feed_back(normed, up_low, expand_ref, shrink_ref, put, first, result_ref, grad_ref):
    hidden_width = expand_ref.shape[1]
    tile = min(HIDDEN_TILE, hidden_width)
    tiles = hidden_width // tile

    @pl.loop(0, tiles)
    def _(j):
        cut = pl.ds(pl.multiple_of(j * tile, tile), tile)
        expand = expand_ref[:, cut]
        shrink = shrink_ref[cut, :]
        hidden, slope = gelu_both(mm(normed, expand))
        hidden = hidden.astype(BF16)
        result_ref[...] += mm(hidden, shrink)
        expanded_grad = (slope * mm_right_t(up_low, shrink)).astype(BF16)
        put(first + j, mm_left_t(normed, expanded_grad))
        put(first + tiles + j, mm_left_t(up_low, hidden))
        grad_ref[...] += mm_right_t(expanded_grad, expand)


def project_back(normed_low, grads, weight_refs, put):
    total = None
    for i, (grad, weight_ref) in enumerate(zip(grads, weight_refs)):
        put(i, mm_left_t(normed_low, grad))
        part = mm_right_t(grad, weight_ref[...])
        total = part if total is None else total + part
    return total


def store_tail(ref, at, gains):
    high = gains.astype(BF16)
    ref[at : at + 8, :] = high
    ref[at + 8 : at + 16, :] = (gains - high.astype(F32)).astype(BF16)


def putter(core, halves):
    width = halves.shape[2]
    blocks = halves.shape[1] // width

    def put(block, value):
        start = pl.multiple_of(lax.rem(block, blocks) * width, width)
        halves[lax.div(block, blocks) ^ core, pl.ds(start, width), :] = value.astype(BF16)

    return put


def emit_grads(halves, gains, keep_ref, send_ref):
    for i, ref in enumerate((keep_ref, send_ref)):
        ref[0 : halves.shape[1], :] = halves[i]
        store_tail(ref, halves.shape[1], gains)


def stack_gains(gain, scale):
    return jnp.concatenate([gain, scale, jnp.zeros((6, gain.shape[1]), F32)], axis=0)


def rows_forward_kernel(
    x_ref, ga_ref, wq_ref, wk_ref, wv_ref, wo_ref, gb_ref, w1_ref, w2_ref,
    send_ref, q_ref, k_ref, v_ref, att_ref, mid_ref, p_ref, hidden_ref, slope_ref, result_ref,
):
    rows, images, cols, width = x_ref.shape
    tokens = rows * images * cols
    features = width // HEADS
    scaling = 1.0 / math.sqrt(features)
    stream = x_ref[...].astype(F32).reshape(tokens, width)
    normed = (normalize(stream)[0] * ga_ref[...]).astype(BF16)
    query = mm(normed, wq_ref[...]).astype(BF16)
    key = mm(normed, wk_ref[...]).astype(BF16)
    value = mm(normed, wv_ref[...]).astype(BF16)
    q_ref[...] = query.reshape(q_ref.shape)
    k_ref[...] = key.reshape(q_ref.shape)
    v_ref[...] = value.reshape(q_ref.shape)
    bias = causal_bias(cols, 1)
    places = head_places(rows * images, cols, features)
    probs = [softmax(mm_right_t(query[at], key[at]) * scaling + bias) for at in places]
    heads = [mm(prob.astype(BF16), value[at]) for prob, at in zip(probs, places)]
    for i, prob in enumerate(probs):
        group, m = divmod(i, HEADS)
        p_ref[group // images, group % images, m] = prob
    attended = merge_heads(heads).astype(BF16)
    att_ref[...] = attended.reshape(att_ref.shape)
    middle = stream + mm(attended, wo_ref[...])
    mid_ref[...] = middle.reshape(mid_ref.shape)
    normed_b = (normalize(middle)[0] * gb_ref[...]).astype(BF16)
    tiles, _, tile = hidden_ref.shape
    result_ref[...] = middle

    @pl.loop(0, tiles)
    def _(j):
        cut = pl.ds(pl.multiple_of(j * tile, tile), tile)
        hidden, slope = gelu_both(mm(normed_b, w1_ref[:, cut]))
        hidden = hidden.astype(BF16)
        hidden_ref[j] = hidden
        slope_ref[j] = slope
        result_ref[...] += mm(hidden, w2_ref[cut, :])

    result = result_ref[...]
    result = result.astype(BF16).reshape(rows, images, cols, width)
    part = send_ref.shape[2]
    for i in range(send_ref.shape[0]):
        image, first = divmod(i * part, cols)
        send_ref[i] = result[:, image, first : first + part]


def rows_backward_kernel(
    core_ref, up_ref, ga_ref, gb_ref, slope_hbm, hidden_hbm, w2_hbm, mid_hbm, w1_hbm, att_hbm, wo_hbm,
    q_hbm, k_hbm, v_hbm, p_hbm, x_hbm, wq_hbm, wk_hbm, wv_hbm, _,
    mid_grad_ref, dq_ref, dk_ref, dv_ref, keep_ref, send_ref,
    halves, feed_grad_ref, slope_ref, hidden_ref, w2_ref, mid_ref, w1_ref, att_ref, wo_ref,
    q_ref, k_ref, v_ref, p_ref, x_ref, wq_ref, wk_ref, wv_ref, done, tile_done,
):
    rows, images, cols, width = x_ref.shape
    tokens = rows * images * cols
    features = width // HEADS
    scaling = 1.0 / math.sqrt(features)
    sources = (
        w2_hbm, mid_hbm, w1_hbm, att_hbm, wo_hbm,
        q_hbm, k_hbm, v_hbm, p_hbm, x_hbm, wq_hbm, wk_hbm, wv_hbm,
    )
    targets = (
        w2_ref, mid_ref, w1_ref, att_ref, wo_ref,
        q_ref, k_ref, v_ref, p_ref, x_ref, wq_ref, wk_ref, wv_ref,
    )
    copies = [pltpu.make_async_copy(sources[i], targets[i], done.at[i]) for i in range(len(sources))]
    tiles, _, tile = slope_ref.shape

    def tile_copies(j):
        return (
            pltpu.make_async_copy(slope_hbm.at[j], slope_ref.at[j], tile_done.at[0, j]),
            pltpu.make_async_copy(hidden_hbm.at[j], hidden_ref.at[j], tile_done.at[1, j]),
        )

    for copy in copies[:3]:
        copy.start()
    for j in range(tiles):
        for copy in tile_copies(j):
            copy.start()
    for copy in copies[3:]:
        copy.start()
    put = putter(core_ref[0], halves)
    up = jnp.concatenate([up_ref[:, r].reshape(images * cols, width) for r in range(rows)], axis=0).astype(F32)
    up_low = up.astype(BF16)
    for copy in copies[:3]:
        copy.wait()
    normal_b, inverse_b = normalize(mid_ref[...].reshape(tokens, width))
    normed_b = (normal_b * gb_ref[...]).astype(BF16)
    feed_grad_ref[...] = jnp.zeros_like(feed_grad_ref)

    @pl.loop(0, tiles)
    def _(j):
        cut = pl.ds(pl.multiple_of(j * tile, tile), tile)
        hidden_grad = mm_right_t(up_low, w2_ref[cut, :])
        for copy in tile_copies(j):
            copy.wait()
        expanded_grad = (slope_ref[j] * hidden_grad).astype(BF16)
        put(4 + j, mm_left_t(normed_b, expanded_grad))
        put(4 + tiles + j, mm_left_t(up_low, hidden_ref[j]))
        feed_grad_ref[...] += mm_right_t(expanded_grad, w1_ref[:, cut])

    normed_grad = feed_grad_ref[...]
    middle_norm, scale_grad = normalize_back(normed_grad, normal_b, inverse_b, gb_ref[...])
    middle_grad = up + middle_norm
    mid_grad_ref[...] = middle_grad
    middle_low = middle_grad.astype(BF16)
    for copy in copies[3:]:
        copy.wait()
    put(3, mm_left_t(att_ref[...].reshape(tokens, width), middle_low))
    up_att = mm_right_t(middle_low, wo_ref[...]).astype(BF16)
    query = q_ref[...].reshape(tokens, width)
    key = k_ref[...].reshape(tokens, width)
    value = v_ref[...].reshape(tokens, width)
    places = head_places(rows * images, cols, features)
    probs = [p_ref[r, i, m] for r in range(rows) for i in range(images) for m in range(HEADS)]
    grads = attend_back(up_att, query, key, value, probs, places, scaling)
    normed_a = (normalize(x_ref[...].astype(F32).reshape(tokens, width))[0] * ga_ref[...]).astype(BF16)
    shared = None
    for i, (grad, target, weight_ref) in enumerate(zip(grads, (dq_ref, dk_ref, dv_ref), (wq_ref, wk_ref, wv_ref))):
        target[...] = grad
        weight_grad = mm_left_t(normed_a, grad)
        put(i, weight_grad)
        part = weight_grad * weight_ref[...].astype(F32)
        shared = part if shared is None else shared + part
    gain_grad = jnp.sum(shared.T, axis=0, keepdims=True) / ga_ref[...]
    emit_grads(halves, stack_gains(gain_grad, scale_grad), keep_ref, send_ref)


def rows_rest_kernel(mid_grad_ref, dq_ref, dk_ref, dv_ref, x_ref, ga_ref, wq_ref, wk_ref, wv_ref, _, grad_ref, token_ref):
    rows, images, cols, width = x_ref.shape
    normal, inverse = normalize(x_ref[...].astype(F32).reshape(rows * images * cols, width))
    normed_grad = None
    for grad_ref_in, weight_ref in zip((dq_ref, dk_ref, dv_ref), (wq_ref, wk_ref, wv_ref)):
        part = mm_right_t(grad_ref_in[...], weight_ref[...])
        normed_grad = part if normed_grad is None else normed_grad + part
    stream_norm, _ = normalize_back(normed_grad, normal, inverse, ga_ref[...])
    grad_ref[...] = (mid_grad_ref[...] + stream_norm).reshape(grad_ref.shape)
    token_ref[...] = jnp.zeros_like(token_ref)


def unpack_kernel(in_ref, _, out_ref, token_ref, done):
    part, cols = in_ref.shape[2], out_ref.shape[2]
    copies = []
    for i in range(in_ref.shape[0]):
        image, first = divmod(i * part, cols)
        target = out_ref.at[:, image, pl.ds(first, part)]
        copies.append(pltpu.make_async_copy(in_ref.at[i], target, done.at[i]))
    for copy in copies:
        copy.start()
    token_ref[...] = jnp.zeros_like(token_ref)
    for copy in copies:
        copy.wait()


def load_groups(ref):
    array = ref[...].astype(F32)
    width = array.shape[-1]
    parts = [array[:, :, i : i + GROUP].reshape(-1, width) for i in range(0, array.shape[2], GROUP)]
    return jnp.concatenate(parts, axis=0)


def store_groups(ref, value):
    sources, rows, cols, width = ref.shape
    groups = cols // GROUP
    tokens = sources * rows * GROUP
    parts = [value[i * tokens : (i + 1) * tokens].reshape(sources, rows, GROUP, width) for i in range(groups)]
    ref[...] = jnp.concatenate(parts, axis=2).astype(ref.dtype)


def columns_kernel(
    core_ref, x_ref, up_ref, ga_ref, gb_ref, wq_hbm, wk_hbm, wv_hbm, wo_hbm, w1_hbm, w2_hbm,
    out_ref, grad_ref, keep_ref, send_ref,
    halves, bias, result_ref, feed_grad_ref, wq_ref, wk_ref, wv_ref, wo_ref, w1_ref, w2_ref, done,
):
    sources, rows, cols, width = x_ref.shape
    groups = cols // GROUP
    tokens = sources * rows * GROUP
    features = width // HEADS
    scaling = 1.0 / math.sqrt(features)
    froms = (wq_hbm, wk_hbm, wv_hbm, wo_hbm, w1_hbm, w2_hbm)
    targets = (wq_ref, wk_ref, wv_ref, wo_ref, w1_ref, w2_ref)
    copies = [pltpu.make_async_copy(froms[i], targets[i], done.at[i]) for i in range(len(froms))]
    for copy in copies:
        copy.start()
    put = putter(core_ref[0], halves)
    bias[...] = causal_bias(tokens, GROUP)
    stream = load_groups(x_ref)
    normal_a, inverse_a = normalize(stream)
    normed_a = (normal_a * ga_ref[...]).astype(BF16)
    for copy in copies[:4]:
        copy.wait()
    query = mm(normed_a, wq_ref[...]).astype(BF16)
    key = mm(normed_a, wk_ref[...]).astype(BF16)
    value = mm(normed_a, wv_ref[...]).astype(BF16)
    places = head_places(groups, tokens, features)
    probs = [softmax(mm_right_t(query[at], key[at]) * scaling + bias[...]) for at in places]
    heads = [mm(prob.astype(BF16), value[at]) for prob, at in zip(probs, places)]
    attended = merge_heads(heads).astype(BF16)
    middle = stream + mm(attended, wo_ref[...])
    normal_b, inverse_b = normalize(middle)
    normed_b = (normal_b * gb_ref[...]).astype(BF16)
    up = load_groups(up_ref)
    up_low = up.astype(BF16)
    for copy in copies[4:]:
        copy.wait()
    result_ref[...] = middle
    feed_grad_ref[...] = jnp.zeros_like(feed_grad_ref)
    feed_back(normed_b, up_low, w1_ref, w2_ref, put, 4, result_ref, feed_grad_ref)
    store_groups(out_ref, result_ref[...])
    normed_grad = feed_grad_ref[...]
    middle_norm, scale_grad = normalize_back(normed_grad, normal_b, inverse_b, gb_ref[...])
    middle_grad = up + middle_norm
    middle_low = middle_grad.astype(BF16)
    put(3, mm_left_t(attended, middle_low))
    up_att = mm_right_t(middle_low, wo_ref[...]).astype(BF16)
    grads = attend_back(up_att, query, key, value, probs, places, scaling)
    normed_grad = project_back(normed_a, grads, (wq_ref, wk_ref, wv_ref), put)
    stream_norm, gain_grad = normalize_back(normed_grad, normal_a, inverse_a, ga_ref[...])
    store_groups(grad_ref, middle_grad + stream_norm)
    emit_grads(halves, stack_gains(gain_grad, scale_grad), keep_ref, send_ref)


def whole(array):
    zeros = (0,) * array.ndim
    return pl.BlockSpec(array.shape, lambda i: zeros)


def whole_out(shape):
    zeros = (0,) * len(shape)
    return pl.BlockSpec(shape, lambda i: zeros)


SCALAR = pl.BlockSpec(memory_space=pltpu.SMEM)
HELD = pl.BlockSpec(memory_space=pltpu.VMEM)
UNREAD = pl.BlockSpec(memory_space=pl.ANY)


def held(array):
    return pltpu.with_memory_space_constraint(array, pltpu.VMEM)


def params(limit=VMEM_LIMIT):
    return pltpu.CompilerParams(vmem_limit_bytes=limit)


def shape_of(shape, dtype):
    return jax.ShapeDtypeStruct(shape, dtype)


def held_shape(shape, dtype):
    return pltpu.VMEM(shape, dtype)


def stored_shape(shape, dtype):
    return pltpu.HBM(shape, dtype)


def stored(array):
    return pltpu.with_memory_space_constraint(array, pltpu.HBM)


def grad_rows(width, hidden_width):
    tile = min(HIDDEN_TILE, hidden_width)
    return 4 * width + 2 * (hidden_width // tile) * width


def cost(*_):
    return pl.CostEstimate(flops=1, bytes_accessed=1, transcendentals=0)


def rows_forward(inputs, gains, matrices, sent_shape):
    rows, images, cols, width = inputs.shape
    low = stored_shape(inputs.shape, BF16)
    wq, wk, wv, wo, w1, w2 = matrices
    tile = min(HIDDEN_TILE, w1.shape[1])
    feed = (w1.shape[1] // tile, rows * images * cols, tile)
    operands = [stored(array) for array in (inputs, gains[0], wq, wk, wv, wo, gains[1], w1, w2)]
    outs = [
        held_shape(sent_shape, BF16),
        low, low, low, low,
        stored_shape(inputs.shape, F32),
        stored_shape((rows, images, HEADS, cols, cols), F32),
        stored_shape(feed, BF16),
        stored_shape(feed, F32),
    ]
    return pl.pallas_call(
        rows_forward_kernel,
        grid=(1,),
        in_specs=[whole(array) for array in operands],
        out_specs=[HELD] + [whole_out(out.shape) for out in outs[1:]],
        out_shape=outs,
        scratch_shapes=[pltpu.VMEM((rows * images * cols, width), F32)],
        compiler_params=params(48 * 1024 * 1024),
        cost_estimate=cost(),
        name="rows_forward",
    )(*operands)


def rows_backward(core, up, gains, kept, after):
    tiles, tokens, _ = kept[0].shape
    hidden_width, width = kept[2].shape
    half = grad_rows(width, hidden_width) // 2
    part = held_shape((half + TAIL, width), BF16)
    grad = held_shape((tokens, width), BF16)
    return pl.pallas_call(
        rows_backward_kernel,
        in_specs=[SCALAR] + [HELD] * 3 + [UNREAD] * (len(kept) + 1),
        out_specs=[HELD] * 6,
        out_shape=[held_shape((tokens, width), F32), grad, grad, grad, part, part],
        scratch_shapes=[pltpu.VMEM((2, half, width), BF16), pltpu.VMEM((tokens, width), F32)]
        + [pltpu.VMEM(array.shape, array.dtype) for array in kept]
        + [pltpu.SemaphoreType.DMA((len(kept) - 2,)), pltpu.SemaphoreType.DMA((2, tiles))],
        compiler_params=params(48 * 1024 * 1024),
        cost_estimate=cost(),
        name="rows_backward",
    )(core, held(up), *gains, *[stored(array) for array in kept], after)


def rows_rest(grads, inputs, gain, matrices, after):
    operands = [stored(array) for array in (inputs, gain, *matrices)]
    return pl.pallas_call(
        rows_rest_kernel,
        grid=(1,),
        in_specs=[HELD] * 4 + [whole(array) for array in operands] + [UNREAD],
        out_specs=[whole_out(inputs.shape), HELD],
        out_shape=[stored_shape(inputs.shape, F32), held_shape((8, 128), F32)],
        compiler_params=params(24 * 1024 * 1024),
        cost_estimate=cost(),
        name="rows_rest",
    )(*[held(grad) for grad in grads], *operands, after)


def unpack(array, shape, after):
    return pl.pallas_call(
        unpack_kernel,
        in_specs=[HELD, UNREAD],
        out_specs=[UNREAD, HELD],
        out_shape=[stored_shape(shape, BF16), held_shape((8, 128), F32)],
        scratch_shapes=[pltpu.SemaphoreType.DMA((array.shape[0],))],
        compiler_params=params(SMALL_LIMIT),
        cost_estimate=cost(),
        name="unpack",
    )(held(array), after)


def columns_both(core, stream, up, gains, matrices):
    sources, rows, cols, width = stream.shape
    half = grad_rows(width, matrices[4].shape[1]) // 2
    tokens = sources * rows * GROUP
    part = (half + TAIL, width)
    return pl.pallas_call(
        columns_kernel,
        in_specs=[SCALAR] + [HELD] * 4 + [UNREAD] * len(matrices),
        out_specs=[HELD] * 4,
        out_shape=[held_shape(stream.shape, BF16)] * 2 + [held_shape(part, BF16)] * 2,
        scratch_shapes=[pltpu.VMEM((2, half, width), BF16), pltpu.VMEM((tokens, tokens), F32)]
        + [pltpu.VMEM((tokens * (cols // GROUP), width), F32)] * 2
        + [pltpu.VMEM(array.shape, array.dtype) for array in matrices]
        + [pltpu.SemaphoreType.DMA((len(matrices),))],
        compiler_params=params(40 * 1024 * 1024),
        cost_estimate=cost(),
        name="columns_both",
    )(core, held(stream), held(up), *gains, *[stored(array) for array in matrices])


def add_parts(refs, size):
    total, gains = None, None
    for ref in refs:
        rows = ref[0:size, :].astype(F32)
        tail = ref[size : size + 8, :].astype(F32) + ref[size + 8 : size + TAIL, :].astype(F32)
        total = rows if total is None else total + rows
        gains = tail if gains is None else gains + tail
    return total.astype(BF16), gains


def sum_split_kernel(count, size, ways, sends, at_ref, *refs):
    ins, rider, outs = refs[:count], refs[count + 1 : -1 - sends], refs[-1 - sends : -1]
    parts = refs[-1]
    total, gains = add_parts(ins, size)
    step = size // ways
    for j in range(ways):
        parts[j] = total[j * step : (j + 1) * step, :]
    for j, out in enumerate(outs):
        out[0:step, :] = parts[(at_ref[0] & (ways - 1)) ^ j]
        store_tail(out, step, gains)
        if rider and j:
            out[step + TAIL :, :] = rider[0][...]


def sum_split(at, arrays, size, ways, sends, after, rider=None):
    width = arrays[0].shape[1]
    step = size // ways
    extra = 0 if rider is None else rider.shape[0]
    shapes = [(step + TAIL + (extra if j else 0), width) for j in range(sends)]
    riders = [] if rider is None else [held(rider)]
    return pl.pallas_call(
        functools.partial(sum_split_kernel, len(arrays), size, ways, sends),
        in_specs=[SCALAR] + [HELD] * len(arrays) + [UNREAD] + [HELD] * len(riders),
        out_specs=[HELD] * sends,
        out_shape=[held_shape(shape, BF16) for shape in shapes],
        scratch_shapes=[pltpu.VMEM((ways, step, width), BF16)],
        compiler_params=params(SMALL_LIMIT),
        cost_estimate=small_cost(arrays),
        name="sum_split",
    )(at, *[held(array) for array in arrays], after, *riders)


def sum_last_kernel(count, size, *refs):
    ins, (part, tail) = refs[:count], refs[count + 1 :]
    total, gains = add_parts(ins, size)
    part[...] = total
    store_tail(tail, 0, gains)


def sum_last(arrays, size, after):
    width = arrays[0].shape[1]
    return pl.pallas_call(
        functools.partial(sum_last_kernel, len(arrays), size),
        in_specs=[HELD] * len(arrays) + [UNREAD],
        out_specs=[HELD] * 2,
        out_shape=[held_shape((size, width), BF16), held_shape((TAIL, width), BF16)],
        compiler_params=params(SMALL_LIMIT),
        cost_estimate=small_cost(arrays),
        name="sum_last",
    )(*[held(array) for array in arrays], after)


def join_kernel(ways, first, at_ref, *refs):
    ins, out = refs[:ways], refs[-1]
    size = out.shape[1]
    for j in range(ways):
        start = first if j else 0
        out[at_ref[0] ^ j] = ins[j][start : start + size, :]


def join(at, arrays, first, after):
    ways, (size, width) = len(arrays), arrays[0].shape
    joined = pl.pallas_call(
        functools.partial(join_kernel, ways, first),
        in_specs=[SCALAR] + [HELD] * ways + [UNREAD],
        out_specs=HELD,
        out_shape=held_shape((ways, size, width), BF16),
        compiler_params=params(SMALL_LIMIT),
        cost_estimate=small_cost(arrays),
        name="join",
    )(at, *[held(array) for array in arrays], after)
    return joined.reshape(ways * size, width)


def finish_kernel(buffers, at_ref, own_ref, other_ref, tail_ref, _, *refs):
    *outs, token_ref, halves = refs
    token_ref[...] = jnp.zeros_like(token_ref)
    width = own_ref.shape[1]
    halves[at_ref[0]] = own_ref[...]
    halves[at_ref[0] ^ 1] = other_ref[...]
    gains = tail_ref[0:8, :].astype(F32) + tail_ref[8:16, :].astype(F32)
    first = 0
    for rows, kinds in buffers:
        at = 0
        for kind in kinds:
            out = outs.pop(0)
            if isinstance(kind, int):
                out[...] = gains[kind : kind + 1, :]
                continue
            for j in range(out.size // (width * width)):
                half, row = divmod(at * width, rows // 2)
                block = halves[half, first + row : first + row + width, :].astype(F32)
                if kind == "rows":
                    out[j * width : (j + 1) * width, :] = block.T
                else:
                    out[:, j * width : (j + 1) * width] = block
                at += 1
        first += rows // 2


def finish(at, own, other, tail, buffers, hidden_width, after):
    half, width = own.shape
    shapes = {"square": (width, width), "columns": (width, hidden_width), "rows": (hidden_width, width)}
    kinds = [kind for _, each in buffers for kind in each]
    outs = [shapes.get(kind, (1, width)) for kind in kinds]
    *outs, token = pl.pallas_call(
        functools.partial(finish_kernel, buffers),
        grid=(1,),
        in_specs=[SCALAR, HELD, HELD, HELD, UNREAD],
        out_specs=[whole_out(shape) for shape in outs] + [HELD],
        out_shape=[shape_of(shape, F32) for shape in outs] + [held_shape((8, 128), F32)],
        scratch_shapes=[pltpu.VMEM((2, half, width), BF16)],
        compiler_params=params(24 * 1024 * 1024),
        cost_estimate=cost(),
        name="finish",
    )(at, held(own), held(other), held(tail), after)
    return [out.reshape(width) if isinstance(kind, int) else out for kind, out in zip(kinds, outs)], token


def small_cost(arrays):
    return pl.CostEstimate(flops=1, bytes_accessed=1, transcendentals=0)


class Exchange:
    def __init__(self, bits, scatter, flat, devices):
        self.bits, self.scatter = bits, scatter
        self.ways = 1 << len(bits)
        place = sum(((flat >> bit) & 1) << i for i, bit in enumerate(bits))
        self.place = jnp.reshape(place, (1,)).astype(jnp.int32)
        self.devices = devices

    def swap(self, array, member):
        mask = sum(1 << bit for i, bit in enumerate(self.bits) if (member >> i) & 1)
        return lax.ppermute(array, ALL, [(i, i ^ mask) for i in range(self.devices)])


class Chain:
    def __init__(self, exchanges, buffers, keep, send, hidden_width):
        self.pair, self.four, *self.others = exchanges
        self.rows = sum(rows for rows, _ in buffers) // 2
        self.arrays = [keep, self.pair.swap(send, 1)]
        self.token = keep
        self.buffers, self.hidden_width = buffers, hidden_width

    def cut(self, after, rider=None):
        ways = self.four.ways
        parts = sum_split(self.four.place, self.arrays, self.rows, ways, ways, after, rider)
        self.arrays = [parts[0]] + [self.four.swap(parts[j], j) for j in range(1, ways)]
        self.rows //= ways
        return parts[0]

    def add(self, after):
        exchange = self.others.pop(0)
        (part,) = sum_split(self.pair.place, self.arrays, self.rows, 1, 1, after)
        self.arrays = [part, exchange.swap(part, 1)]
        return part

    def last(self, after):
        self.part, self.tail = sum_last(self.arrays, self.rows, after)
        return self.part

    def spread(self):
        self.pieces = [self.part] + [self.four.swap(self.part, j) for j in range(1, self.four.ways)]
        self.first = 0

    def ride(self, chain):
        self.pieces = [self.part] + chain.arrays[1:]
        self.first = chain.rows + TAIL

    def join(self, after):
        self.own = join(self.four.place, self.pieces, self.first, after)
        self.other = self.pair.swap(self.own, 1)
        return self.own

    def finish(self, after):
        self.results, token = finish(
            self.pair.place, self.own, self.other, self.tail, self.buffers, self.hidden_width, after
        )
        return token


def on_device(inputs, cotangent, *weights):
    rows, images, cols, width = inputs.shape
    height = lax.axis_size("row")
    devices = height * lax.axis_size("img")
    flat = lax.axis_index("img") * height + lax.axis_index("row")
    top = devices.bit_length() - 2
    exchanges = [Exchange([0], True, flat, devices), Exchange([top, 1], True, flat, devices)]
    exchanges += [Exchange([bit], False, flat, devices) for bit in range(2, top)]
    core = exchanges[0].place
    rows_gains = [weights[i].reshape(1, width) for i in (0, 5)]
    column_gains = [weights[i].reshape(1, width) for i in (8, 13)]
    matrices = [w for w in weights if w.ndim == 2]
    hidden_width = matrices[4].shape[1]
    owned = images * cols // height

    def trade(array):
        return lax.all_to_all(array, "row", 0, 0, tiled=True)

    squares = ("square",) * 4
    total = grad_rows(width, hidden_width)
    sent_shape = (height, rows, owned, width)
    up = cotangent.reshape(rows, height, owned, width).transpose(1, 0, 2, 3)
    up = trade(up)
    sent, query, key, value, attended, middle, probs, hidden, slope = rows_forward(
        inputs, rows_gains, matrices[:6], sent_shape
    )
    sent, up = lax.optimization_barrier((sent, up))
    stream = trade(sent)
    final, between_grad, keep, send = columns_both(core, stream, up, column_gains, matrices[6:])
    kinds = (0, *squares, 1, "columns", "rows")
    columns = Chain(exchanges, ((total, kinds),), keep, send, hidden_width)
    token = columns.add(columns.cut(columns.token))
    between_grad = trade(between_grad)
    between_grad, final, token = lax.optimization_barrier((between_grad, final, token))
    final = trade(final)
    wq, wk, wv, wo, w1, w2 = matrices[:6]
    kept = (slope, hidden, w2, middle, w1, attended, wo, query, key, value, probs, inputs, wq, wk, wv)
    *grads, keep, send = rows_backward(core, between_grad, rows_gains, kept, token)
    rows_chain = Chain(exchanges, ((total, kinds),), keep, send, hidden_width)
    token = rows_chain.cut(rows_chain.token)
    stream_grad, token = rows_rest(grads, inputs, rows_gains[0], (wq, wk, wv), token)
    while columns.others:
        token = columns.add(token)
    final, token = unpack(final, inputs.shape, token)
    token = rows_chain.add(token)
    token = columns.last(token)
    columns.spread()
    while rows_chain.others:
        token = rows_chain.add(token)
    token = rows_chain.last(token)
    token = columns.join(token)
    rows_chain.spread()
    token = columns.finish(token)
    token = rows_chain.join(token)
    rows_chain.finish(token)
    c_gain, c_query, c_keys, c_values, c_mixer, c_scale, c_expand, c_shrink = columns.results
    r_gain, r_query, r_keys, r_values, r_mixer, r_scale, r_expand, r_shrink = rows_chain.results
    return (
        final, stream_grad,
        r_gain, r_query, r_keys, r_values, r_mixer, r_scale, r_expand, r_shrink,
        c_gain, c_query, c_keys, c_values, c_mixer, c_scale, c_expand, c_shrink,
    )


def solution(mesh):
    moved = P("row", "img", None, None)
    return jax.shard_map(
        on_device,
        mesh=mesh,
        in_specs=(moved, moved) + (P(),) * 16,
        out_specs=(moved, moved) + (P(),) * 16,
        check_vma=False,
    )
```

```python
import functools
import math

import jax
import jax.numpy as jnp
from jax import lax
from jax.experimental import pallas as pl
from jax.experimental.pallas import tpu as pltpu
from jax.sharding import PartitionSpec as P

HEADS = 2
EPS = 1e-05
GROUP = 8
TAIL = 16
HIDDEN_TILE = 256
VMEM_LIMIT = 24 * 1024 * 1024
SMALL_LIMIT = 12 * 1024 * 1024
ALL = ("img", "row")
F32 = jnp.float32
BF16 = jnp.bfloat16


def mm(left, right):
    return lax.dot_general(left, right, (((1,), (0,)), ((), ())), preferred_element_type=F32)


def mm_right_t(left, right):
    return lax.dot_general(left, right, (((1,), (1,)), ((), ())), preferred_element_type=F32)


def mm_left_t(left, right):
    return lax.dot_general(left, right, (((0,), (0,)), ((), ())), preferred_element_type=F32)


def normalize(stream):
    centred = stream - jnp.mean(stream, axis=-1, keepdims=True)
    inverse = lax.rsqrt(jnp.mean(centred * centred, axis=-1, keepdims=True) + EPS)
    return centred * inverse, inverse


def normalize_back(upstream, normal, inverse, gain):
    scaled = upstream * gain
    centred = (
        scaled
        - jnp.mean(scaled, axis=-1, keepdims=True)
        - normal * jnp.mean(scaled * normal, axis=-1, keepdims=True)
    )
    return inverse * centred, jnp.sum(upstream * normal, axis=0, keepdims=True)


ROOT = math.sqrt(2.0 / math.pi)
CUBE = 0.044715


def gelu_both(value):
    square = value * value
    bent = jnp.tanh(ROOT * (value + CUBE * (square * value)))
    half = 0.5 * (1.0 + bent)
    slope = half + (0.5 * ROOT) * value * (1.0 - bent * bent) * (1.0 + (3.0 * CUBE) * square)
    return value * half, slope


def softmax(scores):
    risen = jnp.exp(scores - jnp.max(scores, axis=-1, keepdims=True))
    return risen * (1.0 / jnp.sum(risen, axis=-1, keepdims=True))


def causal_bias(size, period):
    row = lax.broadcasted_iota(jnp.int32, (size, size), 0)
    col = lax.broadcasted_iota(jnp.int32, (size, size), 1)
    visible = (row >= col) & (((row ^ col) & (period - 1)) == 0)
    return jnp.where(visible, 0.0, -1e30).astype(F32)


def head_places(groups, tokens, features):
    return [
        (slice(i * tokens, (i + 1) * tokens), slice(m * features, (m + 1) * features))
        for i in range(groups)
        for m in range(HEADS)
    ]


def merge_heads(parts):
    pairs = [parts[i : i + HEADS] for i in range(0, len(parts), HEADS)]
    return jnp.concatenate([jnp.concatenate(pair, axis=1) for pair in pairs], axis=0)


def attend_back(up, query, key, value, probs, places, scaling):
    prob_grads = [mm_right_t(up[at], value[at]) for at in places]
    score_grads = []
    for prob, prob_grad in zip(probs, prob_grads):
        inner = jnp.sum(prob * prob_grad, axis=-1, keepdims=True)
        score_grads.append((prob * (prob_grad - inner)).astype(BF16))
    value_grads = [mm_left_t(prob.astype(BF16), up[at]).astype(BF16) for prob, at in zip(probs, places)]
    query_grads = [(mm(grad, key[at]) * scaling).astype(BF16) for grad, at in zip(score_grads, places)]
    key_grads = [(mm_left_t(grad, query[at]) * scaling).astype(BF16) for grad, at in zip(score_grads, places)]
    return tuple(merge_heads(grads) for grads in (query_grads, key_grads, value_grads))


def feed_back(normed, up_low, expand_ref, shrink_ref, put, first, result_ref, grad_ref):
    hidden_width = expand_ref.shape[1]
    tile = min(HIDDEN_TILE, hidden_width)
    tiles = hidden_width // tile

    @pl.loop(0, tiles)
    def _(j):
        cut = pl.ds(pl.multiple_of(j * tile, tile), tile)
        expand = expand_ref[:, cut]
        shrink = shrink_ref[cut, :]
        hidden, slope = gelu_both(mm(normed, expand))
        hidden = hidden.astype(BF16)
        result_ref[...] += mm(hidden, shrink)
        expanded_grad = (slope * mm_right_t(up_low, shrink)).astype(BF16)
        put(first + j, mm_left_t(normed, expanded_grad))
        put(first + tiles + j, mm_left_t(up_low, hidden))
        grad_ref[...] += mm_right_t(expanded_grad, expand)


def project_back(normed_low, grads, weight_refs, put):
    total = None
    for i, (grad, weight_ref) in enumerate(zip(grads, weight_refs)):
        put(i, mm_left_t(normed_low, grad))
        part = mm_right_t(grad, weight_ref[...])
        total = part if total is None else total + part
    return total


def store_tail(ref, at, gains):
    high = gains.astype(BF16)
    ref[at : at + 8, :] = high
    ref[at + 8 : at + 16, :] = (gains - high.astype(F32)).astype(BF16)


def putter(core, halves):
    width = halves.shape[2]
    blocks = halves.shape[1] // width

    def put(block, value):
        start = pl.multiple_of(lax.rem(block, blocks) * width, width)
        halves[lax.div(block, blocks) ^ core, pl.ds(start, width), :] = value.astype(BF16)

    return put


def emit_grads(halves, gains, keep_ref, send_ref):
    for i, ref in enumerate((keep_ref, send_ref)):
        ref[0 : halves.shape[1], :] = halves[i]
        store_tail(ref, halves.shape[1], gains)


def stack_gains(gain, scale):
    return jnp.concatenate([gain, scale, jnp.zeros((6, gain.shape[1]), F32)], axis=0)


def rows_forward_kernel(
    x_ref, ga_ref, wq_ref, wk_ref, wv_ref, wo_ref, gb_ref, w1_ref, w2_ref,
    send_ref, q_ref, k_ref, v_ref, att_ref, mid_ref, p_ref, hidden_ref, slope_ref, result_ref,
):
    rows, images, cols, width = x_ref.shape
    tokens = rows * images * cols
    features = width // HEADS
    scaling = 1.0 / math.sqrt(features)
    stream = x_ref[...].astype(F32).reshape(tokens, width)
    normed = (normalize(stream)[0] * ga_ref[...]).astype(BF16)
    query = mm(normed, wq_ref[...]).astype(BF16)
    key = mm(normed, wk_ref[...]).astype(BF16)
    value = mm(normed, wv_ref[...]).astype(BF16)
    q_ref[...] = query.reshape(q_ref.shape)
    k_ref[...] = key.reshape(q_ref.shape)
    v_ref[...] = value.reshape(q_ref.shape)
    bias = causal_bias(cols, 1)
    places = head_places(rows * images, cols, features)
    probs = [softmax(mm_right_t(query[at], key[at]) * scaling + bias) for at in places]
    heads = [mm(prob.astype(BF16), value[at]) for prob, at in zip(probs, places)]
    for i, prob in enumerate(probs):
        group, m = divmod(i, HEADS)
        p_ref[group // images, group % images, m] = prob
    attended = merge_heads(heads).astype(BF16)
    att_ref[...] = attended.reshape(att_ref.shape)
    middle = stream + mm(attended, wo_ref[...])
    mid_ref[...] = middle.reshape(mid_ref.shape)
    normed_b = (normalize(middle)[0] * gb_ref[...]).astype(BF16)
    tiles, _, tile = hidden_ref.shape
    result_ref[...] = middle

    @pl.loop(0, tiles)
    def _(j):
        cut = pl.ds(pl.multiple_of(j * tile, tile), tile)
        hidden, slope = gelu_both(mm(normed_b, w1_ref[:, cut]))
        hidden = hidden.astype(BF16)
        hidden_ref[j] = hidden
        slope_ref[j] = slope
        result_ref[...] += mm(hidden, w2_ref[cut, :])

    result = result_ref[...]
    result = result.astype(BF16).reshape(rows, images, cols, width)
    part = send_ref.shape[2]
    for i in range(send_ref.shape[0]):
        image, first = divmod(i * part, cols)
        send_ref[i] = result[:, image, first : first + part]


def rows_backward_kernel(
    core_ref, up_ref, slope_hbm, hidden_hbm, w2_hbm, mid_hbm, w1_hbm, ga_hbm, gb_hbm, att_hbm, wo_hbm,
    q_hbm, k_hbm, v_hbm, p_hbm, x_hbm, wq_hbm, wk_hbm, wv_hbm, _,
    mid_grad_ref, dq_ref, dk_ref, dv_ref, keep_ref, send_ref,
    halves, feed_grad_ref, slope_ref, hidden_ref, w2_ref, mid_ref, w1_ref, ga_ref, gb_ref, att_ref, wo_ref,
    q_ref, k_ref, v_ref, p_ref, x_ref, wq_ref, wk_ref, wv_ref, done, tile_done,
):
    rows, images, cols, width = x_ref.shape
    tokens = rows * images * cols
    features = width // HEADS
    scaling = 1.0 / math.sqrt(features)
    sources = (
        w2_hbm, mid_hbm, w1_hbm, ga_hbm, gb_hbm, att_hbm, wo_hbm,
        q_hbm, k_hbm, v_hbm, p_hbm, x_hbm, wq_hbm, wk_hbm, wv_hbm,
    )
    targets = (
        w2_ref, mid_ref, w1_ref, ga_ref, gb_ref, att_ref, wo_ref,
        q_ref, k_ref, v_ref, p_ref, x_ref, wq_ref, wk_ref, wv_ref,
    )
    copies = [pltpu.make_async_copy(sources[i], targets[i], done.at[i]) for i in range(len(sources))]
    tiles, _, tile = slope_ref.shape

    def tile_copies(j):
        return (
            pltpu.make_async_copy(slope_hbm.at[j], slope_ref.at[j], tile_done.at[0, j]),
            pltpu.make_async_copy(hidden_hbm.at[j], hidden_ref.at[j], tile_done.at[1, j]),
        )

    for copy in copies[:5]:
        copy.start()
    for j in range(tiles):
        for copy in tile_copies(j):
            copy.start()
    for copy in copies[5:]:
        copy.start()
    put = putter(core_ref[0], halves)
    up = jnp.concatenate([up_ref[:, r].reshape(images * cols, width) for r in range(rows)], axis=0).astype(F32)
    up_low = up.astype(BF16)
    for copy in copies[:5]:
        copy.wait()
    normal_b, inverse_b = normalize(mid_ref[...].reshape(tokens, width))
    normed_b = (normal_b * gb_ref[...]).astype(BF16)
    feed_grad_ref[...] = jnp.zeros_like(feed_grad_ref)

    @pl.loop(0, tiles)
    def _(j):
        cut = pl.ds(pl.multiple_of(j * tile, tile), tile)
        hidden_grad = mm_right_t(up_low, w2_ref[cut, :])
        for copy in tile_copies(j):
            copy.wait()
        expanded_grad = (slope_ref[j] * hidden_grad).astype(BF16)
        put(4 + j, mm_left_t(normed_b, expanded_grad))
        put(4 + tiles + j, mm_left_t(up_low, hidden_ref[j]))
        feed_grad_ref[...] += mm_right_t(expanded_grad, w1_ref[:, cut])

    normed_grad = feed_grad_ref[...]
    middle_norm, scale_grad = normalize_back(normed_grad, normal_b, inverse_b, gb_ref[...])
    middle_grad = up + middle_norm
    mid_grad_ref[...] = middle_grad
    middle_low = middle_grad.astype(BF16)
    for copy in copies[5:]:
        copy.wait()
    put(3, mm_left_t(att_ref[...].reshape(tokens, width), middle_low))
    up_att = mm_right_t(middle_low, wo_ref[...]).astype(BF16)
    query = q_ref[...].reshape(tokens, width)
    key = k_ref[...].reshape(tokens, width)
    value = v_ref[...].reshape(tokens, width)
    places = head_places(rows * images, cols, features)
    probs = [p_ref[r, i, m] for r in range(rows) for i in range(images) for m in range(HEADS)]
    grads = attend_back(up_att, query, key, value, probs, places, scaling)
    normed_a = (normalize(x_ref[...].astype(F32).reshape(tokens, width))[0] * ga_ref[...]).astype(BF16)
    shared = None
    for i, (grad, target, weight_ref) in enumerate(zip(grads, (dq_ref, dk_ref, dv_ref), (wq_ref, wk_ref, wv_ref))):
        target[...] = grad
        weight_grad = mm_left_t(normed_a, grad)
        put(i, weight_grad)
        part = weight_grad * weight_ref[...].astype(F32)
        shared = part if shared is None else shared + part
    gain_grad = jnp.sum(shared.T, axis=0, keepdims=True) / ga_ref[...]
    emit_grads(halves, stack_gains(gain_grad, scale_grad), keep_ref, send_ref)


def rows_rest_kernel(mid_grad_ref, dq_ref, dk_ref, dv_ref, x_ref, ga_ref, wq_ref, wk_ref, wv_ref, _, grad_ref, token_ref):
    rows, images, cols, width = x_ref.shape
    normal, inverse = normalize(x_ref[...].astype(F32).reshape(rows * images * cols, width))
    normed_grad = None
    for grad_ref_in, weight_ref in zip((dq_ref, dk_ref, dv_ref), (wq_ref, wk_ref, wv_ref)):
        part = mm_right_t(grad_ref_in[...], weight_ref[...])
        normed_grad = part if normed_grad is None else normed_grad + part
    stream_norm, _ = normalize_back(normed_grad, normal, inverse, ga_ref[...])
    grad_ref[...] = (mid_grad_ref[...] + stream_norm).reshape(grad_ref.shape)
    token_ref[...] = jnp.zeros_like(token_ref)


def unpack_kernel(in_ref, _, out_ref, token_ref, done):
    part, cols = in_ref.shape[2], out_ref.shape[2]
    copies = []
    for i in range(in_ref.shape[0]):
        image, first = divmod(i * part, cols)
        target = out_ref.at[:, image, pl.ds(first, part)]
        copies.append(pltpu.make_async_copy(in_ref.at[i], target, done.at[i]))
    for copy in copies:
        copy.start()
    token_ref[...] = jnp.zeros_like(token_ref)
    for copy in copies:
        copy.wait()


def load_groups(ref):
    array = ref[...].astype(F32)
    width = array.shape[-1]
    parts = [array[:, :, i : i + GROUP].reshape(-1, width) for i in range(0, array.shape[2], GROUP)]
    return jnp.concatenate(parts, axis=0)


def store_groups(ref, value):
    sources, rows, cols, width = ref.shape
    groups = cols // GROUP
    tokens = sources * rows * GROUP
    parts = [value[i * tokens : (i + 1) * tokens].reshape(sources, rows, GROUP, width) for i in range(groups)]
    ref[...] = jnp.concatenate(parts, axis=2).astype(ref.dtype)


def columns_kernel(
    core_ref, x_ref, up_ref, ga_ref, gb_ref, wq_hbm, wk_hbm, wv_hbm, wo_hbm, w1_hbm, w2_hbm,
    out_ref, grad_ref, keep_ref, send_ref,
    halves, bias, result_ref, feed_grad_ref, wq_ref, wk_ref, wv_ref, wo_ref, w1_ref, w2_ref, done,
):
    sources, rows, cols, width = x_ref.shape
    groups = cols // GROUP
    tokens = sources * rows * GROUP
    features = width // HEADS
    scaling = 1.0 / math.sqrt(features)
    froms = (wq_hbm, wk_hbm, wv_hbm, wo_hbm, w1_hbm, w2_hbm)
    targets = (wq_ref, wk_ref, wv_ref, wo_ref, w1_ref, w2_ref)
    copies = [pltpu.make_async_copy(froms[i], targets[i], done.at[i]) for i in range(len(froms))]
    for copy in copies:
        copy.start()
    put = putter(core_ref[0], halves)
    bias[...] = causal_bias(tokens, GROUP)
    stream = load_groups(x_ref)
    normal_a, inverse_a = normalize(stream)
    normed_a = (normal_a * ga_ref[...]).astype(BF16)
    for copy in copies[:4]:
        copy.wait()
    query = mm(normed_a, wq_ref[...]).astype(BF16)
    key = mm(normed_a, wk_ref[...]).astype(BF16)
    value = mm(normed_a, wv_ref[...]).astype(BF16)
    places = head_places(groups, tokens, features)
    probs = [softmax(mm_right_t(query[at], key[at]) * scaling + bias[...]) for at in places]
    heads = [mm(prob.astype(BF16), value[at]) for prob, at in zip(probs, places)]
    attended = merge_heads(heads).astype(BF16)
    middle = stream + mm(attended, wo_ref[...])
    normal_b, inverse_b = normalize(middle)
    normed_b = (normal_b * gb_ref[...]).astype(BF16)
    up = load_groups(up_ref)
    up_low = up.astype(BF16)
    for copy in copies[4:]:
        copy.wait()
    result_ref[...] = middle
    feed_grad_ref[...] = jnp.zeros_like(feed_grad_ref)
    feed_back(normed_b, up_low, w1_ref, w2_ref, put, 4, result_ref, feed_grad_ref)
    store_groups(out_ref, result_ref[...])
    normed_grad = feed_grad_ref[...]
    middle_norm, scale_grad = normalize_back(normed_grad, normal_b, inverse_b, gb_ref[...])
    middle_grad = up + middle_norm
    middle_low = middle_grad.astype(BF16)
    put(3, mm_left_t(attended, middle_low))
    up_att = mm_right_t(middle_low, wo_ref[...]).astype(BF16)
    grads = attend_back(up_att, query, key, value, probs, places, scaling)
    normed_grad = project_back(normed_a, grads, (wq_ref, wk_ref, wv_ref), put)
    stream_norm, gain_grad = normalize_back(normed_grad, normal_a, inverse_a, ga_ref[...])
    store_groups(grad_ref, middle_grad + stream_norm)
    emit_grads(halves, stack_gains(gain_grad, scale_grad), keep_ref, send_ref)


def whole(array):
    zeros = (0,) * array.ndim
    return pl.BlockSpec(array.shape, lambda i: zeros)


def whole_out(shape):
    zeros = (0,) * len(shape)
    return pl.BlockSpec(shape, lambda i: zeros)


SCALAR = pl.BlockSpec(memory_space=pltpu.SMEM)
HELD = pl.BlockSpec(memory_space=pltpu.VMEM)
UNREAD = pl.BlockSpec(memory_space=pl.ANY)


def held(array):
    return pltpu.with_memory_space_constraint(array, pltpu.VMEM)


def params(limit=VMEM_LIMIT):
    return pltpu.CompilerParams(vmem_limit_bytes=limit)


def shape_of(shape, dtype):
    return jax.ShapeDtypeStruct(shape, dtype)


def held_shape(shape, dtype):
    return pltpu.VMEM(shape, dtype)


def stored_shape(shape, dtype):
    return pltpu.HBM(shape, dtype)


def stored(array):
    return pltpu.with_memory_space_constraint(array, pltpu.HBM)


def grad_rows(width, hidden_width):
    tile = min(HIDDEN_TILE, hidden_width)
    return 4 * width + 2 * (hidden_width // tile) * width


def cost(*_):
    return pl.CostEstimate(flops=1, bytes_accessed=1, transcendentals=0)


def rows_forward(inputs, gains, matrices, sent_shape):
    rows, images, cols, width = inputs.shape
    low = stored_shape(inputs.shape, BF16)
    wq, wk, wv, wo, w1, w2 = matrices
    tile = min(HIDDEN_TILE, w1.shape[1])
    feed = (w1.shape[1] // tile, rows * images * cols, tile)
    operands = [stored(array) for array in (inputs, gains[0], wq, wk, wv, wo, gains[1], w1, w2)]
    outs = [
        held_shape(sent_shape, BF16),
        low, low, low, low,
        stored_shape(inputs.shape, F32),
        stored_shape((rows, images, HEADS, cols, cols), F32),
        stored_shape(feed, BF16),
        stored_shape(feed, F32),
    ]
    return pl.pallas_call(
        rows_forward_kernel,
        grid=(1,),
        in_specs=[whole(array) for array in operands],
        out_specs=[HELD] + [whole_out(out.shape) for out in outs[1:]],
        out_shape=outs,
        scratch_shapes=[pltpu.VMEM((rows * images * cols, width), F32)],
        compiler_params=params(48 * 1024 * 1024),
        cost_estimate=cost(),
        name="rows_forward",
    )(*operands)


def rows_backward(core, up, kept, after):
    tiles, tokens, _ = kept[0].shape
    hidden_width, width = kept[2].shape
    half = grad_rows(width, hidden_width) // 2
    part = held_shape((half + TAIL, width), BF16)
    grad = held_shape((tokens, width), BF16)
    return pl.pallas_call(
        rows_backward_kernel,
        in_specs=[SCALAR, HELD] + [UNREAD] * (len(kept) + 1),
        out_specs=[HELD] * 6,
        out_shape=[held_shape((tokens, width), F32), grad, grad, grad, part, part],
        scratch_shapes=[pltpu.VMEM((2, half, width), BF16), pltpu.VMEM((tokens, width), F32)]
        + [pltpu.VMEM(array.shape, array.dtype) for array in kept]
        + [pltpu.SemaphoreType.DMA((len(kept) - 2,)), pltpu.SemaphoreType.DMA((2, tiles))],
        compiler_params=params(48 * 1024 * 1024),
        cost_estimate=cost(),
        name="rows_backward",
    )(core, held(up), *[stored(array) for array in kept], after)


def rows_rest(grads, inputs, gain, matrices, after):
    operands = [stored(array) for array in (inputs, gain, *matrices)]
    return pl.pallas_call(
        rows_rest_kernel,
        grid=(1,),
        in_specs=[HELD] * 4 + [whole(array) for array in operands] + [UNREAD],
        out_specs=[whole_out(inputs.shape), HELD],
        out_shape=[stored_shape(inputs.shape, F32), held_shape((8, 128), F32)],
        compiler_params=params(24 * 1024 * 1024),
        cost_estimate=cost(),
        name="rows_rest",
    )(*[held(grad) for grad in grads], *operands, after)


def unpack(array, shape, after):
    return pl.pallas_call(
        unpack_kernel,
        in_specs=[HELD, UNREAD],
        out_specs=[UNREAD, HELD],
        out_shape=[stored_shape(shape, BF16), held_shape((8, 128), F32)],
        scratch_shapes=[pltpu.SemaphoreType.DMA((array.shape[0],))],
        compiler_params=params(SMALL_LIMIT),
        cost_estimate=cost(),
        name="unpack",
    )(held(array), after)


def columns_both(core, stream, up, gains, matrices):
    sources, rows, cols, width = stream.shape
    half = grad_rows(width, matrices[4].shape[1]) // 2
    tokens = sources * rows * GROUP
    part = (half + TAIL, width)
    return pl.pallas_call(
        columns_kernel,
        in_specs=[SCALAR] + [HELD] * 4 + [UNREAD] * len(matrices),
        out_specs=[HELD] * 4,
        out_shape=[held_shape(stream.shape, BF16)] * 2 + [held_shape(part, BF16)] * 2,
        scratch_shapes=[pltpu.VMEM((2, half, width), BF16), pltpu.VMEM((tokens, tokens), F32)]
        + [pltpu.VMEM((tokens * (cols // GROUP), width), F32)] * 2
        + [pltpu.VMEM(array.shape, array.dtype) for array in matrices]
        + [pltpu.SemaphoreType.DMA((len(matrices),))],
        compiler_params=params(40 * 1024 * 1024),
        cost_estimate=cost(),
        name="columns_both",
    )(core, held(stream), held(up), *gains, *[stored(array) for array in matrices])


def add_parts(refs, size):
    total, gains = None, None
    for ref in refs:
        rows = ref[0:size, :].astype(F32)
        tail = ref[size : size + 8, :].astype(F32) + ref[size + 8 : size + TAIL, :].astype(F32)
        total = rows if total is None else total + rows
        gains = tail if gains is None else gains + tail
    return total.astype(BF16), gains


def sum_split_kernel(count, size, ways, sends, at_ref, *refs):
    ins, rider, outs = refs[:count], refs[count + 1 : -1 - sends], refs[-1 - sends : -1]
    parts = refs[-1]
    total, gains = add_parts(ins, size)
    step = size // ways
    for j in range(ways):
        parts[j] = total[j * step : (j + 1) * step, :]
    for j, out in enumerate(outs):
        out[0:step, :] = parts[(at_ref[0] & (ways - 1)) ^ j]
        store_tail(out, step, gains)
        if rider and j:
            out[step + TAIL :, :] = rider[0][...]


def sum_split(at, arrays, size, ways, sends, after, rider=None):
    width = arrays[0].shape[1]
    step = size // ways
    extra = 0 if rider is None else rider.shape[0]
    shapes = [(step + TAIL + (extra if j else 0), width) for j in range(sends)]
    riders = [] if rider is None else [held(rider)]
    return pl.pallas_call(
        functools.partial(sum_split_kernel, len(arrays), size, ways, sends),
        in_specs=[SCALAR] + [HELD] * len(arrays) + [UNREAD] + [HELD] * len(riders),
        out_specs=[HELD] * sends,
        out_shape=[held_shape(shape, BF16) for shape in shapes],
        scratch_shapes=[pltpu.VMEM((ways, step, width), BF16)],
        compiler_params=params(SMALL_LIMIT),
        cost_estimate=small_cost(arrays),
        name="sum_split",
    )(at, *[held(array) for array in arrays], after, *riders)


def sum_last_kernel(count, size, *refs):
    ins, (part, tail) = refs[:count], refs[count + 1 :]
    total, gains = add_parts(ins, size)
    part[...] = total
    store_tail(tail, 0, gains)


def sum_last(arrays, size, after):
    width = arrays[0].shape[1]
    return pl.pallas_call(
        functools.partial(sum_last_kernel, len(arrays), size),
        in_specs=[HELD] * len(arrays) + [UNREAD],
        out_specs=[HELD] * 2,
        out_shape=[held_shape((size, width), BF16), held_shape((TAIL, width), BF16)],
        compiler_params=params(SMALL_LIMIT),
        cost_estimate=small_cost(arrays),
        name="sum_last",
    )(*[held(array) for array in arrays], after)


def join_kernel(ways, first, at_ref, *refs):
    ins, out = refs[:ways], refs[-1]
    size = out.shape[1]
    for j in range(ways):
        start = first if j else 0
        out[at_ref[0] ^ j] = ins[j][start : start + size, :]


def join(at, arrays, first, after):
    ways, (size, width) = len(arrays), arrays[0].shape
    joined = pl.pallas_call(
        functools.partial(join_kernel, ways, first),
        in_specs=[SCALAR] + [HELD] * ways + [UNREAD],
        out_specs=HELD,
        out_shape=held_shape((ways, size, width), BF16),
        compiler_params=params(SMALL_LIMIT),
        cost_estimate=small_cost(arrays),
        name="join",
    )(at, *[held(array) for array in arrays], after)
    return joined.reshape(ways * size, width)


def finish_kernel(buffers, at_ref, own_ref, other_ref, tail_ref, _, *refs):
    *outs, token_ref, halves = refs
    token_ref[...] = jnp.zeros_like(token_ref)
    width = own_ref.shape[1]
    halves[at_ref[0]] = own_ref[...]
    halves[at_ref[0] ^ 1] = other_ref[...]
    gains = tail_ref[0:8, :].astype(F32) + tail_ref[8:16, :].astype(F32)
    first = 0
    for rows, kinds in buffers:
        at = 0
        for kind in kinds:
            out = outs.pop(0)
            if isinstance(kind, int):
                out[...] = gains[kind : kind + 1, :]
                continue
            for j in range(out.size // (width * width)):
                half, row = divmod(at * width, rows // 2)
                block = halves[half, first + row : first + row + width, :].astype(F32)
                if kind == "rows":
                    out[j * width : (j + 1) * width, :] = block.T
                else:
                    out[:, j * width : (j + 1) * width] = block
                at += 1
        first += rows // 2


def finish(at, own, other, tail, buffers, hidden_width, after):
    half, width = own.shape
    shapes = {"square": (width, width), "columns": (width, hidden_width), "rows": (hidden_width, width)}
    kinds = [kind for _, each in buffers for kind in each]
    outs = [shapes.get(kind, (1, width)) for kind in kinds]
    *outs, token = pl.pallas_call(
        functools.partial(finish_kernel, buffers),
        grid=(1,),
        in_specs=[SCALAR, HELD, HELD, HELD, UNREAD],
        out_specs=[whole_out(shape) for shape in outs] + [HELD],
        out_shape=[shape_of(shape, F32) for shape in outs] + [held_shape((8, 128), F32)],
        scratch_shapes=[pltpu.VMEM((2, half, width), BF16)],
        compiler_params=params(24 * 1024 * 1024),
        cost_estimate=cost(),
        name="finish",
    )(at, held(own), held(other), held(tail), after)
    return [out.reshape(width) if isinstance(kind, int) else out for kind, out in zip(kinds, outs)], token


def small_cost(arrays):
    return pl.CostEstimate(flops=1, bytes_accessed=1, transcendentals=0)


class Exchange:
    def __init__(self, bits, scatter, flat, devices):
        self.bits, self.scatter = bits, scatter
        self.ways = 1 << len(bits)
        place = sum(((flat >> bit) & 1) << i for i, bit in enumerate(bits))
        self.place = jnp.reshape(place, (1,)).astype(jnp.int32)
        self.devices = devices

    def swap(self, array, member):
        mask = sum(1 << bit for i, bit in enumerate(self.bits) if (member >> i) & 1)
        return lax.ppermute(array, ALL, [(i, i ^ mask) for i in range(self.devices)])


class Chain:
    def __init__(self, exchanges, buffers, keep, send, hidden_width):
        self.pair, self.four, *self.others = exchanges
        self.rows = sum(rows for rows, _ in buffers) // 2
        self.arrays = [keep, self.pair.swap(send, 1)]
        self.token = keep
        self.buffers, self.hidden_width = buffers, hidden_width

    def cut(self, after, rider=None):
        ways = self.four.ways
        parts = sum_split(self.four.place, self.arrays, self.rows, ways, ways, after, rider)
        self.arrays = [parts[0]] + [self.four.swap(parts[j], j) for j in range(1, ways)]
        self.rows //= ways
        return parts[0]

    def add(self, after):
        exchange = self.others.pop(0)
        (part,) = sum_split(self.pair.place, self.arrays, self.rows, 1, 1, after)
        self.arrays = [part, exchange.swap(part, 1)]
        return part

    def last(self, after):
        self.part, self.tail = sum_last(self.arrays, self.rows, after)
        return self.part

    def spread(self):
        self.pieces = [self.part] + [self.four.swap(self.part, j) for j in range(1, self.four.ways)]
        self.first = 0

    def ride(self, chain):
        self.pieces = [self.part] + chain.arrays[1:]
        self.first = chain.rows + TAIL

    def join(self, after):
        self.own = join(self.four.place, self.pieces, self.first, after)
        self.other = self.pair.swap(self.own, 1)
        return self.own

    def finish(self, after):
        self.results, token = finish(
            self.pair.place, self.own, self.other, self.tail, self.buffers, self.hidden_width, after
        )
        return token


def on_device(inputs, cotangent, *weights):
    rows, images, cols, width = inputs.shape
    height = lax.axis_size("row")
    devices = height * lax.axis_size("img")
    flat = lax.axis_index("img") * height + lax.axis_index("row")
    top = devices.bit_length() - 2
    exchanges = [Exchange([0], True, flat, devices), Exchange([top, 1], True, flat, devices)]
    exchanges += [Exchange([bit], False, flat, devices) for bit in range(2, top)]
    core = exchanges[0].place
    rows_gains = [weights[i].reshape(1, width) for i in (0, 5)]
    column_gains = [weights[i].reshape(1, width) for i in (8, 13)]
    matrices = [w for w in weights if w.ndim == 2]
    hidden_width = matrices[4].shape[1]
    owned = images * cols // height

    def trade(array):
        return lax.all_to_all(array, "row", 0, 0, tiled=True)

    squares = ("square",) * 4
    total = grad_rows(width, hidden_width)
    sent_shape = (height, rows, owned, width)
    up = cotangent.reshape(rows, height, owned, width).transpose(1, 0, 2, 3)
    up = trade(up)
    sent, query, key, value, attended, middle, probs, hidden, slope = rows_forward(
        inputs, rows_gains, matrices[:6], sent_shape
    )
    sent, up = lax.optimization_barrier((sent, up))
    stream = trade(sent)
    final, between_grad, keep, send = columns_both(core, stream, up, column_gains, matrices[6:])
    kinds = (0, *squares, 1, "columns", "rows")
    columns = Chain(exchanges, ((total, kinds),), keep, send, hidden_width)
    token = columns.add(columns.cut(columns.token))
    between_grad = trade(between_grad)
    between_grad, final, token = lax.optimization_barrier((between_grad, final, token))
    final = trade(final)
    wq, wk, wv, wo, w1, w2 = matrices[:6]
    kept = (slope, hidden, w2, middle, w1, *rows_gains, attended, wo, query, key, value, probs, inputs, wq, wk, wv)
    *grads, keep, send = rows_backward(core, between_grad, kept, token)
    rows_chain = Chain(exchanges, ((total, kinds),), keep, send, hidden_width)
    token = rows_chain.cut(rows_chain.token)
    stream_grad, token = rows_rest(grads, inputs, rows_gains[0], (wq, wk, wv), token)
    while columns.others:
        token = columns.add(token)
    final, token = unpack(final, inputs.shape, token)
    token = rows_chain.add(token)
    token = columns.last(token)
    columns.spread()
    while rows_chain.others:
        token = rows_chain.add(token)
    token = rows_chain.last(token)
    token = columns.join(token)
    rows_chain.spread()
    token = columns.finish(token)
    token = rows_chain.join(token)
    rows_chain.finish(token)
    c_gain, c_query, c_keys, c_values, c_mixer, c_scale, c_expand, c_shrink = columns.results
    r_gain, r_query, r_keys, r_values, r_mixer, r_scale, r_expand, r_shrink = rows_chain.results
    return (
        final, stream_grad,
        r_gain, r_query, r_keys, r_values, r_mixer, r_scale, r_expand, r_shrink,
        c_gain, c_query, c_keys, c_values, c_mixer, c_scale, c_expand, c_shrink,
    )


def solution(mesh):
    moved = P("row", "img", None, None)
    return jax.shard_map(
        on_device,
        mesh=mesh,
        in_specs=(moved, moved) + (P(),) * 16,
        out_specs=(moved, moved) + (P(),) * 16,
        check_vma=False,
    )
```

```python
import functools
import math

import jax
import jax.numpy as jnp
from jax import lax
from jax.experimental import pallas as pl
from jax.experimental.pallas import tpu as pltpu
from jax.sharding import PartitionSpec as P

HEADS = 2
EPS = 1e-05
GROUP = 8
TAIL = 16
HIDDEN_TILE = 256
VMEM_LIMIT = 24 * 1024 * 1024
SMALL_LIMIT = 12 * 1024 * 1024
ALL = ("img", "row")
F32 = jnp.float32
BF16 = jnp.bfloat16


def mm(left, right):
    return lax.dot_general(left, right, (((1,), (0,)), ((), ())), preferred_element_type=F32)


def mm_right_t(left, right):
    return lax.dot_general(left, right, (((1,), (1,)), ((), ())), preferred_element_type=F32)


def mm_left_t(left, right):
    return lax.dot_general(left, right, (((0,), (0,)), ((), ())), preferred_element_type=F32)


def normalize(stream):
    centred = stream - jnp.mean(stream, axis=-1, keepdims=True)
    inverse = lax.rsqrt(jnp.mean(centred * centred, axis=-1, keepdims=True) + EPS)
    return centred * inverse, inverse


def normalize_back(upstream, normal, inverse, gain):
    scaled = upstream * gain
    centred = (
        scaled
        - jnp.mean(scaled, axis=-1, keepdims=True)
        - normal * jnp.mean(scaled * normal, axis=-1, keepdims=True)
    )
    return inverse * centred, jnp.sum(upstream * normal, axis=0, keepdims=True)


ROOT = math.sqrt(2.0 / math.pi)
CUBE = 0.044715


def gelu_both(value):
    square = value * value
    bent = jnp.tanh(ROOT * (value + CUBE * (square * value)))
    half = 0.5 * (1.0 + bent)
    slope = half + (0.5 * ROOT) * value * (1.0 - bent * bent) * (1.0 + (3.0 * CUBE) * square)
    return value * half, slope


def softmax(scores):
    risen = jnp.exp(scores - jnp.max(scores, axis=-1, keepdims=True))
    return risen * (1.0 / jnp.sum(risen, axis=-1, keepdims=True))


def causal_bias(size, period):
    row = lax.broadcasted_iota(jnp.int32, (size, size), 0)
    col = lax.broadcasted_iota(jnp.int32, (size, size), 1)
    visible = (row >= col) & (((row ^ col) & (period - 1)) == 0)
    return jnp.where(visible, 0.0, -1e30).astype(F32)


def head_places(groups, tokens, features):
    return [
        (slice(i * tokens, (i + 1) * tokens), slice(m * features, (m + 1) * features))
        for i in range(groups)
        for m in range(HEADS)
    ]


def merge_heads(parts):
    pairs = [parts[i : i + HEADS] for i in range(0, len(parts), HEADS)]
    return jnp.concatenate([jnp.concatenate(pair, axis=1) for pair in pairs], axis=0)


def attend_back(up, query, key, value, probs, places, scaling):
    prob_grads = [mm_right_t(up[at], value[at]) for at in places]
    score_grads = []
    for prob, prob_grad in zip(probs, prob_grads):
        inner = jnp.sum(prob * prob_grad, axis=-1, keepdims=True)
        score_grads.append((prob * (prob_grad - inner)).astype(BF16))
    value_grads = [mm_left_t(prob.astype(BF16), up[at]).astype(BF16) for prob, at in zip(probs, places)]
    query_grads = [(mm(grad, key[at]) * scaling).astype(BF16) for grad, at in zip(score_grads, places)]
    key_grads = [(mm_left_t(grad, query[at]) * scaling).astype(BF16) for grad, at in zip(score_grads, places)]
    return tuple(merge_heads(grads) for grads in (query_grads, key_grads, value_grads))


def feed_back(normed, up_low, expand_ref, shrink_ref, put, first, result_ref, grad_ref):
    hidden_width = expand_ref.shape[1]
    tile = min(HIDDEN_TILE, hidden_width)
    tiles = hidden_width // tile

    @pl.loop(0, tiles, unroll=2)
    def _(j):
        cut = pl.ds(pl.multiple_of(j * tile, tile), tile)
        expand = expand_ref[:, cut]
        shrink = shrink_ref[cut, :]
        hidden, slope = gelu_both(mm(normed, expand))
        hidden = hidden.astype(BF16)
        result_ref[...] += mm(hidden, shrink)
        expanded_grad = (slope * mm_right_t(up_low, shrink)).astype(BF16)
        put(first + j, mm_left_t(normed, expanded_grad))
        put(first + tiles + j, mm_left_t(up_low, hidden))
        grad_ref[...] += mm_right_t(expanded_grad, expand)


def project_back(normed_low, grads, weight_refs, put):
    total = None
    for i, (grad, weight_ref) in enumerate(zip(grads, weight_refs)):
        put(i, mm_left_t(normed_low, grad))
        part = mm_right_t(grad, weight_ref[...])
        total = part if total is None else total + part
    return total


def store_tail(ref, at, gains):
    high = gains.astype(BF16)
    ref[at : at + 8, :] = high
    ref[at + 8 : at + 16, :] = (gains - high.astype(F32)).astype(BF16)


def putter(core, halves):
    width = halves.shape[2]
    blocks = halves.shape[1] // width

    def put(block, value):
        start = pl.multiple_of(lax.rem(block, blocks) * width, width)
        halves[lax.div(block, blocks) ^ core, pl.ds(start, width), :] = value.astype(BF16)

    return put


def emit_grads(halves, gains, keep_ref, send_ref):
    for i, ref in enumerate((keep_ref, send_ref)):
        ref[0 : halves.shape[1], :] = halves[i]
        store_tail(ref, halves.shape[1], gains)


def stack_gains(gain, scale):
    return jnp.concatenate([gain, scale, jnp.zeros((6, gain.shape[1]), F32)], axis=0)


def rows_forward_kernel(
    x_ref, ga_ref, wq_ref, wk_ref, wv_ref, wo_ref, gb_ref, w1_ref, w2_ref,
    send_ref, q_ref, k_ref, v_ref, att_ref, mid_ref, p_ref, hidden_ref, slope_ref, result_ref,
):
    rows, images, cols, width = x_ref.shape
    tokens = rows * images * cols
    features = width // HEADS
    scaling = 1.0 / math.sqrt(features)
    stream = x_ref[...].astype(F32).reshape(tokens, width)
    normed = (normalize(stream)[0] * ga_ref[...]).astype(BF16)
    query = mm(normed, wq_ref[...]).astype(BF16)
    key = mm(normed, wk_ref[...]).astype(BF16)
    value = mm(normed, wv_ref[...]).astype(BF16)
    q_ref[...] = query.reshape(q_ref.shape)
    k_ref[...] = key.reshape(q_ref.shape)
    v_ref[...] = value.reshape(q_ref.shape)
    bias = causal_bias(cols, 1)
    places = head_places(rows * images, cols, features)
    probs = [softmax(mm_right_t(query[at], key[at]) * scaling + bias) for at in places]
    heads = [mm(prob.astype(BF16), value[at]) for prob, at in zip(probs, places)]
    for i, prob in enumerate(probs):
        group, m = divmod(i, HEADS)
        p_ref[group // images, group % images, m] = prob
    attended = merge_heads(heads).astype(BF16)
    att_ref[...] = attended.reshape(att_ref.shape)
    middle = stream + mm(attended, wo_ref[...])
    mid_ref[...] = middle.reshape(mid_ref.shape)
    normed_b = (normalize(middle)[0] * gb_ref[...]).astype(BF16)
    tiles, _, tile = hidden_ref.shape
    result_ref[...] = middle

    @pl.loop(0, tiles)
    def _(j):
        cut = pl.ds(pl.multiple_of(j * tile, tile), tile)
        hidden, slope = gelu_both(mm(normed_b, w1_ref[:, cut]))
        hidden = hidden.astype(BF16)
        hidden_ref[j] = hidden
        slope_ref[j] = slope
        result_ref[...] += mm(hidden, w2_ref[cut, :])

    result = result_ref[...]
    result = result.astype(BF16).reshape(rows, images, cols, width)
    part = send_ref.shape[2]
    for i in range(send_ref.shape[0]):
        image, first = divmod(i * part, cols)
        send_ref[i] = result[:, image, first : first + part]


def rows_backward_kernel(
    core_ref, up_ref, slope_hbm, hidden_hbm, w2_hbm, mid_hbm, w1_hbm, ga_hbm, gb_hbm, att_hbm, wo_hbm,
    q_hbm, k_hbm, v_hbm, p_hbm, x_hbm, wq_hbm, wk_hbm, wv_hbm, _,
    mid_grad_ref, dq_ref, dk_ref, dv_ref, keep_ref, send_ref,
    halves, feed_grad_ref, slope_ref, hidden_ref, w2_ref, mid_ref, w1_ref, ga_ref, gb_ref, att_ref, wo_ref,
    q_ref, k_ref, v_ref, p_ref, x_ref, wq_ref, wk_ref, wv_ref, done, tile_done,
):
    rows, images, cols, width = x_ref.shape
    tokens = rows * images * cols
    features = width // HEADS
    scaling = 1.0 / math.sqrt(features)
    sources = (
        w2_hbm, mid_hbm, w1_hbm, ga_hbm, gb_hbm, att_hbm, wo_hbm,
        q_hbm, k_hbm, v_hbm, p_hbm, x_hbm, wq_hbm, wk_hbm, wv_hbm,
    )
    targets = (
        w2_ref, mid_ref, w1_ref, ga_ref, gb_ref, att_ref, wo_ref,
        q_ref, k_ref, v_ref, p_ref, x_ref, wq_ref, wk_ref, wv_ref,
    )
    copies = [pltpu.make_async_copy(sources[i], targets[i], done.at[i]) for i in range(len(sources))]
    tiles, _, tile = slope_ref.shape

    def tile_copies(j):
        return (
            pltpu.make_async_copy(slope_hbm.at[j], slope_ref.at[j], tile_done.at[0, j]),
            pltpu.make_async_copy(hidden_hbm.at[j], hidden_ref.at[j], tile_done.at[1, j]),
        )

    for copy in copies[:5]:
        copy.start()
    for j in range(tiles):
        for copy in tile_copies(j):
            copy.start()
    for copy in copies[5:]:
        copy.start()
    put = putter(core_ref[0], halves)
    up = jnp.concatenate([up_ref[:, r].reshape(images * cols, width) for r in range(rows)], axis=0).astype(F32)
    up_low = up.astype(BF16)
    for copy in copies[:5]:
        copy.wait()
    normal_b, inverse_b = normalize(mid_ref[...].reshape(tokens, width))
    normed_b = (normal_b * gb_ref[...]).astype(BF16)
    feed_grad_ref[...] = jnp.zeros_like(feed_grad_ref)

    @pl.loop(0, tiles, unroll=2)
    def _(j):
        cut = pl.ds(pl.multiple_of(j * tile, tile), tile)
        hidden_grad = mm_right_t(up_low, w2_ref[cut, :])
        for copy in tile_copies(j):
            copy.wait()
        expanded_grad = (slope_ref[j] * hidden_grad).astype(BF16)
        put(4 + j, mm_left_t(normed_b, expanded_grad))
        put(4 + tiles + j, mm_left_t(up_low, hidden_ref[j]))
        feed_grad_ref[...] += mm_right_t(expanded_grad, w1_ref[:, cut])

    normed_grad = feed_grad_ref[...]
    middle_norm, scale_grad = normalize_back(normed_grad, normal_b, inverse_b, gb_ref[...])
    middle_grad = up + middle_norm
    mid_grad_ref[...] = middle_grad
    middle_low = middle_grad.astype(BF16)
    for copy in copies[5:]:
        copy.wait()
    put(3, mm_left_t(att_ref[...].reshape(tokens, width), middle_low))
    up_att = mm_right_t(middle_low, wo_ref[...]).astype(BF16)
    query = q_ref[...].reshape(tokens, width)
    key = k_ref[...].reshape(tokens, width)
    value = v_ref[...].reshape(tokens, width)
    places = head_places(rows * images, cols, features)
    probs = [p_ref[r, i, m] for r in range(rows) for i in range(images) for m in range(HEADS)]
    grads = attend_back(up_att, query, key, value, probs, places, scaling)
    normed_a = (normalize(x_ref[...].astype(F32).reshape(tokens, width))[0] * ga_ref[...]).astype(BF16)
    shared = None
    for i, (grad, target, weight_ref) in enumerate(zip(grads, (dq_ref, dk_ref, dv_ref), (wq_ref, wk_ref, wv_ref))):
        target[...] = grad
        weight_grad = mm_left_t(normed_a, grad)
        put(i, weight_grad)
        part = weight_grad * weight_ref[...].astype(F32)
        shared = part if shared is None else shared + part
    gain_grad = jnp.sum(shared.T, axis=0, keepdims=True) / ga_ref[...]
    emit_grads(halves, stack_gains(gain_grad, scale_grad), keep_ref, send_ref)


def rows_rest_kernel(mid_grad_ref, dq_ref, dk_ref, dv_ref, x_ref, ga_ref, wq_ref, wk_ref, wv_ref, _, grad_ref, token_ref):
    rows, images, cols, width = x_ref.shape
    normal, inverse = normalize(x_ref[...].astype(F32).reshape(rows * images * cols, width))
    normed_grad = None
    for grad_ref_in, weight_ref in zip((dq_ref, dk_ref, dv_ref), (wq_ref, wk_ref, wv_ref)):
        part = mm_right_t(grad_ref_in[...], weight_ref[...])
        normed_grad = part if normed_grad is None else normed_grad + part
    stream_norm, _ = normalize_back(normed_grad, normal, inverse, ga_ref[...])
    grad_ref[...] = (mid_grad_ref[...] + stream_norm).reshape(grad_ref.shape)
    token_ref[...] = jnp.zeros_like(token_ref)


def unpack_kernel(in_ref, _, out_ref, token_ref, done):
    part, cols = in_ref.shape[2], out_ref.shape[2]
    copies = []
    for i in range(in_ref.shape[0]):
        image, first = divmod(i * part, cols)
        target = out_ref.at[:, image, pl.ds(first, part)]
        copies.append(pltpu.make_async_copy(in_ref.at[i], target, done.at[i]))
    for copy in copies:
        copy.start()
    token_ref[...] = jnp.zeros_like(token_ref)
    for copy in copies:
        copy.wait()


def load_groups(ref):
    array = ref[...].astype(F32)
    width = array.shape[-1]
    parts = [array[:, :, i : i + GROUP].reshape(-1, width) for i in range(0, array.shape[2], GROUP)]
    return jnp.concatenate(parts, axis=0)


def store_groups(ref, value):
    sources, rows, cols, width = ref.shape
    groups = cols // GROUP
    tokens = sources * rows * GROUP
    parts = [value[i * tokens : (i + 1) * tokens].reshape(sources, rows, GROUP, width) for i in range(groups)]
    ref[...] = jnp.concatenate(parts, axis=2).astype(ref.dtype)


def columns_kernel(
    core_ref, x_ref, up_ref, ga_ref, gb_ref, wq_hbm, wk_hbm, wv_hbm, wo_hbm, w1_hbm, w2_hbm,
    out_ref, grad_ref, keep_ref, send_ref,
    halves, bias, result_ref, feed_grad_ref, wq_ref, wk_ref, wv_ref, wo_ref, w1_ref, w2_ref, done,
):
    sources, rows, cols, width = x_ref.shape
    groups = cols // GROUP
    tokens = sources * rows * GROUP
    features = width // HEADS
    scaling = 1.0 / math.sqrt(features)
    froms = (wq_hbm, wk_hbm, wv_hbm, wo_hbm, w1_hbm, w2_hbm)
    targets = (wq_ref, wk_ref, wv_ref, wo_ref, w1_ref, w2_ref)
    copies = [pltpu.make_async_copy(froms[i], targets[i], done.at[i]) for i in range(len(froms))]
    for copy in copies:
        copy.start()
    put = putter(core_ref[0], halves)
    bias[...] = causal_bias(tokens, GROUP)
    stream = load_groups(x_ref)
    normal_a, inverse_a = normalize(stream)
    normed_a = (normal_a * ga_ref[...]).astype(BF16)
    for copy in copies[:4]:
        copy.wait()
    query = mm(normed_a, wq_ref[...]).astype(BF16)
    key = mm(normed_a, wk_ref[...]).astype(BF16)
    value = mm(normed_a, wv_ref[...]).astype(BF16)
    places = head_places(groups, tokens, features)
    probs = [softmax(mm_right_t(query[at], key[at]) * scaling + bias[...]) for at in places]
    heads = [mm(prob.astype(BF16), value[at]) for prob, at in zip(probs, places)]
    attended = merge_heads(heads).astype(BF16)
    middle = stream + mm(attended, wo_ref[...])
    normal_b, inverse_b = normalize(middle)
    normed_b = (normal_b * gb_ref[...]).astype(BF16)
    up = load_groups(up_ref)
    up_low = up.astype(BF16)
    for copy in copies[4:]:
        copy.wait()
    result_ref[...] = middle
    feed_grad_ref[...] = jnp.zeros_like(feed_grad_ref)
    feed_back(normed_b, up_low, w1_ref, w2_ref, put, 4, result_ref, feed_grad_ref)
    store_groups(out_ref, result_ref[...])
    normed_grad = feed_grad_ref[...]
    middle_norm, scale_grad = normalize_back(normed_grad, normal_b, inverse_b, gb_ref[...])
    middle_grad = up + middle_norm
    middle_low = middle_grad.astype(BF16)
    put(3, mm_left_t(attended, middle_low))
    up_att = mm_right_t(middle_low, wo_ref[...]).astype(BF16)
    grads = attend_back(up_att, query, key, value, probs, places, scaling)
    normed_grad = project_back(normed_a, grads, (wq_ref, wk_ref, wv_ref), put)
    stream_norm, gain_grad = normalize_back(normed_grad, normal_a, inverse_a, ga_ref[...])
    store_groups(grad_ref, middle_grad + stream_norm)
    emit_grads(halves, stack_gains(gain_grad, scale_grad), keep_ref, send_ref)


def whole(array):
    zeros = (0,) * array.ndim
    return pl.BlockSpec(array.shape, lambda i: zeros)


def whole_out(shape):
    zeros = (0,) * len(shape)
    return pl.BlockSpec(shape, lambda i: zeros)


SCALAR = pl.BlockSpec(memory_space=pltpu.SMEM)
HELD = pl.BlockSpec(memory_space=pltpu.VMEM)
UNREAD = pl.BlockSpec(memory_space=pl.ANY)


def held(array):
    return pltpu.with_memory_space_constraint(array, pltpu.VMEM)


def params(limit=VMEM_LIMIT):
    return pltpu.CompilerParams(vmem_limit_bytes=limit)


def shape_of(shape, dtype):
    return jax.ShapeDtypeStruct(shape, dtype)


def held_shape(shape, dtype):
    return pltpu.VMEM(shape, dtype)


def stored_shape(shape, dtype):
    return pltpu.HBM(shape, dtype)


def stored(array):
    return pltpu.with_memory_space_constraint(array, pltpu.HBM)


def grad_rows(width, hidden_width):
    tile = min(HIDDEN_TILE, hidden_width)
    return 4 * width + 2 * (hidden_width // tile) * width


def cost(*_):
    return pl.CostEstimate(flops=1, bytes_accessed=1, transcendentals=0)


def rows_forward(inputs, gains, matrices, sent_shape):
    rows, images, cols, width = inputs.shape
    low = stored_shape(inputs.shape, BF16)
    wq, wk, wv, wo, w1, w2 = matrices
    tile = min(HIDDEN_TILE, w1.shape[1])
    feed = (w1.shape[1] // tile, rows * images * cols, tile)
    operands = [stored(array) for array in (inputs, gains[0], wq, wk, wv, wo, gains[1], w1, w2)]
    outs = [
        held_shape(sent_shape, BF16),
        low, low, low, low,
        stored_shape(inputs.shape, F32),
        stored_shape((rows, images, HEADS, cols, cols), F32),
        stored_shape(feed, BF16),
        stored_shape(feed, F32),
    ]
    return pl.pallas_call(
        rows_forward_kernel,
        grid=(1,),
        in_specs=[whole(array) for array in operands],
        out_specs=[HELD] + [whole_out(out.shape) for out in outs[1:]],
        out_shape=outs,
        scratch_shapes=[pltpu.VMEM((rows * images * cols, width), F32)],
        compiler_params=params(48 * 1024 * 1024),
        cost_estimate=cost(),
        name="rows_forward",
    )(*operands)


def rows_backward(core, up, kept, after):
    tiles, tokens, _ = kept[0].shape
    hidden_width, width = kept[2].shape
    half = grad_rows(width, hidden_width) // 2
    part = held_shape((half + TAIL, width), BF16)
    grad = held_shape((tokens, width), BF16)
    return pl.pallas_call(
        rows_backward_kernel,
        in_specs=[SCALAR, HELD] + [UNREAD] * (len(kept) + 1),
        out_specs=[HELD] * 6,
        out_shape=[held_shape((tokens, width), F32), grad, grad, grad, part, part],
        scratch_shapes=[pltpu.VMEM((2, half, width), BF16), pltpu.VMEM((tokens, width), F32)]
        + [pltpu.VMEM(array.shape, array.dtype) for array in kept]
        + [pltpu.SemaphoreType.DMA((len(kept) - 2,)), pltpu.SemaphoreType.DMA((2, tiles))],
        compiler_params=params(48 * 1024 * 1024),
        cost_estimate=cost(),
        name="rows_backward",
    )(core, held(up), *[stored(array) for array in kept], after)


def rows_rest(grads, inputs, gain, matrices, after):
    operands = [stored(array) for array in (inputs, gain, *matrices)]
    return pl.pallas_call(
        rows_rest_kernel,
        grid=(1,),
        in_specs=[HELD] * 4 + [whole(array) for array in operands] + [UNREAD],
        out_specs=[whole_out(inputs.shape), HELD],
        out_shape=[stored_shape(inputs.shape, F32), held_shape((8, 128), F32)],
        compiler_params=params(24 * 1024 * 1024),
        cost_estimate=cost(),
        name="rows_rest",
    )(*[held(grad) for grad in grads], *operands, after)


def unpack(array, shape, after):
    return pl.pallas_call(
        unpack_kernel,
        in_specs=[HELD, UNREAD],
        out_specs=[UNREAD, HELD],
        out_shape=[stored_shape(shape, BF16), held_shape((8, 128), F32)],
        scratch_shapes=[pltpu.SemaphoreType.DMA((array.shape[0],))],
        compiler_params=params(SMALL_LIMIT),
        cost_estimate=cost(),
        name="unpack",
    )(held(array), after)


def columns_both(core, stream, up, gains, matrices):
    sources, rows, cols, width = stream.shape
    half = grad_rows(width, matrices[4].shape[1]) // 2
    tokens = sources * rows * GROUP
    part = (half + TAIL, width)
    return pl.pallas_call(
        columns_kernel,
        in_specs=[SCALAR] + [HELD] * 4 + [UNREAD] * len(matrices),
        out_specs=[HELD] * 4,
        out_shape=[held_shape(stream.shape, BF16)] * 2 + [held_shape(part, BF16)] * 2,
        scratch_shapes=[pltpu.VMEM((2, half, width), BF16), pltpu.VMEM((tokens, tokens), F32)]
        + [pltpu.VMEM((tokens * (cols // GROUP), width), F32)] * 2
        + [pltpu.VMEM(array.shape, array.dtype) for array in matrices]
        + [pltpu.SemaphoreType.DMA((len(matrices),))],
        compiler_params=params(40 * 1024 * 1024),
        cost_estimate=cost(),
        name="columns_both",
    )(core, held(stream), held(up), *gains, *[stored(array) for array in matrices])


def add_parts(refs, size):
    total, gains = None, None
    for ref in refs:
        rows = ref[0:size, :].astype(F32)
        tail = ref[size : size + 8, :].astype(F32) + ref[size + 8 : size + TAIL, :].astype(F32)
        total = rows if total is None else total + rows
        gains = tail if gains is None else gains + tail
    return total.astype(BF16), gains


def sum_split_kernel(count, size, ways, sends, at_ref, *refs):
    ins, rider, outs = refs[:count], refs[count + 1 : -1 - sends], refs[-1 - sends : -1]
    parts = refs[-1]
    total, gains = add_parts(ins, size)
    step = size // ways
    for j in range(ways):
        parts[j] = total[j * step : (j + 1) * step, :]
    for j, out in enumerate(outs):
        out[0:step, :] = parts[(at_ref[0] & (ways - 1)) ^ j]
        store_tail(out, step, gains)
        if rider and j:
            out[step + TAIL :, :] = rider[0][...]


def sum_split(at, arrays, size, ways, sends, after, rider=None):
    width = arrays[0].shape[1]
    step = size // ways
    extra = 0 if rider is None else rider.shape[0]
    shapes = [(step + TAIL + (extra if j else 0), width) for j in range(sends)]
    riders = [] if rider is None else [held(rider)]
    return pl.pallas_call(
        functools.partial(sum_split_kernel, len(arrays), size, ways, sends),
        in_specs=[SCALAR] + [HELD] * len(arrays) + [UNREAD] + [HELD] * len(riders),
        out_specs=[HELD] * sends,
        out_shape=[held_shape(shape, BF16) for shape in shapes],
        scratch_shapes=[pltpu.VMEM((ways, step, width), BF16)],
        compiler_params=params(SMALL_LIMIT),
        cost_estimate=small_cost(arrays),
        name="sum_split",
    )(at, *[held(array) for array in arrays], after, *riders)


def sum_last_kernel(count, size, *refs):
    ins, (part, tail) = refs[:count], refs[count + 1 :]
    total, gains = add_parts(ins, size)
    part[...] = total
    store_tail(tail, 0, gains)


def sum_last(arrays, size, after):
    width = arrays[0].shape[1]
    return pl.pallas_call(
        functools.partial(sum_last_kernel, len(arrays), size),
        in_specs=[HELD] * len(arrays) + [UNREAD],
        out_specs=[HELD] * 2,
        out_shape=[held_shape((size, width), BF16), held_shape((TAIL, width), BF16)],
        compiler_params=params(SMALL_LIMIT),
        cost_estimate=small_cost(arrays),
        name="sum_last",
    )(*[held(array) for array in arrays], after)


def join_kernel(ways, first, at_ref, *refs):
    ins, out = refs[:ways], refs[-1]
    size = out.shape[1]
    for j in range(ways):
        start = first if j else 0
        out[at_ref[0] ^ j] = ins[j][start : start + size, :]


def join(at, arrays, first, after):
    ways, (size, width) = len(arrays), arrays[0].shape
    joined = pl.pallas_call(
        functools.partial(join_kernel, ways, first),
        in_specs=[SCALAR] + [HELD] * ways + [UNREAD],
        out_specs=HELD,
        out_shape=held_shape((ways, size, width), BF16),
        compiler_params=params(SMALL_LIMIT),
        cost_estimate=small_cost(arrays),
        name="join",
    )(at, *[held(array) for array in arrays], after)
    return joined.reshape(ways * size, width)


def finish_kernel(buffers, at_ref, own_ref, other_ref, tail_ref, _, *refs):
    *outs, token_ref, halves = refs
    token_ref[...] = jnp.zeros_like(token_ref)
    width = own_ref.shape[1]
    halves[at_ref[0]] = own_ref[...]
    halves[at_ref[0] ^ 1] = other_ref[...]
    gains = tail_ref[0:8, :].astype(F32) + tail_ref[8:16, :].astype(F32)
    first = 0
    for rows, kinds in buffers:
        at = 0
        for kind in kinds:
            out = outs.pop(0)
            if isinstance(kind, int):
                out[...] = gains[kind : kind + 1, :]
                continue
            for j in range(out.size // (width * width)):
                half, row = divmod(at * width, rows // 2)
                block = halves[half, first + row : first + row + width, :].astype(F32)
                if kind == "rows":
                    out[j * width : (j + 1) * width, :] = block.T
                else:
                    out[:, j * width : (j + 1) * width] = block
                at += 1
        first += rows // 2


def finish(at, own, other, tail, buffers, hidden_width, after):
    half, width = own.shape
    shapes = {"square": (width, width), "columns": (width, hidden_width), "rows": (hidden_width, width)}
    kinds = [kind for _, each in buffers for kind in each]
    outs = [shapes.get(kind, (1, width)) for kind in kinds]
    *outs, token = pl.pallas_call(
        functools.partial(finish_kernel, buffers),
        grid=(1,),
        in_specs=[SCALAR, HELD, HELD, HELD, UNREAD],
        out_specs=[whole_out(shape) for shape in outs] + [HELD],
        out_shape=[shape_of(shape, F32) for shape in outs] + [held_shape((8, 128), F32)],
        scratch_shapes=[pltpu.VMEM((2, half, width), BF16)],
        compiler_params=params(24 * 1024 * 1024),
        cost_estimate=cost(),
        name="finish",
    )(at, held(own), held(other), held(tail), after)
    return [out.reshape(width) if isinstance(kind, int) else out for kind, out in zip(kinds, outs)], token


def small_cost(arrays):
    return pl.CostEstimate(flops=1, bytes_accessed=1, transcendentals=0)


class Exchange:
    def __init__(self, bits, scatter, flat, devices):
        self.bits, self.scatter = bits, scatter
        self.ways = 1 << len(bits)
        place = sum(((flat >> bit) & 1) << i for i, bit in enumerate(bits))
        self.place = jnp.reshape(place, (1,)).astype(jnp.int32)
        self.devices = devices

    def swap(self, array, member):
        mask = sum(1 << bit for i, bit in enumerate(self.bits) if (member >> i) & 1)
        return lax.ppermute(array, ALL, [(i, i ^ mask) for i in range(self.devices)])


class Chain:
    def __init__(self, exchanges, buffers, keep, send, hidden_width):
        self.pair, self.four, *self.others = exchanges
        self.rows = sum(rows for rows, _ in buffers) // 2
        self.arrays = [keep, self.pair.swap(send, 1)]
        self.token = keep
        self.buffers, self.hidden_width = buffers, hidden_width

    def cut(self, after, rider=None):
        ways = self.four.ways
        parts = sum_split(self.four.place, self.arrays, self.rows, ways, ways, after, rider)
        self.arrays = [parts[0]] + [self.four.swap(parts[j], j) for j in range(1, ways)]
        self.rows //= ways
        return parts[0]

    def add(self, after):
        exchange = self.others.pop(0)
        (part,) = sum_split(self.pair.place, self.arrays, self.rows, 1, 1, after)
        self.arrays = [part, exchange.swap(part, 1)]
        return part

    def last(self, after):
        self.part, self.tail = sum_last(self.arrays, self.rows, after)
        return self.part

    def spread(self):
        self.pieces = [self.part] + [self.four.swap(self.part, j) for j in range(1, self.four.ways)]
        self.first = 0

    def ride(self, chain):
        self.pieces = [self.part] + chain.arrays[1:]
        self.first = chain.rows + TAIL

    def join(self, after):
        self.own = join(self.four.place, self.pieces, self.first, after)
        self.other = self.pair.swap(self.own, 1)
        return self.own

    def finish(self, after):
        self.results, token = finish(
            self.pair.place, self.own, self.other, self.tail, self.buffers, self.hidden_width, after
        )
        return token


def on_device(inputs, cotangent, *weights):
    rows, images, cols, width = inputs.shape
    height = lax.axis_size("row")
    devices = height * lax.axis_size("img")
    flat = lax.axis_index("img") * height + lax.axis_index("row")
    top = devices.bit_length() - 2
    exchanges = [Exchange([0], True, flat, devices), Exchange([top, 1], True, flat, devices)]
    exchanges += [Exchange([bit], False, flat, devices) for bit in range(2, top)]
    core = exchanges[0].place
    rows_gains = [weights[i].reshape(1, width) for i in (0, 5)]
    column_gains = [weights[i].reshape(1, width) for i in (8, 13)]
    matrices = [w for w in weights if w.ndim == 2]
    hidden_width = matrices[4].shape[1]
    owned = images * cols // height

    def trade(array):
        return lax.all_to_all(array, "row", 0, 0, tiled=True)

    squares = ("square",) * 4
    total = grad_rows(width, hidden_width)
    sent_shape = (height, rows, owned, width)
    up = cotangent.reshape(rows, height, owned, width).transpose(1, 0, 2, 3)
    up = trade(up)
    sent, query, key, value, attended, middle, probs, hidden, slope = rows_forward(
        inputs, rows_gains, matrices[:6], sent_shape
    )
    sent, up = lax.optimization_barrier((sent, up))
    stream = trade(sent)
    final, between_grad, keep, send = columns_both(core, stream, up, column_gains, matrices[6:])
    kinds = (0, *squares, 1, "columns", "rows")
    columns = Chain(exchanges, ((total, kinds),), keep, send, hidden_width)
    token = columns.add(columns.cut(columns.token))
    between_grad = trade(between_grad)
    between_grad, final, token = lax.optimization_barrier((between_grad, final, token))
    final = trade(final)
    wq, wk, wv, wo, w1, w2 = matrices[:6]
    kept = (slope, hidden, w2, middle, w1, *rows_gains, attended, wo, query, key, value, probs, inputs, wq, wk, wv)
    *grads, keep, send = rows_backward(core, between_grad, kept, token)
    rows_chain = Chain(exchanges, ((total, kinds),), keep, send, hidden_width)
    token = rows_chain.cut(rows_chain.token)
    stream_grad, token = rows_rest(grads, inputs, rows_gains[0], (wq, wk, wv), token)
    while columns.others:
        token = columns.add(token)
    final, token = unpack(final, inputs.shape, token)
    token = rows_chain.add(token)
    token = columns.last(token)
    columns.spread()
    while rows_chain.others:
        token = rows_chain.add(token)
    token = rows_chain.last(token)
    token = columns.join(token)
    rows_chain.spread()
    token = columns.finish(token)
    token = rows_chain.join(token)
    rows_chain.finish(token)
    c_gain, c_query, c_keys, c_values, c_mixer, c_scale, c_expand, c_shrink = columns.results
    r_gain, r_query, r_keys, r_values, r_mixer, r_scale, r_expand, r_shrink = rows_chain.results
    return (
        final, stream_grad,
        r_gain, r_query, r_keys, r_values, r_mixer, r_scale, r_expand, r_shrink,
        c_gain, c_query, c_keys, c_values, c_mixer, c_scale, c_expand, c_shrink,
    )


def solution(mesh):
    moved = P("row", "img", None, None)
    return jax.shard_map(
        on_device,
        mesh=mesh,
        in_specs=(moved, moved) + (P(),) * 16,
        out_specs=(moved, moved) + (P(),) * 16,
        check_vma=False,
    )
```

```python
import functools
import math

import jax
import jax.numpy as jnp
from jax import lax
from jax.experimental import pallas as pl
from jax.experimental.pallas import tpu as pltpu
from jax.sharding import PartitionSpec as P

HEADS = 2
EPS = 1e-05
GROUP = 8
TAIL = 16
HIDDEN_TILE = 256
VMEM_LIMIT = 24 * 1024 * 1024
SMALL_LIMIT = 12 * 1024 * 1024
ALL = ("img", "row")
F32 = jnp.float32
BF16 = jnp.bfloat16


def mm(left, right):
    return lax.dot_general(left, right, (((1,), (0,)), ((), ())), preferred_element_type=F32)


def mm_right_t(left, right):
    return lax.dot_general(left, right, (((1,), (1,)), ((), ())), preferred_element_type=F32)


def mm_left_t(left, right):
    return lax.dot_general(left, right, (((0,), (0,)), ((), ())), preferred_element_type=F32)


def normalize(stream):
    centred = stream - jnp.mean(stream, axis=-1, keepdims=True)
    inverse = lax.rsqrt(jnp.mean(centred * centred, axis=-1, keepdims=True) + EPS)
    return centred * inverse, inverse


def normalize_back(upstream, normal, inverse, gain):
    scaled = upstream * gain
    centred = (
        scaled
        - jnp.mean(scaled, axis=-1, keepdims=True)
        - normal * jnp.mean(scaled * normal, axis=-1, keepdims=True)
    )
    return inverse * centred, jnp.sum(upstream * normal, axis=0, keepdims=True)


ROOT = math.sqrt(2.0 / math.pi)
CUBE = 0.044715


def gelu_both(value):
    square = value * value
    bent = jnp.tanh(ROOT * (value + CUBE * (square * value)))
    half = 0.5 * (1.0 + bent)
    slope = half + (0.5 * ROOT) * value * (1.0 - bent * bent) * (1.0 + (3.0 * CUBE) * square)
    return value * half, slope


def softmax(scores):
    risen = jnp.exp(scores - jnp.max(scores, axis=-1, keepdims=True))
    return risen * (1.0 / jnp.sum(risen, axis=-1, keepdims=True))


def causal_bias(size, period):
    row = lax.broadcasted_iota(jnp.int32, (size, size), 0)
    col = lax.broadcasted_iota(jnp.int32, (size, size), 1)
    visible = (row >= col) & (((row ^ col) & (period - 1)) == 0)
    return jnp.where(visible, 0.0, -1e30).astype(F32)


def head_places(groups, tokens, features):
    return [
        (slice(i * tokens, (i + 1) * tokens), slice(m * features, (m + 1) * features))
        for i in range(groups)
        for m in range(HEADS)
    ]


def merge_heads(parts):
    pairs = [parts[i : i + HEADS] for i in range(0, len(parts), HEADS)]
    return jnp.concatenate([jnp.concatenate(pair, axis=1) for pair in pairs], axis=0)


def attend_back(up, query, key, value, probs, places, scaling):
    prob_grads = [mm_right_t(up[at], value[at]) for at in places]
    score_grads = []
    for prob, prob_grad in zip(probs, prob_grads):
        inner = jnp.sum(prob * prob_grad, axis=-1, keepdims=True)
        score_grads.append((prob * (prob_grad - inner)).astype(BF16))
    value_grads = [mm_left_t(prob.astype(BF16), up[at]).astype(BF16) for prob, at in zip(probs, places)]
    query_grads = [(mm(grad, key[at]) * scaling).astype(BF16) for grad, at in zip(score_grads, places)]
    key_grads = [(mm_left_t(grad, query[at]) * scaling).astype(BF16) for grad, at in zip(score_grads, places)]
    return tuple(merge_heads(grads) for grads in (query_grads, key_grads, value_grads))


def feed_back(normed, up_low, expand_ref, shrink_ref, put, first, result_ref, grad_ref):
    hidden_width = expand_ref.shape[1]
    tile = min(HIDDEN_TILE, hidden_width)
    tiles = hidden_width // tile

    @pl.loop(0, tiles, unroll=2)
    def _(j):
        cut = pl.ds(pl.multiple_of(j * tile, tile), tile)
        expand = expand_ref[:, cut]
        shrink = shrink_ref[cut, :]
        hidden, slope = gelu_both(mm(normed, expand))
        hidden = hidden.astype(BF16)
        result_ref[...] += mm(hidden, shrink)
        expanded_grad = (slope * mm_right_t(up_low, shrink)).astype(BF16)
        put(first + j, mm_left_t(normed, expanded_grad))
        put(first + tiles + j, mm_left_t(up_low, hidden))
        grad_ref[...] += mm_right_t(expanded_grad, expand)


def project_back(normed_low, grads, weight_refs, put):
    total = None
    for i, (grad, weight_ref) in enumerate(zip(grads, weight_refs)):
        put(i, mm_left_t(normed_low, grad))
        part = mm_right_t(grad, weight_ref[...])
        total = part if total is None else total + part
    return total


def store_tail(ref, at, gains):
    high = gains.astype(BF16)
    ref[at : at + 8, :] = high
    ref[at + 8 : at + 16, :] = (gains - high.astype(F32)).astype(BF16)


def putter(core, halves):
    width = halves.shape[2]
    blocks = halves.shape[1] // width

    def put(block, value):
        start = pl.multiple_of(lax.rem(block, blocks) * width, width)
        halves[lax.div(block, blocks) ^ core, pl.ds(start, width), :] = value.astype(BF16)

    return put


def emit_grads(halves, gains, keep_ref, send_ref):
    for i, ref in enumerate((keep_ref, send_ref)):
        ref[0 : halves.shape[1], :] = halves[i]
        store_tail(ref, halves.shape[1], gains)


def stack_gains(gain, scale):
    return jnp.concatenate([gain, scale, jnp.zeros((6, gain.shape[1]), F32)], axis=0)


def rows_forward_kernel(
    x_ref, ga_ref, wq_ref, wk_ref, wv_ref, wo_ref, gb_ref, w1_ref, w2_ref,
    send_ref, q_ref, k_ref, v_ref, att_ref, mid_ref, p_ref, hidden_ref, slope_ref, result_ref,
):
    rows, images, cols, width = x_ref.shape
    tokens = rows * images * cols
    features = width // HEADS
    scaling = 1.0 / math.sqrt(features)
    stream = x_ref[...].astype(F32).reshape(tokens, width)
    normed = (normalize(stream)[0] * ga_ref[...]).astype(BF16)
    query = mm(normed, wq_ref[...]).astype(BF16)
    key = mm(normed, wk_ref[...]).astype(BF16)
    value = mm(normed, wv_ref[...]).astype(BF16)
    q_ref[...] = query.reshape(q_ref.shape)
    k_ref[...] = key.reshape(q_ref.shape)
    v_ref[...] = value.reshape(q_ref.shape)
    bias = causal_bias(cols, 1)
    places = head_places(rows * images, cols, features)
    probs = [softmax(mm_right_t(query[at], key[at]) * scaling + bias) for at in places]
    heads = [mm(prob.astype(BF16), value[at]) for prob, at in zip(probs, places)]
    for i, prob in enumerate(probs):
        group, m = divmod(i, HEADS)
        p_ref[group // images, group % images, m] = prob
    attended = merge_heads(heads).astype(BF16)
    att_ref[...] = attended.reshape(att_ref.shape)
    middle = stream + mm(attended, wo_ref[...])
    mid_ref[...] = middle.reshape(mid_ref.shape)
    normed_b = (normalize(middle)[0] * gb_ref[...]).astype(BF16)
    tiles, _, tile = hidden_ref.shape
    result_ref[...] = middle

    @pl.loop(0, tiles)
    def _(j):
        cut = pl.ds(pl.multiple_of(j * tile, tile), tile)
        hidden, slope = gelu_both(mm(normed_b, w1_ref[:, cut]))
        hidden = hidden.astype(BF16)
        hidden_ref[j] = hidden
        slope_ref[j] = slope
        result_ref[...] += mm(hidden, w2_ref[cut, :])

    result = result_ref[...]
    result = result.astype(BF16).reshape(rows, images, cols, width)
    part = send_ref.shape[2]
    for i in range(send_ref.shape[0]):
        image, first = divmod(i * part, cols)
        send_ref[i] = result[:, image, first : first + part]


def rows_backward_kernel(
    core_ref, up_ref, slope_hbm, hidden_hbm, w2_hbm, mid_hbm, w1_hbm, ga_hbm, gb_hbm, att_hbm, wo_hbm,
    q_hbm, k_hbm, v_hbm, p_hbm, x_hbm, wq_hbm, wk_hbm, wv_hbm, _,
    mid_grad_ref, dq_ref, dk_ref, dv_ref, keep_ref, send_ref,
    halves, feed_grad_ref, slope_ref, hidden_ref, w2_ref, mid_ref, w1_ref, ga_ref, gb_ref, att_ref, wo_ref,
    q_ref, k_ref, v_ref, p_ref, x_ref, wq_ref, wk_ref, wv_ref, done, tile_done,
):
    rows, images, cols, width = x_ref.shape
    tokens = rows * images * cols
    features = width // HEADS
    scaling = 1.0 / math.sqrt(features)
    sources = (
        w2_hbm, mid_hbm, w1_hbm, ga_hbm, gb_hbm, att_hbm, wo_hbm,
        q_hbm, k_hbm, v_hbm, p_hbm, x_hbm, wq_hbm, wk_hbm, wv_hbm,
    )
    targets = (
        w2_ref, mid_ref, w1_ref, ga_ref, gb_ref, att_ref, wo_ref,
        q_ref, k_ref, v_ref, p_ref, x_ref, wq_ref, wk_ref, wv_ref,
    )
    copies = [pltpu.make_async_copy(sources[i], targets[i], done.at[i]) for i in range(len(sources))]
    tiles, _, tile = slope_ref.shape

    def tile_copies(j):
        return (
            pltpu.make_async_copy(slope_hbm.at[j], slope_ref.at[j], tile_done.at[0, j]),
            pltpu.make_async_copy(hidden_hbm.at[j], hidden_ref.at[j], tile_done.at[1, j]),
        )

    for copy in copies[:5]:
        copy.start()
    for j in range(tiles):
        for copy in tile_copies(j):
            copy.start()
    for copy in copies[5:]:
        copy.start()
    put = putter(core_ref[0], halves)
    up = jnp.concatenate([up_ref[:, r].reshape(images * cols, width) for r in range(rows)], axis=0).astype(F32)
    up_low = up.astype(BF16)
    for copy in copies[:5]:
        copy.wait()
    normal_b, inverse_b = normalize(mid_ref[...].reshape(tokens, width))
    normed_b = (normal_b * gb_ref[...]).astype(BF16)
    feed_grad_ref[...] = jnp.zeros_like(feed_grad_ref)

    @pl.loop(0, tiles, unroll=2)
    def _(j):
        cut = pl.ds(pl.multiple_of(j * tile, tile), tile)
        hidden_grad = mm_right_t(up_low, w2_ref[cut, :])
        for copy in tile_copies(j):
            copy.wait()
        expanded_grad = (slope_ref[j] * hidden_grad).astype(BF16)
        put(4 + j, mm_left_t(normed_b, expanded_grad))
        put(4 + tiles + j, mm_left_t(up_low, hidden_ref[j]))
        feed_grad_ref[...] += mm_right_t(expanded_grad, w1_ref[:, cut])

    normed_grad = feed_grad_ref[...]
    middle_norm, scale_grad = normalize_back(normed_grad, normal_b, inverse_b, gb_ref[...])
    middle_grad = up + middle_norm
    mid_grad_ref[...] = middle_grad
    middle_low = middle_grad.astype(BF16)
    for copy in copies[5:]:
        copy.wait()
    put(3, mm_left_t(att_ref[...].reshape(tokens, width), middle_low))
    up_att = mm_right_t(middle_low, wo_ref[...]).astype(BF16)
    query = q_ref[...].reshape(tokens, width)
    key = k_ref[...].reshape(tokens, width)
    value = v_ref[...].reshape(tokens, width)
    places = head_places(rows * images, cols, features)
    probs = [p_ref[r, i, m] for r in range(rows) for i in range(images) for m in range(HEADS)]
    grads = attend_back(up_att, query, key, value, probs, places, scaling)
    normed_a = (normalize(x_ref[...].astype(F32).reshape(tokens, width))[0] * ga_ref[...]).astype(BF16)
    shared = None
    for i, (grad, target, weight_ref) in enumerate(zip(grads, (dq_ref, dk_ref, dv_ref), (wq_ref, wk_ref, wv_ref))):
        target[...] = grad
        weight_grad = mm_left_t(normed_a, grad)
        put(i, weight_grad)
        part = weight_grad * weight_ref[...].astype(F32)
        shared = part if shared is None else shared + part
    gain_grad = jnp.sum(shared.T, axis=0, keepdims=True) / ga_ref[...]
    emit_grads(halves, stack_gains(gain_grad, scale_grad), keep_ref, send_ref)


def rows_rest_kernel(mid_grad_ref, dq_ref, dk_ref, dv_ref, x_ref, ga_ref, wq_ref, wk_ref, wv_ref, _, grad_ref, token_ref):
    rows, images, cols, width = x_ref.shape
    normal, inverse = normalize(x_ref[...].astype(F32).reshape(rows * images * cols, width))
    normed_grad = None
    for grad_ref_in, weight_ref in zip((dq_ref, dk_ref, dv_ref), (wq_ref, wk_ref, wv_ref)):
        part = mm_right_t(grad_ref_in[...], weight_ref[...])
        normed_grad = part if normed_grad is None else normed_grad + part
    stream_norm, _ = normalize_back(normed_grad, normal, inverse, ga_ref[...])
    grad_ref[...] = (mid_grad_ref[...] + stream_norm).reshape(grad_ref.shape)
    token_ref[...] = jnp.zeros_like(token_ref)


def unpack_kernel(in_ref, _, out_ref, token_ref, done):
    part, cols = in_ref.shape[2], out_ref.shape[2]
    copies = []
    for i in range(in_ref.shape[0]):
        image, first = divmod(i * part, cols)
        target = out_ref.at[:, image, pl.ds(first, part)]
        copies.append(pltpu.make_async_copy(in_ref.at[i], target, done.at[i]))
    for copy in copies:
        copy.start()
    token_ref[...] = jnp.zeros_like(token_ref)
    for copy in copies:
        copy.wait()


def load_groups(ref):
    array = ref[...].astype(F32)
    width = array.shape[-1]
    parts = [array[:, :, i : i + GROUP].reshape(-1, width) for i in range(0, array.shape[2], GROUP)]
    return jnp.concatenate(parts, axis=0)


def store_groups(ref, value):
    sources, rows, cols, width = ref.shape
    groups = cols // GROUP
    tokens = sources * rows * GROUP
    parts = [value[i * tokens : (i + 1) * tokens].reshape(sources, rows, GROUP, width) for i in range(groups)]
    ref[...] = jnp.concatenate(parts, axis=2).astype(ref.dtype)


def columns_kernel(
    core_ref, x_ref, up_ref, ga_ref, gb_ref, wq_hbm, wk_hbm, wv_hbm, wo_hbm, w1_hbm, w2_hbm,
    out_ref, grad_ref, keep_ref, send_ref,
    halves, bias, result_ref, feed_grad_ref, wq_ref, wk_ref, wv_ref, wo_ref, w1_ref, w2_ref, done,
):
    sources, rows, cols, width = x_ref.shape
    groups = cols // GROUP
    tokens = sources * rows * GROUP
    features = width // HEADS
    scaling = 1.0 / math.sqrt(features)
    froms = (wq_hbm, wk_hbm, wv_hbm, wo_hbm, w1_hbm, w2_hbm)
    targets = (wq_ref, wk_ref, wv_ref, wo_ref, w1_ref, w2_ref)
    copies = [pltpu.make_async_copy(froms[i], targets[i], done.at[i]) for i in range(len(froms))]
    for copy in copies:
        copy.start()
    put = putter(core_ref[0], halves)
    bias[...] = causal_bias(tokens, GROUP)
    stream = load_groups(x_ref)
    normal_a, inverse_a = normalize(stream)
    normed_a = (normal_a * ga_ref[...]).astype(BF16)
    for copy in copies[:4]:
        copy.wait()
    query = mm(normed_a, wq_ref[...]).astype(BF16)
    key = mm(normed_a, wk_ref[...]).astype(BF16)
    value = mm(normed_a, wv_ref[...]).astype(BF16)
    places = head_places(groups, tokens, features)
    probs = [softmax(mm_right_t(query[at], key[at]) * scaling + bias[...]) for at in places]
    heads = [mm(prob.astype(BF16), value[at]) for prob, at in zip(probs, places)]
    attended = merge_heads(heads).astype(BF16)
    middle = stream + mm(attended, wo_ref[...])
    normal_b, inverse_b = normalize(middle)
    normed_b = (normal_b * gb_ref[...]).astype(BF16)
    up = load_groups(up_ref)
    up_low = up.astype(BF16)
    for copy in copies[4:]:
        copy.wait()
    result_ref[...] = middle
    feed_grad_ref[...] = jnp.zeros_like(feed_grad_ref)
    feed_back(normed_b, up_low, w1_ref, w2_ref, put, 4, result_ref, feed_grad_ref)
    store_groups(out_ref, result_ref[...])
    normed_grad = feed_grad_ref[...]
    middle_norm, scale_grad = normalize_back(normed_grad, normal_b, inverse_b, gb_ref[...])
    middle_grad = up + middle_norm
    middle_low = middle_grad.astype(BF16)
    put(3, mm_left_t(attended, middle_low))
    up_att = mm_right_t(middle_low, wo_ref[...]).astype(BF16)
    grads = attend_back(up_att, query, key, value, probs, places, scaling)
    normed_grad = project_back(normed_a, grads, (wq_ref, wk_ref, wv_ref), put)
    stream_norm, gain_grad = normalize_back(normed_grad, normal_a, inverse_a, ga_ref[...])
    store_groups(grad_ref, middle_grad + stream_norm)
    emit_grads(halves, stack_gains(gain_grad, scale_grad), keep_ref, send_ref)


def whole(array):
    zeros = (0,) * array.ndim
    return pl.BlockSpec(array.shape, lambda i: zeros)


def whole_out(shape):
    zeros = (0,) * len(shape)
    return pl.BlockSpec(shape, lambda i: zeros)


SCALAR = pl.BlockSpec(memory_space=pltpu.SMEM)
HELD = pl.BlockSpec(memory_space=pltpu.VMEM)
UNREAD = pl.BlockSpec(memory_space=pl.ANY)


def held(array):
    return pltpu.with_memory_space_constraint(array, pltpu.VMEM)


def params(limit=VMEM_LIMIT):
    return pltpu.CompilerParams(vmem_limit_bytes=limit)


def shape_of(shape, dtype):
    return jax.ShapeDtypeStruct(shape, dtype)


def held_shape(shape, dtype):
    return pltpu.VMEM(shape, dtype)


def stored_shape(shape, dtype):
    return pltpu.HBM(shape, dtype)


def stored(array):
    return pltpu.with_memory_space_constraint(array, pltpu.HBM)


def grad_rows(width, hidden_width):
    tile = min(HIDDEN_TILE, hidden_width)
    return 4 * width + 2 * (hidden_width // tile) * width


def cost(*_):
    return pl.CostEstimate(flops=1, bytes_accessed=1, transcendentals=0)


def rows_forward(inputs, gains, matrices, sent_shape):
    rows, images, cols, width = inputs.shape
    low = stored_shape(inputs.shape, BF16)
    wq, wk, wv, wo, w1, w2 = matrices
    tile = min(HIDDEN_TILE, w1.shape[1])
    feed = (w1.shape[1] // tile, rows * images * cols, tile)
    operands = [stored(array) for array in (inputs, gains[0], wq, wk, wv, wo, gains[1], w1, w2)]
    outs = [
        held_shape(sent_shape, BF16),
        low, low, low, low,
        stored_shape(inputs.shape, F32),
        stored_shape((rows, images, HEADS, cols, cols), F32),
        stored_shape(feed, BF16),
        stored_shape(feed, F32),
    ]
    return pl.pallas_call(
        rows_forward_kernel,
        grid=(1,),
        in_specs=[whole(array) for array in operands],
        out_specs=[HELD] + [whole_out(out.shape) for out in outs[1:]],
        out_shape=outs,
        scratch_shapes=[pltpu.VMEM((rows * images * cols, width), F32)],
        compiler_params=params(48 * 1024 * 1024),
        cost_estimate=cost(),
        name="rows_forward",
    )(*operands)


def rows_backward(core, up, kept, after):
    tiles, tokens, _ = kept[0].shape
    hidden_width, width = kept[2].shape
    half = grad_rows(width, hidden_width) // 2
    part = held_shape((half + TAIL, width), BF16)
    grad = held_shape((tokens, width), BF16)
    return pl.pallas_call(
        rows_backward_kernel,
        in_specs=[SCALAR, HELD] + [UNREAD] * (len(kept) + 1),
        out_specs=[HELD] * 6,
        out_shape=[held_shape((tokens, width), F32), grad, grad, grad, part, part],
        scratch_shapes=[pltpu.VMEM((2, half, width), BF16), pltpu.VMEM((tokens, width), F32)]
        + [pltpu.VMEM(array.shape, array.dtype) for array in kept]
        + [pltpu.SemaphoreType.DMA((len(kept) - 2,)), pltpu.SemaphoreType.DMA((2, tiles))],
        compiler_params=params(48 * 1024 * 1024),
        cost_estimate=cost(),
        name="rows_backward",
    )(core, held(up), *[stored(array) for array in kept], after)


def rows_rest(grads, inputs, gain, matrices, after):
    operands = [stored(array) for array in (inputs, gain, *matrices)]
    return pl.pallas_call(
        rows_rest_kernel,
        grid=(1,),
        in_specs=[HELD] * 4 + [whole(array) for array in operands] + [UNREAD],
        out_specs=[whole_out(inputs.shape), HELD],
        out_shape=[stored_shape(inputs.shape, F32), held_shape((8, 128), F32)],
        compiler_params=params(24 * 1024 * 1024),
        cost_estimate=cost(),
        name="rows_rest",
    )(*[held(grad) for grad in grads], *operands, after)


def unpack(array, shape, after):
    return pl.pallas_call(
        unpack_kernel,
        in_specs=[HELD, UNREAD],
        out_specs=[UNREAD, HELD],
        out_shape=[stored_shape(shape, BF16), held_shape((8, 128), F32)],
        scratch_shapes=[pltpu.SemaphoreType.DMA((array.shape[0],))],
        compiler_params=params(SMALL_LIMIT),
        cost_estimate=cost(),
        name="unpack",
    )(held(array), after)


def columns_both(core, stream, up, gains, matrices):
    sources, rows, cols, width = stream.shape
    half = grad_rows(width, matrices[4].shape[1]) // 2
    tokens = sources * rows * GROUP
    part = (half + TAIL, width)
    return pl.pallas_call(
        columns_kernel,
        in_specs=[SCALAR] + [HELD] * 4 + [UNREAD] * len(matrices),
        out_specs=[HELD] * 4,
        out_shape=[held_shape(stream.shape, BF16)] * 2 + [held_shape(part, BF16)] * 2,
        scratch_shapes=[pltpu.VMEM((2, half, width), BF16), pltpu.VMEM((tokens, tokens), F32)]
        + [pltpu.VMEM((tokens * (cols // GROUP), width), F32)] * 2
        + [pltpu.VMEM(array.shape, array.dtype) for array in matrices]
        + [pltpu.SemaphoreType.DMA((len(matrices),))],
        compiler_params=params(40 * 1024 * 1024),
        cost_estimate=cost(),
        name="columns_both",
    )(core, held(stream), held(up), *gains, *[stored(array) for array in matrices])


def add_parts(refs, size):
    total, gains = None, None
    for ref in refs:
        rows = ref[0:size, :].astype(F32)
        tail = ref[size : size + 8, :].astype(F32) + ref[size + 8 : size + TAIL, :].astype(F32)
        total = rows if total is None else total + rows
        gains = tail if gains is None else gains + tail
    return total.astype(BF16), gains


def sum_split_kernel(count, size, ways, sends, at_ref, *refs):
    ins, rider, outs = refs[:count], refs[count + 1 : -1 - sends], refs[-1 - sends : -1]
    parts = refs[-1]
    total, gains = add_parts(ins, size)
    step = size // ways
    for j in range(ways):
        parts[j] = total[j * step : (j + 1) * step, :]
    for j, out in enumerate(outs):
        out[0:step, :] = parts[(at_ref[0] & (ways - 1)) ^ j]
        store_tail(out, step, gains)
        if rider and j:
            out[step + TAIL :, :] = rider[0][...]


def sum_split(at, arrays, size, ways, sends, after, rider=None):
    width = arrays[0].shape[1]
    step = size // ways
    extra = 0 if rider is None else rider.shape[0]
    shapes = [(step + TAIL + (extra if j else 0), width) for j in range(sends)]
    riders = [] if rider is None else [held(rider)]
    return pl.pallas_call(
        functools.partial(sum_split_kernel, len(arrays), size, ways, sends),
        in_specs=[SCALAR] + [HELD] * len(arrays) + [UNREAD] + [HELD] * len(riders),
        out_specs=[HELD] * sends,
        out_shape=[held_shape(shape, BF16) for shape in shapes],
        scratch_shapes=[pltpu.VMEM((ways, step, width), BF16)],
        compiler_params=params(SMALL_LIMIT),
        cost_estimate=small_cost(arrays),
        name="sum_split",
    )(at, *[held(array) for array in arrays], after, *riders)


def sum_last_kernel(count, size, *refs):
    ins, (part, tail) = refs[:count], refs[count + 1 :]
    total, gains = add_parts(ins, size)
    part[...] = total
    store_tail(tail, 0, gains)


def sum_last(arrays, size, after):
    width = arrays[0].shape[1]
    return pl.pallas_call(
        functools.partial(sum_last_kernel, len(arrays), size),
        in_specs=[HELD] * len(arrays) + [UNREAD],
        out_specs=[HELD] * 2,
        out_shape=[held_shape((size, width), BF16), held_shape((TAIL, width), BF16)],
        compiler_params=params(SMALL_LIMIT),
        cost_estimate=small_cost(arrays),
        name="sum_last",
    )(*[held(array) for array in arrays], after)


def join_kernel(ways, first, at_ref, *refs):
    ins, out = refs[:ways], refs[-1]
    size = out.shape[1]
    for j in range(ways):
        start = first if j else 0
        out[at_ref[0] ^ j] = ins[j][start : start + size, :]


def join(at, arrays, first, after):
    ways, (size, width) = len(arrays), arrays[0].shape
    joined = pl.pallas_call(
        functools.partial(join_kernel, ways, first),
        in_specs=[SCALAR] + [HELD] * ways + [UNREAD],
        out_specs=HELD,
        out_shape=held_shape((ways, size, width), BF16),
        compiler_params=params(SMALL_LIMIT),
        cost_estimate=small_cost(arrays),
        name="join",
    )(at, *[held(array) for array in arrays], after)
    return joined.reshape(ways * size, width)


def finish_kernel(buffers, at_ref, own_ref, other_ref, tail_ref, _, *refs):
    *outs, token_ref, halves = refs
    token_ref[...] = jnp.zeros_like(token_ref)
    width = own_ref.shape[1]
    halves[at_ref[0]] = own_ref[...]
    halves[at_ref[0] ^ 1] = other_ref[...]
    gains = tail_ref[0:8, :].astype(F32) + tail_ref[8:16, :].astype(F32)
    first = 0
    for rows, kinds in buffers:
        at = 0
        for kind in kinds:
            out = outs.pop(0)
            if isinstance(kind, int):
                out[...] = gains[kind : kind + 1, :]
                continue
            for j in range(out.size // (width * width)):
                half, row = divmod(at * width, rows // 2)
                block = halves[half, first + row : first + row + width, :].astype(F32)
                if kind == "rows":
                    out[j * width : (j + 1) * width, :] = block.T
                else:
                    out[:, j * width : (j + 1) * width] = block
                at += 1
        first += rows // 2


def finish(at, own, other, tail, buffers, hidden_width, after):
    half, width = own.shape
    shapes = {"square": (width, width), "columns": (width, hidden_width), "rows": (hidden_width, width)}
    kinds = [kind for _, each in buffers for kind in each]
    outs = [shapes.get(kind, (1, width)) for kind in kinds]
    *outs, token = pl.pallas_call(
        functools.partial(finish_kernel, buffers),
        grid=(1,),
        in_specs=[SCALAR, HELD, HELD, HELD, UNREAD],
        out_specs=[whole_out(shape) for shape in outs] + [HELD],
        out_shape=[shape_of(shape, F32) for shape in outs] + [held_shape((8, 128), F32)],
        scratch_shapes=[pltpu.VMEM((2, half, width), BF16)],
        compiler_params=params(24 * 1024 * 1024),
        cost_estimate=cost(),
        name="finish",
    )(at, held(own), held(other), held(tail), after)
    return [out.reshape(width) if isinstance(kind, int) else out for kind, out in zip(kinds, outs)], token


def small_cost(arrays):
    return pl.CostEstimate(flops=1, bytes_accessed=1, transcendentals=0)


class Exchange:
    def __init__(self, bits, scatter, flat, devices):
        self.bits, self.scatter = bits, scatter
        self.ways = 1 << len(bits)
        place = sum(((flat >> bit) & 1) << i for i, bit in enumerate(bits))
        self.place = jnp.reshape(place, (1,)).astype(jnp.int32)
        self.devices = devices

    def swap(self, array, member):
        mask = sum(1 << bit for i, bit in enumerate(self.bits) if (member >> i) & 1)
        return lax.ppermute(array, ALL, [(i, i ^ mask) for i in range(self.devices)])


class Chain:
    def __init__(self, exchanges, buffers, keep, send, hidden_width):
        self.pair, self.four, *self.others = exchanges
        self.rows = sum(rows for rows, _ in buffers) // 2
        self.arrays = [keep, self.pair.swap(send, 1)]
        self.token = keep
        self.buffers, self.hidden_width = buffers, hidden_width

    def cut(self, after, rider=None):
        ways = self.four.ways
        parts = sum_split(self.four.place, self.arrays, self.rows, ways, ways, after, rider)
        self.arrays = [parts[0]] + [self.four.swap(parts[j], j) for j in range(1, ways)]
        self.rows //= ways
        return parts[0]

    def add(self, after):
        exchange = self.others.pop(0)
        (part,) = sum_split(self.pair.place, self.arrays, self.rows, 1, 1, after)
        self.arrays = [part, exchange.swap(part, 1)]
        return part

    def last(self, after):
        self.part, self.tail = sum_last(self.arrays, self.rows, after)
        return self.part

    def spread(self):
        self.pieces = [self.part] + [self.four.swap(self.part, j) for j in range(1, self.four.ways)]
        self.first = 0

    def ride(self, chain):
        self.pieces = [self.part] + chain.arrays[1:]
        self.first = chain.rows + TAIL

    def join(self, after):
        self.own = join(self.four.place, self.pieces, self.first, after)
        self.other = self.pair.swap(self.own, 1)
        return self.own

    def finish(self, after):
        self.results, token = finish(
            self.pair.place, self.own, self.other, self.tail, self.buffers, self.hidden_width, after
        )
        return token


def on_device(inputs, cotangent, *weights):
    rows, images, cols, width = inputs.shape
    height = lax.axis_size("row")
    devices = height * lax.axis_size("img")
    flat = lax.axis_index("img") * height + lax.axis_index("row")
    top = devices.bit_length() - 2
    exchanges = [Exchange([0], True, flat, devices), Exchange([top, 1], True, flat, devices)]
    exchanges += [Exchange([bit], False, flat, devices) for bit in range(2, top)]
    core = exchanges[0].place
    rows_gains = [weights[i].reshape(1, width) for i in (0, 5)]
    column_gains = [weights[i].reshape(1, width) for i in (8, 13)]
    matrices = [w for w in weights if w.ndim == 2]
    hidden_width = matrices[4].shape[1]
    owned = images * cols // height

    def trade(array):
        return lax.all_to_all(array, "row", 0, 0, tiled=True)

    squares = ("square",) * 4
    total = grad_rows(width, hidden_width)
    sent_shape = (height, rows, owned, width)
    up = cotangent.reshape(rows, height, owned, width).transpose(1, 0, 2, 3)
    up = trade(up)
    sent, query, key, value, attended, middle, probs, hidden, slope = rows_forward(
        inputs, rows_gains, matrices[:6], sent_shape
    )
    sent, up = lax.optimization_barrier((sent, up))
    stream = trade(sent)
    final, between_grad, keep, send = columns_both(core, stream, up, column_gains, matrices[6:])
    kinds = (0, *squares, 1, "columns", "rows")
    columns = Chain(exchanges, ((total, kinds),), keep, send, hidden_width)
    token = columns.add(columns.cut(columns.token))
    between_grad = trade(between_grad)
    between_grad, final, token = lax.optimization_barrier((between_grad, final, token))
    final = trade(final)
    wq, wk, wv, wo, w1, w2 = matrices[:6]
    kept = (slope, hidden, w2, middle, w1, *rows_gains, attended, wo, query, key, value, probs, inputs, wq, wk, wv)
    *grads, keep, send = rows_backward(core, between_grad, kept, token)
    rows_chain = Chain(exchanges, ((total, kinds),), keep, send, hidden_width)
    token = rows_chain.cut(rows_chain.token)
    stream_grad, token = rows_rest(grads, inputs, rows_gains[0], (wq, wk, wv), token)
    while columns.others:
        token = columns.add(token)
    token = rows_chain.add(token)
    final, token = unpack(final, inputs.shape, token)
    token = columns.last(token)
    columns.spread()
    while rows_chain.others:
        token = rows_chain.add(token)
    token = rows_chain.last(token)
    token = columns.join(token)
    rows_chain.spread()
    token = columns.finish(token)
    token = rows_chain.join(token)
    rows_chain.finish(token)
    c_gain, c_query, c_keys, c_values, c_mixer, c_scale, c_expand, c_shrink = columns.results
    r_gain, r_query, r_keys, r_values, r_mixer, r_scale, r_expand, r_shrink = rows_chain.results
    return (
        final, stream_grad,
        r_gain, r_query, r_keys, r_values, r_mixer, r_scale, r_expand, r_shrink,
        c_gain, c_query, c_keys, c_values, c_mixer, c_scale, c_expand, c_shrink,
    )


def solution(mesh):
    moved = P("row", "img", None, None)
    return jax.shard_map(
        on_device,
        mesh=mesh,
        in_specs=(moved, moved) + (P(),) * 16,
        out_specs=(moved, moved) + (P(),) * 16,
        check_vma=False,
    )
```
